32 devices in a mesh: groups: 2 (over x), blk: 16 (over z, y, core).
Axes of the slice: x: 2, y: 2, z: 4, core: 2. Of those that a mesh axis runs over, the one named last changes fastest.
Arguments:
- cache_kv: bfloat16 [32768, 2, 1536], P(('groups', 'blk')), parts along dimension 0, may hold values from -6 to 6
- fresh_qkv: bfloat16 [2, 192, 3, 1536], P(None, ('groups', 'blk')), parts along dimension 1, may hold values from -100 to 100
- list_rows: int32 [2, 192], P(None, ('groups', 'blk')), parts along dimension 1, may hold values from 0 to 1023, as said below
- counts: int32 [2, 32], P(None, 'groups'), parts along dimension 1, may hold values from 1 to 6, 64 in all within a row
Outputs:
- attended: bfloat16 [2, 128, 1536], P(None, ('groups', 'blk')), parts along dimension 1
The draws below stay inside these ranges and needn't reach their ends.
There are 2 independent parts, one for each index of `groups`. The reference program is written for one: setup_inputs(seed, part) draws one part's arguments, and reference() takes and returns one part's arrays. A program takes and returns all parts, laid end to end along the dimension named above; each array names one. Nothing has to cross between parts.
Inputs may be any that keep to these rules, and one draw needn't show every extreme that they name: `list_rows`: the entries of one device and one step are distinct rows of that device. The counts of each step sum to 64.
All inputs are finite; a program needn't handle non-finite values.
Results may differ from the reference program's by a relative error of at most 0.005.
Values may be sent and summed in bfloat16 or wider, within the bound.
No kernel may reach another device: no remote copies, remote signals or barrier semaphores. Data moves between devices by JAX's collectives and lax.ppermute only.
A program may use at most 128 MiB of HBM per device.

```python
import math
import jax
import jax.numpy as jnp
import numpy as np
from jax import lax

HEADS = 12
HEAD = 128
TOK_DEV = 1024
STEPS = 2
CAPH = 6
TOKENS = 16384
PADDED = 96
QUERIES = 64
N_BLK = 16


def draw_cache_kv(key, part):
    key = jax.random.fold_in(key, 1)
    kv_cache = jnp.clip(jax.random.normal(key, (TOKENS, 2, HEADS * HEAD), jnp.float32), -6.0, 6.0)
    return kv_cache.astype(jnp.bfloat16)


def draw_fresh_qkv(key, part):
    key = jax.random.fold_in(key, 2)
    fresh = jnp.clip(jax.random.normal(key, (STEPS, PADDED, 3, HEADS * HEAD), jnp.float32), -6.0, 6.0)
    fresh = fresh * jnp.array([3.2, 1.0, 1.0], jnp.float32)[None, None, :, None]
    return fresh.astype(jnp.bfloat16)


def one_list(single, first):
    drawn = jax.random.permutation(single, TOK_DEV)[:CAPH].astype(jnp.int32)
    inner = (jax.random.permutation(jax.random.fold_in(single, 7), TOK_DEV - 2)[:CAPH - 2] + 1).astype(jnp.int32)
    ends = jnp.array([0, TOK_DEV - 1], jnp.int32)
    forced = jax.random.permutation(jax.random.fold_in(single, 8), jnp.concatenate([ends, inner])).astype(jnp.int32)
    return jnp.where(first, forced, drawn).astype(jnp.int32)


def draw_list_rows(key, part):
    key = jax.random.fold_in(key, 3)
    many_keys = jax.random.split(key, STEPS * N_BLK)
    firsts = jnp.arange(STEPS * N_BLK, dtype=jnp.int32) == 0
    picks = jax.vmap(one_list)(many_keys, firsts)
    return picks.reshape(STEPS, PADDED).astype(jnp.int32)


def split_up(number_of, total, bound, slope):
    loads = [(1 << 20) // math.isqrt(grade ** slope) + 1 for grade in range(2, number_of + 1)]
    surplus, given = total - bound - (number_of - 1), [1] * (number_of - 1)
    while surplus > 0:
        movable = [i for i in range(number_of - 1) if given[i] < bound]
        whole, budget = sum([loads[i] for i in movable]), surplus
        for i in movable:
            more = min(bound - given[i], max(1, budget * loads[i] // whole), surplus)
            given[i] = given[i] + more
            surplus = surplus - more
    return np.array([bound] + given)


def uneven_parts(rng, amount, total, most, slope):
    if amount == 2:
        one = jax.random.randint(rng, (), max(1, total - most), min(most, total - 1) + 1)
        return jnp.stack([one, total - one])
    lengths = jnp.asarray(split_up(amount, total, most, slope), jnp.int32)
    couples = (amount - 1) // 2
    source_of, sink = lengths[1:1 + 2 * couples:2], lengths[2:2 + 2 * couples:2]
    margin = jnp.minimum(source_of - 1, most - sink)
    shifted = jax.random.randint(jax.random.fold_in(rng, 1), (couples,), 0, 1 << 20) % (margin + 1)
    lengths = lengths.at[1:1 + 2 * couples:2].set(source_of - shifted).at[2:2 + 2 * couples:2].set(sink + shifted)
    return lengths[jax.random.permutation(jax.random.fold_in(rng, 2), amount)]


def setup_inputs(seed: int = 0, part: int = 0) -> dict:
    arg_keys = jax.random.split(jax.random.key(seed), 5)
    own_keys = jax.random.split(jax.random.fold_in(arg_keys[4], part), 5)
    cache_kv = draw_cache_kv(jax.random.fold_in(jax.random.fold_in(arg_keys[4], part), 71), part)
    fresh_qkv = draw_fresh_qkv(jax.random.fold_in(jax.random.fold_in(arg_keys[4], part), 71), part)
    list_rows = draw_list_rows(jax.random.fold_in(jax.random.fold_in(arg_keys[4], part), 71), part)
    counts = jax.vmap(lambda own: uneven_parts(own, N_BLK, QUERIES, CAPH, 2))(jax.random.split(own_keys[3], STEPS)).reshape((STEPS, N_BLK)).astype(jnp.int32)
    return dict(cache_kv=cache_kv, fresh_qkv=fresh_qkv, list_rows=list_rows, counts=counts)


def compact_order(step_counts, query_count, slot_count):
    step_counts = step_counts.astype(jnp.int32)
    count_ends = jnp.cumsum(step_counts).astype(jnp.int32)
    rank_order = jnp.arange(query_count, dtype=jnp.int32)
    before = count_ends[None, :] <= rank_order[:, None]
    home_dev = jnp.sum(before.astype(jnp.int32), axis=1).astype(jnp.int32)
    home_start = jnp.sum(jnp.where(before, step_counts[None, :], 0), axis=1).astype(jnp.int32)
    return (home_dev * slot_count + rank_order - home_start).astype(jnp.int32)


def reference(cache_kv, fresh_qkv, list_rows, counts):
    row_width = HEADS * HEAD
    kv_cache = cache_kv
    slot_index = jnp.arange(PADDED, dtype=jnp.int32)
    home_dev = slot_index // CAPH
    results = []
    for step_index in range(STEPS):
        step_counts = counts[step_index].astype(jnp.int32)
        is_live = (slot_index % CAPH) < step_counts[home_dev]
        target = jnp.where(is_live, home_dev * TOK_DEV + list_rows[step_index].astype(jnp.int32), TOKENS)
        kv_cache = kv_cache.at[target].set(fresh_qkv[step_index, :, 1:3, :], mode="drop")
        picked = fresh_qkv[step_index, :, 0, :][compact_order(step_counts, QUERIES, CAPH)]
        key_rows = kv_cache[:, 0, :].astype(jnp.float32).reshape(TOKENS, HEADS, HEAD)
        value_rows = kv_cache[:, 1, :].astype(jnp.float32).reshape(TOKENS, HEADS, HEAD)
        row_block = min(16, QUERIES)

        def one_block(queries):
            queries = queries.astype(jnp.float32).reshape(row_block, HEADS, HEAD)
            scores = jnp.einsum("bhd,thd->bht", queries, key_rows) * (HEAD ** -0.5)
            highest = jnp.max(scores, axis=2)
            exact = jnp.exp(scores - highest[:, :, None])
            total_weight = jnp.sum(exact, axis=2)
            rounded = lax.optimization_barrier(exact.astype(jnp.bfloat16))
            weighted = jnp.einsum("bht,thd->bhd", rounded.astype(jnp.float32), value_rows)
            return (weighted / total_weight[:, :, None]).reshape(row_block, row_width)

        output = lax.map(one_block, picked.reshape(QUERIES // row_block, row_block, row_width))
        results.append(output.reshape(QUERIES, row_width).astype(jnp.bfloat16))
    return jnp.stack(results)
```

```python
import functools

import jax
import jax.numpy as jnp
from jax import lax
from jax.experimental import pallas as pl
from jax.experimental.pallas import tpu as pltpu
from jax.sharding import PartitionSpec as P

HEAD = 128
SLOT = 4
STEPS = 2
PAIR = STEPS * SLOT
LOG2E = 1.4426950408889634
SCALE = HEAD ** -0.5 * LOG2E
FAR = -1e30
LANES = 128


def split_kernel(kv_ref, key_ref, value_ref):
    rows = kv_ref.shape[0]
    half = rows // 2
    out = lax.broadcasted_iota(jnp.int32, (rows, rows), 0)
    src = lax.broadcasted_iota(jnp.int32, (rows, rows), 1)
    want = jnp.where(out < half, 2 * out, 2 * (out - half) + 1)
    order = (src == want).astype(jnp.bfloat16)
    for c in range(0, kv_ref.shape[1], 256):
        part = jnp.dot(order, kv_ref[:, c:c + 256], preferred_element_type=jnp.float32)
        key_ref[:, c:c + 256] = part[:half].astype(jnp.bfloat16)
        value_ref[:, c:c + 256] = part[half:].astype(jnp.bfloat16)


def split_cache(cache):
    tokens, _, width = cache.shape
    block = min(128, tokens)
    shape = jax.ShapeDtypeStruct((tokens, width), jnp.bfloat16)
    spec = pl.BlockSpec((block, width), lambda i: (i, 0))
    return pl.pallas_call(
        split_kernel,
        grid=(tokens // block,),
        out_shape=(shape, shape),
        in_specs=[pl.BlockSpec((2 * block, width), lambda i: (i, 0))],
        out_specs=(spec, spec),
        compiler_params=pltpu.CompilerParams(vmem_limit_bytes=32 << 20),
        cost_estimate=pl.CostEstimate(
            flops=4 * block * 2 * tokens * width, bytes_accessed=8 * tokens * width, transcendentals=0
        ),
        name="split_cache",
    )(cache.reshape(2 * tokens, width))


def two_parts(x):
    high = x.astype(jnp.bfloat16).astype(jnp.float32)
    return high, x - high


def attend_kernel(target_ref, bias_ref, fresh_bias_ref, fresh_key_ref, fresh_value_ref, key_ref, value_ref, *rest):
    gathered_refs, out_ref = rest[:-1], rest[-1]
    heads = key_ref.shape[1] // HEAD
    chunk = 128
    chunks = out_ref.shape[0] * PAIR // chunk
    nt = (((1,), (1,)), ((), ()))

    def one_chunk(i):
        base = i * chunk
        want = target_ref[0:1, :] - base
        row = lax.broadcasted_iota(jnp.int32, (chunk, want.shape[1]), 0)
        pick = (row == want).astype(jnp.bfloat16)
        slots = jnp.concatenate([g[...] for g in gathered_refs], axis=0)
        queries = jnp.dot(pick, slots, preferred_element_type=jnp.float32).astype(jnp.bfloat16)
        bias = bias_ref[...]
        fresh_bias = fresh_bias_ref[...]
        lane = lax.broadcasted_iota(jnp.int32, (chunk, LANES), 1)
        highs = jnp.zeros((chunk, LANES), jnp.float32)
        totals = jnp.zeros((chunk, LANES), jnp.float32)
        for h in range(heads):
            cols = slice(h * HEAD, (h + 1) * HEAD)
            q = queries[:, cols]
            s = lax.dot_general(q, key_ref[:, cols], nt, preferred_element_type=jnp.float32)
            sf = lax.dot_general(q, fresh_key_ref[:, cols], nt, preferred_element_type=jnp.float32)
            s = (s.reshape(chunk // PAIR, PAIR, -1) + bias[None]).reshape(chunk, -1)
            sf = (sf.reshape(chunk // PAIR, PAIR, -1) + fresh_bias[None]).reshape(chunk, -1)
            high = jnp.maximum(jnp.max(s, axis=1, keepdims=True), jnp.max(sf, axis=1, keepdims=True))
            w = jnp.exp2((s - high) * SCALE)
            wf = jnp.exp2((sf - high) * SCALE)
            total = jnp.sum(w, axis=1, keepdims=True) + jnp.sum(wf, axis=1, keepdims=True)
            o = jnp.dot(w.astype(jnp.bfloat16), value_ref[:, cols], preferred_element_type=jnp.float32)
            o += jnp.dot(wf.astype(jnp.bfloat16), fresh_value_ref[:, cols], preferred_element_type=jnp.float32)
            o = (o / total).astype(jnp.bfloat16)
            out_ref[pl.ds(i * (chunk // PAIR), chunk // PAIR), :, cols] = o.reshape(chunk // PAIR, PAIR, HEAD)
            highs = jnp.where(lane == h, high, highs)
            totals = jnp.where(lane == h, total, totals)
        h1, r = two_parts(highs)
        h2, h3 = two_parts(r)
        t1, t2 = two_parts(totals)
        stats = h1
        for n, part in enumerate((h2, h3, t1, t2)):
            stats = stats + pltpu.roll(part, 16 * (n + 1), 1)
        stats = stats.astype(jnp.bfloat16)
        width = heads * HEAD
        out_ref[pl.ds(i * (chunk // PAIR), chunk // PAIR), :, width:] = stats.reshape(chunk // PAIR, PAIR, LANES)

    if chunks == 1:
        one_chunk(0)
    else:
        pl.loop(0, chunks)(one_chunk)


def attend(target, bias, fresh_bias, fresh_key, fresh_value, key, value, gathered):
    device_count = target.shape[1] // fresh_key.shape[0]
    tokens, width = key.shape
    rows = device_count * PAIR
    vmem = pl.BlockSpec(memory_space=pltpu.VMEM)
    return pl.pallas_call(
        attend_kernel,
        out_shape=jax.ShapeDtypeStruct((device_count, PAIR, width + LANES), jnp.bfloat16),
        in_specs=[vmem] * (7 + len(gathered)),
        out_specs=vmem,
        compiler_params=pltpu.CompilerParams(vmem_limit_bytes=48 << 20),
        cost_estimate=pl.CostEstimate(
            flops=4 * rows * tokens * width, bytes_accessed=4 * tokens * width,
            transcendentals=rows * tokens * width // HEAD,
        ),
        name="attend",
    )(target, bias, fresh_bias, fresh_key, fresh_value, key, value, *gathered)


def combine_kernel(parts_ref, out_ref):
    width = out_ref.shape[1]
    heads = width // HEAD
    stats = parts_ref[:, :, width:].astype(jnp.float32)

    def part(n):
        return stats[:, :, 16 * n:16 * n + heads]

    high = part(0) + part(1) + part(2)
    total = part(3) + part(4)
    top = jnp.max(high, axis=0, keepdims=True)
    weight = total * jnp.exp2((high - top) * SCALE)
    weight = weight / jnp.sum(weight, axis=0, keepdims=True)
    for h in range(heads):
        cols = slice(h * HEAD, (h + 1) * HEAD)
        o = parts_ref[:, :, cols].astype(jnp.float32) * weight[:, :, h:h + 1]
        out_ref[:, cols] = jnp.sum(o, axis=0).astype(jnp.bfloat16)


def combine(parts):
    vmem = pl.BlockSpec(memory_space=pltpu.VMEM)
    width = parts.shape[2] - LANES
    return pl.pallas_call(
        combine_kernel,
        out_shape=jax.ShapeDtypeStruct((PAIR, width), jnp.bfloat16),
        in_specs=[vmem],
        out_specs=vmem,
        compiler_params=pltpu.CompilerParams(vmem_limit_bytes=32 << 20),
        name="combine",
    )(parts)


def plan_rows(counts, list_rows, my_index, token_count, slot_rows):
    device_count = counts.shape[1]
    slot_count = list_rows.shape[1]
    before = jnp.arange(device_count)[:, None] < jnp.arange(device_count)[None, :]
    starts = jnp.sum(jnp.where(before[None], counts[:, :, None], 0), axis=1)
    device = (my_index - jnp.arange(device_count)) % device_count
    chosen = device[:, None] == jnp.arange(device_count)[None, :]
    start = jnp.sum(jnp.where(chosen[None], starts[:, None, :], 0), axis=2)
    count = jnp.sum(jnp.where(chosen[None], counts[:, None, :], 0), axis=2)
    at = jnp.arange(slot_rows)
    slot, step = at // STEPS, at % STEPS
    start = jnp.where(step[None, :] == 0, start[0][:, None], start[1][:, None])
    count = jnp.where(step[None, :] == 0, count[0][:, None], count[1][:, None])
    rank = start + slot[None, :]
    row = (rank // SLOT) * PAIR + step[None, :] * SLOT + rank % SLOT
    target = jnp.where(slot[None, :] < count, row, -1).reshape(1, -1).astype(jnp.int32)

    mine = jnp.sum(jnp.where(jnp.arange(device_count)[None, :] == my_index, counts, 0), axis=1)
    live = jnp.arange(slot_count)[None, :] < mine[:, None]
    place = jnp.where(live, list_rows, -1)
    hit = jnp.any(place[:, :, None] == jnp.arange(token_count)[None, None, :], axis=1)
    gone = jnp.stack([hit[0], hit[0] | hit[1]])
    bias = jnp.where(gone, FAR, 0.0).astype(jnp.float32)
    bias = jnp.repeat(bias, SLOT, axis=0)
    again = jnp.any(place[0][:, None] == place[1][None, :], axis=1)
    none = jnp.zeros_like(live[0])
    first = jnp.stack([live[0], none], axis=1).reshape(-1)
    second = jnp.stack([live[0] & ~again, live[1]], axis=1).reshape(-1)
    seen = jnp.stack([first, second])
    seen = jnp.pad(seen, ((0, 0), (0, slot_rows - seen.shape[1])))
    fresh_bias = jnp.repeat(jnp.where(seen, 0.0, FAR).astype(jnp.float32), SLOT, axis=0)
    return target, bias, fresh_bias


def body(cache_kv, fresh_qkv, list_rows, counts):
    device_count = lax.axis_size("blk")
    my_index = lax.axis_index("blk")
    slot_count = list_rows.shape[1]
    width = cache_kv.shape[2]
    slot_rows = -(-slot_count * STEPS // 16) * 16
    fresh = fresh_qkv.transpose(2, 1, 0, 3).reshape(3, slot_count * STEPS, width)
    fresh = jnp.pad(fresh, ((0, 0), (0, slot_rows - slot_count * STEPS), (0, 0)))
    mine = fresh[0]
    gathered = [mine]
    for k in range(1, device_count):
        pairs = [(i, (i + k) % device_count) for i in range(device_count)]
        gathered.append(lax.ppermute(mine, "blk", pairs))
    if device_count > 16:
        gathered = [jnp.concatenate(gathered)]
    target, bias, fresh_bias = plan_rows(counts, list_rows, my_index, cache_kv.shape[0], slot_rows)
    key, value = split_cache(cache_kv)
    parts = attend(target, bias, fresh_bias, fresh[1], fresh[2], key, value, gathered)
    parts = lax.all_to_all(parts, "blk", split_axis=0, concat_axis=0, tiled=True)
    return combine(parts).reshape(STEPS, SLOT, width)


def solution(mesh):
    in_specs = (
        P(("groups", "blk"), None, None),
        P(None, ("groups", "blk"), None, None),
        P(None, ("groups", "blk")),
        P(None, "groups"),
    )
    out_specs = P(None, ("groups", "blk"), None)
    return jax.shard_map(body, mesh=mesh, in_specs=in_specs, out_specs=out_specs, check_vma=False)
```

```python
import jax
import jax.numpy as jnp
from jax import lax
from jax.experimental import pallas as pl
from jax.experimental.pallas import tpu as pltpu
from jax.sharding import PartitionSpec as P

HEAD = 128
SLOT = 4
STEPS = 2
PAIR = STEPS * SLOT
LOG2E = 1.4426950408889634
SCALE = HEAD ** -0.5 * LOG2E
FAR = -1e30
LANES = 128
PART = 16
SLOT_BITS = 2
VMEM = pl.BlockSpec(memory_space=pltpu.VMEM)
SMEM = pl.BlockSpec(memory_space=pltpu.SMEM)
ANY = pl.BlockSpec(memory_space=pl.ANY)


def mesh_digits(device_count):
    bits = (device_count // 2).bit_length() - 1
    far_bits = (bits + 1) // 2
    return 1 << far_bits, 1 << (bits - far_bits)


def place_of(mask, far, near):
    near_bits = near.bit_length() - 1
    core = mask & 1
    near_digit = (mask >> 1) & (near - 1)
    far_digit = mask >> (1 + near_bits)
    return (core * near + near_digit) * far + far_digit


def prepare_kernel(me_ref, counts_ref, rows_ref, cache_ref, fresh_ref,
                   key_ref, value_ref, fresh_key_ref, fresh_value_ref, target_ref, bias_ref, fresh_bias_ref,
                   held, fresh_held, sems):
    tokens, _, width = cache_ref.shape
    slots = fresh_ref.shape[0]
    device_count = counts_ref.shape[1]
    far, near = mesh_digits(device_count)
    block = min(128, tokens)
    blocks = tokens // block

    def fetch(i):
        part = pl.ds(i * block, block)
        return pltpu.make_async_copy(cache_ref.at[part], held.at[part], sems.at[i])

    def fetch_fresh(i):
        return pltpu.make_async_copy(fresh_ref.at[:, 1 + i], fresh_held.at[i], sems.at[blocks + i])

    for i in range(blocks):
        fetch(i).start()
    for i in range(2):
        fetch_fresh(i).start()

    me = me_ref[0]
    col = lax.broadcasted_iota(jnp.int32, target_ref.shape, 1)

    def one_device(dev, carry):
        start0, start1, target = carry
        count0, count1 = counts_ref[0, dev], counts_ref[1, dev]
        local = col - place_of(dev ^ me, far, near) * (STEPS * slots)
        slot, step = local >> 1, local & 1
        rank = slot + jnp.where(step == 0, start0, start1)
        row = place_of((rank >> SLOT_BITS) ^ me, far, near) * PAIR + step * SLOT + (rank & (SLOT - 1))
        good = (local >= 0) & (slot < jnp.where(step == 0, count0, count1))
        return start0 + count0, start1 + count1, jnp.where(good, row, target)

    carry = (jnp.int32(0), jnp.int32(0), jnp.full(target_ref.shape, -1, jnp.int32))
    if device_count <= 16:
        for dev in range(device_count):
            carry = one_device(dev, carry)
    else:
        carry = lax.fori_loop(0, device_count, one_device, carry)
    target_ref[...] = carry[2]

    live0 = [i < counts_ref[0, me] for i in range(slots)]
    live1 = [i < counts_ref[1, me] for i in range(slots)]
    row0 = [jnp.where(live0[i], rows_ref[0, i], -1) for i in range(slots)]
    row1 = [jnp.where(live1[i], rows_ref[1, i], -2) for i in range(slots)]
    token = lax.broadcasted_iota(jnp.int32, bias_ref.shape, 1)
    second = lax.broadcasted_iota(jnp.int32, bias_ref.shape, 0) >= SLOT
    gone = token == row0[0]
    for i in range(1, slots):
        gone = gone | (token == row0[i])
    later = token == row1[0]
    for i in range(1, slots):
        later = later | (token == row1[i])
    bias_ref[...] = jnp.where(gone | (second & later), FAR, 0.0)
    col = lax.broadcasted_iota(jnp.int32, fresh_bias_ref.shape, 1)
    second = (lax.broadcasted_iota(jnp.int32, fresh_bias_ref.shape, 0) >= SLOT).astype(jnp.int32)
    seen = jnp.zeros(fresh_bias_ref.shape, jnp.int32)
    for i in range(slots):
        again = row1[0] == row0[i]
        for j in range(1, slots):
            again = again | (row1[j] == row0[i])
        kept = (live0[i] & jnp.logical_not(again)).astype(jnp.int32)
        early = jnp.where(second == 1, kept, live0[i].astype(jnp.int32))
        seen = jnp.where(col == 2 * i, early, seen)
        seen = jnp.where(col == 2 * i + 1, second * live1[i].astype(jnp.int32), seen)
    fresh_bias_ref[...] = jnp.where(seen == 1, 0.0, FAR)

    out = lax.broadcasted_iota(jnp.int32, (2 * block, 2 * block), 0)
    src = lax.broadcasted_iota(jnp.int32, (2 * block, 2 * block), 1)
    order = (src == jnp.where(out < block, 2 * out, 2 * (out - block) + 1)).astype(jnp.bfloat16)
    pairs = held.reshape(2 * tokens, width)
    for i in range(blocks):
        fetch(i).wait()
        rows = slice(i * block, (i + 1) * block)
        for c in range(0, width, 256):
            part = pairs[2 * i * block:2 * (i + 1) * block, c:c + 256]
            part = jnp.dot(order, part, preferred_element_type=jnp.float32).astype(jnp.bfloat16)
            key_ref[rows, c:c + 256] = part[:block]
            value_ref[rows, c:c + 256] = part[block:]
    for i, ref in enumerate((fresh_key_ref, fresh_value_ref)):
        fetch_fresh(i).wait()
        ref[...] = jnp.zeros_like(ref)
        ref[0:STEPS * slots, :] = fresh_held.at[i].reshape(STEPS * slots, width)[...]


def prepare(me, counts, list_rows, cache, fresh):
    tokens, _, width = cache.shape
    slots = fresh.shape[0]
    fresh_rows = -(-STEPS * slots // 16) * 16
    f32, bf16 = jnp.float32, jnp.bfloat16
    shapes = (
        jax.ShapeDtypeStruct((tokens, width), bf16),
        jax.ShapeDtypeStruct((tokens, width), bf16),
        jax.ShapeDtypeStruct((fresh_rows, width), bf16),
        jax.ShapeDtypeStruct((fresh_rows, width), bf16),
        jax.ShapeDtypeStruct((1, counts.shape[1] * STEPS * slots), jnp.int32),
        jax.ShapeDtypeStruct((PAIR, tokens), f32),
        jax.ShapeDtypeStruct((PAIR, fresh_rows), f32),
    )
    blocks = tokens // min(128, tokens)
    return pl.pallas_call(
        prepare_kernel,
        out_shape=shapes,
        in_specs=[SMEM, SMEM, SMEM, ANY, ANY],
        out_specs=(VMEM,) * len(shapes),
        scratch_shapes=[
            pltpu.VMEM((tokens, 2, width), bf16),
            pltpu.VMEM((2, slots, STEPS, width), bf16),
            pltpu.SemaphoreType.DMA((blocks + 2,)),
        ],
        compiler_params=pltpu.CompilerParams(vmem_limit_bytes=22 << 20),
        cost_estimate=pl.CostEstimate(
            flops=8 * 128 * tokens * width, bytes_accessed=8 * tokens * width, transcendentals=0
        ),
        name="prepare",
    )(me, counts, list_rows, cache, fresh)


def two_parts(x):
    high = x.astype(jnp.bfloat16).astype(jnp.float32)
    return high, x - high


def pack_stats(high, total):
    lane = lax.broadcasted_iota(jnp.int32, high.shape, 1)
    high = jnp.where(lane < PART, high, 0.0)
    total = jnp.where(lane < PART, total, 0.0)
    stats, rest = two_parts(high)
    second, third = two_parts(rest)
    for n, part in enumerate((second, third) + two_parts(total)):
        stats = stats + pltpu.roll(part, PART * (n + 1), 1)
    return stats


def unpack_stats(stats):
    def part(n):
        return pltpu.roll(stats, LANES - PART * n, 1)

    return stats + part(1) + part(2), part(3) + part(4)


def attend_kernel(target_ref, bias_ref, fresh_bias_ref, fresh_key_ref, fresh_value_ref, key_ref, value_ref, *rest):
    gathered_refs, (keep_ref, send_ref) = rest[:-2], rest[-2:]
    width = key_ref.shape[1]
    heads = width // HEAD
    half = keep_ref.shape[0]
    nt = (((1,), (1,)), ((), ()))

    def attend_rows(base, chunk, stores):
        row = lax.broadcasted_iota(jnp.int32, (chunk, target_ref.shape[1]), 0)
        pick = (row == target_ref[...] - base).astype(jnp.bfloat16)
        queries, at = None, 0
        for ref in gathered_refs:
            count = ref.shape[0] * STEPS
            slots = ref.reshape(count, width)[...]
            part = jnp.dot(pick[:, at:at + count], slots, preferred_element_type=jnp.float32)
            queries = part if queries is None else queries + part
            at += count
        queries = queries.astype(jnp.bfloat16)
        bias = bias_ref[...]
        fresh_bias = fresh_bias_ref[...]
        lane = lax.broadcasted_iota(jnp.int32, (chunk, LANES), 1)
        highs = jnp.zeros((chunk, LANES), jnp.float32)
        totals = jnp.zeros((chunk, LANES), jnp.float32)
        for h in range(heads):
            cols = slice(h * HEAD, (h + 1) * HEAD)
            q = queries[:, cols]
            s = lax.dot_general(q, key_ref[:, cols], nt, preferred_element_type=jnp.float32)
            sf = lax.dot_general(q, fresh_key_ref[:, cols], nt, preferred_element_type=jnp.float32)
            s = (s.reshape(chunk // PAIR, PAIR, -1) + bias[None]).reshape(chunk, -1)
            sf = (sf.reshape(chunk // PAIR, PAIR, -1) + fresh_bias[None]).reshape(chunk, -1)
            high = jnp.maximum(jnp.max(s, axis=1, keepdims=True), jnp.max(sf, axis=1, keepdims=True))
            w = jnp.exp2((s - high) * SCALE)
            wf = jnp.exp2((sf - high) * SCALE)
            total = jnp.sum(w, axis=1, keepdims=True) + jnp.sum(wf, axis=1, keepdims=True)
            o = jnp.dot(w.astype(jnp.bfloat16), value_ref[:, cols], preferred_element_type=jnp.float32)
            o += jnp.dot(wf.astype(jnp.bfloat16), fresh_value_ref[:, cols], preferred_element_type=jnp.float32)
            o = o * (1.0 / total)
            for ref, to, start, count in stores:
                ref[pl.ds(to, count), cols] = o[start:start + count].astype(ref.dtype)
            highs = jnp.where(lane == h, high, highs)
            totals = jnp.where(lane == h, total, totals)
        stats = pack_stats(highs, totals)
        for ref, to, start, count in stores:
            ref[pl.ds(to, count), width:] = stats[start:start + count].astype(ref.dtype)

    if 2 * half <= 128:
        attend_rows(0, 2 * half, [(keep_ref, 0, 0, half), (send_ref, 0, half, half)])
    else:
        for ref, base in ((keep_ref, 0), (send_ref, half)):
            @pl.loop(0, half // 128)
            def _(i, ref=ref, base=base):
                to = pl.multiple_of(i * 128, 128)
                attend_rows(base + to, 128, [(ref, to, 0, 128)])


def attend(slots, target, bias, fresh_bias, fresh_key, fresh_value, key, value, gathered):
    tokens, width = key.shape
    rows = target.shape[1] * SLOT // slots
    shape = (rows // 2, width + LANES)
    return pl.pallas_call(
        attend_kernel,
        out_shape=(jax.ShapeDtypeStruct(shape, jnp.float32), jax.ShapeDtypeStruct(shape, jnp.bfloat16)),
        in_specs=[VMEM] * (7 + len(gathered)),
        out_specs=(VMEM, VMEM),
        compiler_params=pltpu.CompilerParams(vmem_limit_bytes=24 << 20),
        cost_estimate=pl.CostEstimate(
            flops=4 * rows * tokens * width, bytes_accessed=4 * tokens * width,
            transcendentals=rows * tokens * width // HEAD,
        ),
        name="attend",
    )(target, bias, fresh_bias, fresh_key, fresh_value, key, value, *gathered)


def merge_kernel(count, last, *refs):
    parts, outs = refs[:count], refs[count:]
    rows, width = parts[0].shape
    width -= LANES
    stats = [unpack_stats(ref[:, width:].astype(jnp.float32)) for ref in parts]
    top = stats[0][0]
    for high, _ in stats[1:]:
        top = jnp.maximum(top, high)
    weights = [total * jnp.exp2((high - top) * SCALE) for high, total in stats]
    total = weights[0]
    for w in weights[1:]:
        total = total + w
    used = lax.broadcasted_iota(jnp.int32, total.shape, 1) < width // HEAD
    share = 1.0 / jnp.where(used, total, 1.0)
    weights = [w * share for w in weights]
    for h in range(width // HEAD):
        cols = slice(h * HEAD, (h + 1) * HEAD)
        o = parts[0][:, cols].astype(jnp.float32) * weights[0][:, h:h + 1]
        for ref, w in zip(parts[1:], weights[1:]):
            o = o + ref[:, cols].astype(jnp.float32) * w[:, h:h + 1]
        if last:
            for s in range(STEPS):
                outs[0][s, :, cols] = o[s * SLOT:(s + 1) * SLOT].astype(jnp.bfloat16)
        else:
            step = rows // len(outs)
            for n, ref in enumerate(outs):
                ref[:, cols] = o[n * step:(n + 1) * step].astype(ref.dtype)
    if not last:
        packed = pack_stats(jnp.where(used, top, 0.0), jnp.where(used, total, 0.0))
        for n, ref in enumerate(outs):
            ref[:, width:] = packed[n * step:(n + 1) * step].astype(ref.dtype)


def merge(parts, out_count, name):
    rows, width = parts[0].shape
    last = out_count == 0
    if last:
        shapes = (jax.ShapeDtypeStruct((STEPS, SLOT, width - LANES), jnp.bfloat16),)
    else:
        shapes = tuple(
            jax.ShapeDtypeStruct((rows // out_count, width), jnp.bfloat16 if n else jnp.float32)
            for n in range(out_count)
        )

    def kernel(*refs):
        merge_kernel(len(parts), last, *refs)

    return pl.pallas_call(
        kernel,
        out_shape=shapes,
        in_specs=[VMEM] * len(parts),
        out_specs=(VMEM,) * len(shapes),
        compiler_params=pltpu.CompilerParams(vmem_limit_bytes=16 << 20),
        name=name,
    )(*parts)


def body(cache_kv, fresh_qkv, list_rows, counts):
    device_count = lax.axis_size("blk")
    me = lax.axis_index("blk")
    far, near = mesh_digits(device_count)

    def swap(x, mask):
        return lax.ppermute(x, "blk", [(i, i ^ mask) for i in range(device_count)])

    fresh = fresh_qkv.transpose(1, 2, 0, 3)
    mine = fresh[:, 0]
    column = jnp.concatenate([mine] + [swap(mine, k * near * 2) for k in range(1, far)])
    plane = [column] + [swap(column, k * 2) for k in range(1, near)]
    gathered = plane + [swap(x, 1) for x in plane]
    ready = prepare(me.reshape(1), counts, list_rows, cache_kv, fresh)
    key, value, fresh_key, fresh_value, target, bias, fresh_bias = ready
    keep, send = attend(list_rows.shape[1], target, bias, fresh_bias, fresh_key, fresh_value, key, value, gathered)
    keep, *sends = merge([keep, swap(send, 1)], near, "merge_core")
    sends = [swap(x, (k + 1) * 2) for k, x in enumerate(sends)]
    keep, *sends = merge([keep] + sends, far, "merge_near")
    sends = [swap(x, (k + 1) * near * 2) for k, x in enumerate(sends)]
    return merge([keep] + sends, 0, "merge_far")[0]


def solution(mesh):
    in_specs = (
        P(("groups", "blk"), None, None),
        P(None, ("groups", "blk"), None, None),
        P(None, ("groups", "blk")),
        P(None, "groups"),
    )
    out_specs = P(None, ("groups", "blk"), None)
    return jax.shard_map(body, mesh=mesh, in_specs=in_specs, out_specs=out_specs, check_vma=False)
```

```python
import jax
import jax.numpy as jnp
from jax import lax
from jax.experimental import pallas as pl
from jax.experimental.pallas import tpu as pltpu
from jax.sharding import PartitionSpec as P

HEAD = 128
SLOT = 4
STEPS = 2
PAIR = STEPS * SLOT
LOG2E = 1.4426950408889634
SCALE = HEAD ** -0.5 * LOG2E
FAR = -1e30
LANES = 128
PART = 16
SLOT_BITS = 2
VMEM = pl.BlockSpec(memory_space=pltpu.VMEM)
SMEM = pl.BlockSpec(memory_space=pltpu.SMEM)
HBM = pl.BlockSpec(memory_space=pltpu.HBM)


def mesh_digits(device_count):
    bits = (device_count // 2).bit_length() - 1
    far_bits = (bits + 1) // 2
    return 1 << far_bits, 1 << (bits - far_bits)


def place_of(mask, far, near):
    near_bits = near.bit_length() - 1
    core = mask & 1
    near_digit = (mask >> 1) & (near - 1)
    far_digit = mask >> (1 + near_bits)
    return (core * near + near_digit) * far + far_digit


def prepare_kernel(table_ref, cache_ref, new_key_ref, new_value_ref,
                   key_ref, value_ref, fresh_key_ref, fresh_value_ref, target_ref, bias_ref, fresh_bias_ref,
                   held, sems):
    tokens, _, width = cache_ref.shape
    slots = new_key_ref.shape[0]
    device_count = table_ref.shape[1] - slots - 1
    far, near = mesh_digits(device_count)
    block = min(128, tokens)
    blocks = tokens // block

    def fetch(i):
        part = pl.ds(i * block, block)
        return pltpu.make_async_copy(cache_ref.at[part], held.at[part], sems.at[i])

    for i in range(blocks):
        fetch(i).start()

    me = table_ref[0, device_count + slots]
    col = lax.broadcasted_iota(jnp.int32, target_ref.shape, 1)

    def one_device(dev, carry):
        start0, start1, target = carry
        count0, count1 = table_ref[0, dev], table_ref[1, dev]
        local = col - place_of(dev ^ me, far, near) * (STEPS * slots)
        slot, step = local >> 1, local & 1
        rank = slot + jnp.where(step == 0, start0, start1)
        row = place_of((rank >> SLOT_BITS) ^ me, far, near) * PAIR + step * SLOT + (rank & (SLOT - 1))
        good = (local >= 0) & (slot < jnp.where(step == 0, count0, count1))
        return start0 + count0, start1 + count1, jnp.where(good, row, target)

    carry = (jnp.int32(0), jnp.int32(0), jnp.full(target_ref.shape, -1, jnp.int32))
    if device_count <= 16:
        for dev in range(device_count):
            carry = one_device(dev, carry)
    else:
        carry = lax.fori_loop(0, device_count, one_device, carry)
    target_ref[...] = carry[2]

    live0 = [i < table_ref[0, me] for i in range(slots)]
    live1 = [i < table_ref[1, me] for i in range(slots)]
    row0 = [jnp.where(live0[i], table_ref[0, device_count + i], -1) for i in range(slots)]
    row1 = [jnp.where(live1[i], table_ref[1, device_count + i], -2) for i in range(slots)]
    token = lax.broadcasted_iota(jnp.int32, bias_ref.shape, 1)
    second = lax.broadcasted_iota(jnp.int32, bias_ref.shape, 0) >= SLOT
    gone = token == row0[0]
    for i in range(1, slots):
        gone = gone | (token == row0[i])
    later = token == row1[0]
    for i in range(1, slots):
        later = later | (token == row1[i])
    bias_ref[...] = jnp.where(gone | (second & later), FAR, 0.0)
    col = lax.broadcasted_iota(jnp.int32, fresh_bias_ref.shape, 1)
    second = (lax.broadcasted_iota(jnp.int32, fresh_bias_ref.shape, 0) >= SLOT).astype(jnp.int32)
    seen = jnp.zeros(fresh_bias_ref.shape, jnp.int32)
    for i in range(slots):
        again = row1[0] == row0[i]
        for j in range(1, slots):
            again = again | (row1[j] == row0[i])
        kept = (live0[i] & jnp.logical_not(again)).astype(jnp.int32)
        early = jnp.where(second == 1, kept, live0[i].astype(jnp.int32))
        seen = jnp.where(col == 2 * i, early, seen)
        seen = jnp.where(col == 2 * i + 1, second * live1[i].astype(jnp.int32), seen)
    fresh_bias_ref[...] = jnp.where(seen == 1, 0.0, FAR)

    out = lax.broadcasted_iota(jnp.int32, (2 * block, 2 * block), 0)
    src = lax.broadcasted_iota(jnp.int32, (2 * block, 2 * block), 1)
    order = (src == jnp.where(out < block, 2 * out, 2 * (out - block) + 1)).astype(jnp.bfloat16)
    pairs = held.reshape(2 * tokens, width)
    for i in range(blocks):
        fetch(i).wait()
        rows = slice(i * block, (i + 1) * block)
        for c in range(0, width, 256):
            part = pairs[2 * i * block:2 * (i + 1) * block, c:c + 256]
            part = jnp.dot(order, part, preferred_element_type=jnp.float32).astype(jnp.bfloat16)
            key_ref[rows, c:c + 256] = part[:block]
            value_ref[rows, c:c + 256] = part[block:]
    for ref, new_ref in ((fresh_key_ref, new_key_ref), (fresh_value_ref, new_value_ref)):
        ref[...] = jnp.zeros_like(ref)
        ref[0:STEPS * slots, :] = new_ref.reshape(STEPS * slots, width)[...]


def prepare(table, cache, fresh_key, fresh_value):
    tokens, _, width = cache.shape
    slots = fresh_key.shape[0]
    device_count = table.shape[1] - slots - 1
    fresh_rows = -(-STEPS * slots // 16) * 16
    f32, bf16 = jnp.float32, jnp.bfloat16
    shapes = (
        jax.ShapeDtypeStruct((tokens, width), bf16),
        jax.ShapeDtypeStruct((tokens, width), bf16),
        jax.ShapeDtypeStruct((fresh_rows, width), bf16),
        jax.ShapeDtypeStruct((fresh_rows, width), bf16),
        jax.ShapeDtypeStruct((1, device_count * STEPS * slots), jnp.int32),
        jax.ShapeDtypeStruct((PAIR, tokens), f32),
        jax.ShapeDtypeStruct((PAIR, fresh_rows), f32),
    )
    blocks = tokens // min(128, tokens)
    return pl.pallas_call(
        prepare_kernel,
        out_shape=shapes,
        in_specs=[SMEM, HBM, VMEM, VMEM],
        out_specs=(VMEM,) * len(shapes),
        scratch_shapes=[
            pltpu.VMEM((tokens, 2, width), bf16),
            pltpu.SemaphoreType.DMA((blocks,)),
        ],
        compiler_params=pltpu.CompilerParams(vmem_limit_bytes=45 << 20),
        cost_estimate=pl.CostEstimate(
            flops=8 * 128 * tokens * width, bytes_accessed=8 * tokens * width, transcendentals=0
        ),
        name="prepare",
    )(table, cache, fresh_key, fresh_value)


def two_parts(x):
    high = x.astype(jnp.bfloat16).astype(jnp.float32)
    return high, x - high


def pack_stats(high, total):
    lane = lax.broadcasted_iota(jnp.int32, high.shape, 1)
    high = jnp.where(lane < PART, high, 0.0)
    total = jnp.where(lane < PART, total, 0.0)
    stats, rest = two_parts(high)
    second, third = two_parts(rest)
    for n, part in enumerate((second, third) + two_parts(total)):
        stats = stats + pltpu.roll(part, PART * (n + 1), 1)
    return stats


def unpack_stats(stats):
    def part(n):
        return pltpu.roll(stats, LANES - PART * n, 1)

    return stats + part(1) + part(2), part(3) + part(4)


def attend_kernel(target_ref, bias_ref, fresh_bias_ref, fresh_key_ref, fresh_value_ref, key_ref, value_ref, *rest):
    gathered_refs, (keep_ref, send_ref) = rest[:-2], rest[-2:]
    width = key_ref.shape[1]
    heads = width // HEAD
    half = keep_ref.shape[0]
    nt = (((1,), (1,)), ((), ()))

    def attend_rows(base, chunk, stores):
        row = lax.broadcasted_iota(jnp.int32, (chunk, target_ref.shape[1]), 0)
        pick = (row == target_ref[...] - base).astype(jnp.bfloat16)
        queries, at = None, 0
        for ref in gathered_refs:
            count = ref.shape[0] * STEPS
            slots = ref.reshape(count, width)[...]
            part = jnp.dot(pick[:, at:at + count], slots, preferred_element_type=jnp.float32)
            queries = part if queries is None else queries + part
            at += count
        queries = queries.astype(jnp.bfloat16)
        bias = bias_ref[...]
        fresh_bias = fresh_bias_ref[...]
        lane = lax.broadcasted_iota(jnp.int32, (chunk, LANES), 1)
        highs = jnp.zeros((chunk, LANES), jnp.float32)
        totals = jnp.zeros((chunk, LANES), jnp.float32)
        for h in range(heads):
            cols = slice(h * HEAD, (h + 1) * HEAD)
            q = queries[:, cols]
            s = lax.dot_general(q, key_ref[:, cols], nt, preferred_element_type=jnp.float32)
            sf = lax.dot_general(q, fresh_key_ref[:, cols], nt, preferred_element_type=jnp.float32)
            s = (s.reshape(chunk // PAIR, PAIR, -1) + bias[None]).reshape(chunk, -1)
            sf = (sf.reshape(chunk // PAIR, PAIR, -1) + fresh_bias[None]).reshape(chunk, -1)
            high = jnp.maximum(jnp.max(s, axis=1, keepdims=True), jnp.max(sf, axis=1, keepdims=True))
            w = jnp.exp2((s - high) * SCALE)
            wf = jnp.exp2((sf - high) * SCALE)
            total = jnp.sum(w, axis=1, keepdims=True) + jnp.sum(wf, axis=1, keepdims=True)
            o = jnp.dot(w.astype(jnp.bfloat16), value_ref[:, cols], preferred_element_type=jnp.float32)
            o += jnp.dot(wf.astype(jnp.bfloat16), fresh_value_ref[:, cols], preferred_element_type=jnp.float32)
            o = o * (1.0 / total)
            for ref, to, start, count in stores:
                ref[pl.ds(to, count), cols] = o[start:start + count].astype(ref.dtype)
            highs = jnp.where(lane == h, high, highs)
            totals = jnp.where(lane == h, total, totals)
        stats = pack_stats(highs, totals)
        for ref, to, start, count in stores:
            ref[pl.ds(to, count), width:] = stats[start:start + count].astype(ref.dtype)

    if 2 * half <= 128:
        attend_rows(0, 2 * half, [(keep_ref, 0, 0, half), (send_ref, 0, half, half)])
    else:
        for ref, base in ((keep_ref, 0), (send_ref, half)):
            @pl.loop(0, half // 128)
            def _(i, ref=ref, base=base):
                to = pl.multiple_of(i * 128, 128)
                attend_rows(base + to, 128, [(ref, to, 0, 128)])


def attend(slots, target, bias, fresh_bias, fresh_key, fresh_value, key, value, gathered):
    tokens, width = key.shape
    rows = target.shape[1] * SLOT // slots
    shape = (rows // 2, width + LANES)
    return pl.pallas_call(
        attend_kernel,
        out_shape=(jax.ShapeDtypeStruct(shape, jnp.float32), jax.ShapeDtypeStruct(shape, jnp.bfloat16)),
        in_specs=[VMEM] * (7 + len(gathered)),
        out_specs=(VMEM, VMEM),
        compiler_params=pltpu.CompilerParams(vmem_limit_bytes=24 << 20),
        cost_estimate=pl.CostEstimate(
            flops=4 * rows * tokens * width, bytes_accessed=4 * tokens * width,
            transcendentals=rows * tokens * width // HEAD,
        ),
        name="attend",
    )(target, bias, fresh_bias, fresh_key, fresh_value, key, value, *gathered)


def merge_kernel(count, last, *refs):
    parts, outs = refs[:count], refs[count:]
    rows, width = parts[0].shape
    width -= LANES
    stats = [unpack_stats(ref[:, width:].astype(jnp.float32)) for ref in parts]
    top = stats[0][0]
    for high, _ in stats[1:]:
        top = jnp.maximum(top, high)
    weights = [total * jnp.exp2((high - top) * SCALE) for high, total in stats]
    total = weights[0]
    for w in weights[1:]:
        total = total + w
    used = lax.broadcasted_iota(jnp.int32, total.shape, 1) < width // HEAD
    share = 1.0 / jnp.where(used, total, 1.0)
    weights = [w * share for w in weights]
    for h in range(width // HEAD):
        cols = slice(h * HEAD, (h + 1) * HEAD)
        o = parts[0][:, cols].astype(jnp.float32) * weights[0][:, h:h + 1]
        for ref, w in zip(parts[1:], weights[1:]):
            o = o + ref[:, cols].astype(jnp.float32) * w[:, h:h + 1]
        if last:
            for s in range(STEPS):
                outs[0][s, :, cols] = o[s * SLOT:(s + 1) * SLOT].astype(jnp.bfloat16)
        else:
            step = rows // len(outs)
            for n, ref in enumerate(outs):
                ref[:, cols] = o[n * step:(n + 1) * step].astype(ref.dtype)
    if not last:
        packed = pack_stats(jnp.where(used, top, 0.0), jnp.where(used, total, 0.0))
        for n, ref in enumerate(outs):
            ref[:, width:] = packed[n * step:(n + 1) * step].astype(ref.dtype)


def merge(parts, out_count, name):
    rows, width = parts[0].shape
    last = out_count == 0
    if last:
        shapes = (jax.ShapeDtypeStruct((STEPS, SLOT, width - LANES), jnp.bfloat16),)
    else:
        shapes = tuple(
            jax.ShapeDtypeStruct((rows // out_count, width), jnp.bfloat16 if n else jnp.float32)
            for n in range(out_count)
        )

    def kernel(*refs):
        merge_kernel(len(parts), last, *refs)

    return pl.pallas_call(
        kernel,
        out_shape=shapes,
        in_specs=[VMEM] * len(parts),
        out_specs=(VMEM,) * len(shapes),
        compiler_params=pltpu.CompilerParams(vmem_limit_bytes=16 << 20),
        name=name,
    )(*parts)


def body(cache_kv, fresh_qkv, list_rows, counts):
    device_count = lax.axis_size("blk")
    me = lax.axis_index("blk")
    far, near = mesh_digits(device_count)

    def swap(x, mask):
        return lax.ppermute(x, "blk", [(i, i ^ mask) for i in range(device_count)])

    fresh = fresh_qkv.transpose(1, 2, 0, 3)
    mine, fresh_key, fresh_value = (fresh[:, i] for i in range(3))
    table = jnp.concatenate([counts, list_rows, jnp.full((STEPS, 1), me, jnp.int32)], axis=1)
    ready = prepare(table, cache_kv, fresh_key, fresh_value)
    column = [swap(mine, k * near * 2) for k in range(1, far)]
    column, ready = lax.optimization_barrier((column, ready))
    column = jnp.concatenate([mine] + column)
    plane = [column] + [swap(column, k * 2) for k in range(1, near)]
    gathered = plane + [swap(x, 1) for x in plane]
    key, value, fresh_key, fresh_value, target, bias, fresh_bias = ready
    keep, send = attend(list_rows.shape[1], target, bias, fresh_bias, fresh_key, fresh_value, key, value, gathered)
    chips = near * far
    keep, *sends = merge([keep, swap(send, 1)], chips, "merge_core")
    sends = [swap(x, ((n % far) * near + n // far) * 2) for n, x in enumerate(sends, 1)]
    return merge([keep] + sends, 0, "merge_chips")[0]


def solution(mesh):
    in_specs = (
        P(("groups", "blk"), None, None),
        P(None, ("groups", "blk"), None, None),
        P(None, ("groups", "blk")),
        P(None, "groups"),
    )
    out_specs = P(None, ("groups", "blk"), None)
    return jax.shard_map(body, mesh=mesh, in_specs=in_specs, out_specs=out_specs, check_vma=False)
```

```python
import jax
import jax.numpy as jnp
from jax import lax
from jax.experimental import pallas as pl
from jax.experimental.pallas import tpu as pltpu
from jax.sharding import PartitionSpec as P

HEAD = 128
SLOT = 4
STEPS = 2
PAIR = STEPS * SLOT
LOG2E = 1.4426950408889634
SCALE = HEAD ** -0.5 * LOG2E
FAR = -1e30
LANES = 128
PART = 16
SLOT_BITS = 2
VMEM = pl.BlockSpec(memory_space=pltpu.VMEM)
SMEM = pl.BlockSpec(memory_space=pltpu.SMEM)
HBM = pl.BlockSpec(memory_space=pltpu.HBM)


def place_of(mask, bits):
    place = 0
    for n in range(bits):
        place = place + (((mask >> n) & 1) << (bits - 1 - n))
    return place


def prepare_kernel(table_ref, cache_ref, new_key_ref, new_value_ref,
                   key_ref, value_ref, fresh_key_ref, fresh_value_ref, target_ref, bias_ref, fresh_bias_ref,
                   held, sems):
    tokens, _, width = cache_ref.shape
    slots = new_key_ref.shape[0]
    device_count = table_ref.shape[1] - slots - 1
    bits = device_count.bit_length() - 1
    block = min(128, tokens)
    blocks = tokens // block

    def fetch(i):
        part = pl.ds(i * block, block)
        return pltpu.make_async_copy(cache_ref.at[part], held.at[part], sems.at[i])

    for i in range(blocks):
        fetch(i).start()

    me = table_ref[0, device_count + slots]
    col = lax.broadcasted_iota(jnp.int32, target_ref.shape, 1)

    def one_device(dev, carry):
        start0, start1, target = carry
        count0, count1 = table_ref[0, dev], table_ref[1, dev]
        local = col - place_of(dev ^ me, bits) * (STEPS * slots)
        slot, step = local >> 1, local & 1
        rank = slot + jnp.where(step == 0, start0, start1)
        row = place_of((rank >> SLOT_BITS) ^ me, bits) * PAIR + step * SLOT + (rank & (SLOT - 1))
        good = (local >= 0) & (slot < jnp.where(step == 0, count0, count1))
        return start0 + count0, start1 + count1, jnp.where(good, row, target)

    carry = (jnp.int32(0), jnp.int32(0), jnp.full(target_ref.shape, -1, jnp.int32))
    if device_count <= 16:
        for dev in range(device_count):
            carry = one_device(dev, carry)
    else:
        carry = lax.fori_loop(0, device_count, one_device, carry)
    target_ref[...] = carry[2]

    live0 = [i < table_ref[0, me] for i in range(slots)]
    live1 = [i < table_ref[1, me] for i in range(slots)]
    row0 = [jnp.where(live0[i], table_ref[0, device_count + i], -1) for i in range(slots)]
    row1 = [jnp.where(live1[i], table_ref[1, device_count + i], -2) for i in range(slots)]
    token = lax.broadcasted_iota(jnp.int32, bias_ref.shape, 1)
    second = lax.broadcasted_iota(jnp.int32, bias_ref.shape, 0) >= SLOT
    gone = token == row0[0]
    for i in range(1, slots):
        gone = gone | (token == row0[i])
    later = token == row1[0]
    for i in range(1, slots):
        later = later | (token == row1[i])
    bias_ref[...] = jnp.where(gone | (second & later), FAR, 0.0)
    col = lax.broadcasted_iota(jnp.int32, fresh_bias_ref.shape, 1)
    second = (lax.broadcasted_iota(jnp.int32, fresh_bias_ref.shape, 0) >= SLOT).astype(jnp.int32)
    seen = jnp.zeros(fresh_bias_ref.shape, jnp.int32)
    for i in range(slots):
        again = row1[0] == row0[i]
        for j in range(1, slots):
            again = again | (row1[j] == row0[i])
        kept = (live0[i] & jnp.logical_not(again)).astype(jnp.int32)
        early = jnp.where(second == 1, kept, live0[i].astype(jnp.int32))
        seen = jnp.where(col == 2 * i, early, seen)
        seen = jnp.where(col == 2 * i + 1, second * live1[i].astype(jnp.int32), seen)
    fresh_bias_ref[...] = jnp.where(seen == 1, 0.0, FAR)

    out = lax.broadcasted_iota(jnp.int32, (2 * block, 2 * block), 0)
    src = lax.broadcasted_iota(jnp.int32, (2 * block, 2 * block), 1)
    order = (src == jnp.where(out < block, 2 * out, 2 * (out - block) + 1)).astype(jnp.bfloat16)
    pairs = held.reshape(2 * tokens, width)
    for i in range(blocks):
        fetch(i).wait()
        rows = slice(i * block, (i + 1) * block)
        for c in range(0, width, 256):
            part = pairs[2 * i * block:2 * (i + 1) * block, c:c + 256]
            part = jnp.dot(order, part, preferred_element_type=jnp.float32).astype(jnp.bfloat16)
            key_ref[rows, c:c + 256] = part[:block]
            value_ref[rows, c:c + 256] = part[block:]
    for ref, new_ref in ((fresh_key_ref, new_key_ref), (fresh_value_ref, new_value_ref)):
        ref[...] = jnp.zeros_like(ref)
        ref[0:STEPS * slots, :] = new_ref.reshape(STEPS * slots, width)[...]


def prepare(table, cache, fresh_key, fresh_value):
    tokens, _, width = cache.shape
    slots = fresh_key.shape[0]
    device_count = table.shape[1] - slots - 1
    fresh_rows = -(-STEPS * slots // 16) * 16
    f32, bf16 = jnp.float32, jnp.bfloat16
    shapes = (
        jax.ShapeDtypeStruct((tokens, width), bf16),
        jax.ShapeDtypeStruct((tokens, width), bf16),
        jax.ShapeDtypeStruct((fresh_rows, width), bf16),
        jax.ShapeDtypeStruct((fresh_rows, width), bf16),
        jax.ShapeDtypeStruct((1, device_count * STEPS * slots), jnp.int32),
        jax.ShapeDtypeStruct((PAIR, tokens), f32),
        jax.ShapeDtypeStruct((PAIR, fresh_rows), f32),
    )
    blocks = tokens // min(128, tokens)
    return pl.pallas_call(
        prepare_kernel,
        out_shape=shapes,
        in_specs=[SMEM, HBM, VMEM, VMEM],
        out_specs=(VMEM,) * len(shapes),
        scratch_shapes=[
            pltpu.VMEM((tokens, 2, width), bf16),
            pltpu.SemaphoreType.DMA((blocks,)),
        ],
        compiler_params=pltpu.CompilerParams(vmem_limit_bytes=45 << 20),
        cost_estimate=pl.CostEstimate(
            flops=8 * 128 * tokens * width, bytes_accessed=8 * tokens * width, transcendentals=0
        ),
        name="prepare",
    )(table, cache, fresh_key, fresh_value)


def two_parts(x):
    high = x.astype(jnp.bfloat16).astype(jnp.float32)
    return high, x - high


def pack_stats(high, total):
    lane = lax.broadcasted_iota(jnp.int32, high.shape, 1)
    high = jnp.where(lane < PART, high, 0.0)
    total = jnp.where(lane < PART, total, 0.0)
    stats, rest = two_parts(high)
    second, third = two_parts(rest)
    for n, part in enumerate((second, third) + two_parts(total)):
        stats = stats + pltpu.roll(part, PART * (n + 1), 1)
    return stats


def unpack_stats(stats):
    def part(n):
        return pltpu.roll(stats, LANES - PART * n, 1)

    return stats + part(1) + part(2), part(3) + part(4)


def attend_kernel(target_ref, bias_ref, fresh_bias_ref, fresh_key_ref, fresh_value_ref, key_ref, value_ref, *rest):
    gathered_refs, (keep_ref, send_ref) = rest[:-2], rest[-2:]
    width = key_ref.shape[1]
    heads = width // HEAD
    half = keep_ref.shape[0]
    nt = (((1,), (1,)), ((), ()))

    def attend_rows(base, chunk, stores):
        row = lax.broadcasted_iota(jnp.int32, (chunk, target_ref.shape[1]), 0)
        pick = (row == target_ref[...] - base).astype(jnp.bfloat16)
        queries, at = None, 0
        for ref in gathered_refs:
            count = ref.shape[0] * STEPS
            slots = ref.reshape(count, width)[...]
            part = jnp.dot(pick[:, at:at + count], slots, preferred_element_type=jnp.float32)
            queries = part if queries is None else queries + part
            at += count
        queries = queries.astype(jnp.bfloat16)
        bias = bias_ref[...]
        fresh_bias = fresh_bias_ref[...]
        lane = lax.broadcasted_iota(jnp.int32, (chunk, LANES), 1)
        highs = jnp.zeros((chunk, LANES), jnp.float32)
        totals = jnp.zeros((chunk, LANES), jnp.float32)
        for h in range(heads):
            cols = slice(h * HEAD, (h + 1) * HEAD)
            q = queries[:, cols]
            s = lax.dot_general(q, key_ref[:, cols], nt, preferred_element_type=jnp.float32)
            sf = lax.dot_general(q, fresh_key_ref[:, cols], nt, preferred_element_type=jnp.float32)
            s = (s.reshape(chunk // PAIR, PAIR, -1) + bias[None]).reshape(chunk, -1)
            sf = (sf.reshape(chunk // PAIR, PAIR, -1) + fresh_bias[None]).reshape(chunk, -1)
            high = jnp.maximum(jnp.max(s, axis=1, keepdims=True), jnp.max(sf, axis=1, keepdims=True))
            w = jnp.exp2((s - high) * SCALE)
            wf = jnp.exp2((sf - high) * SCALE)
            total = jnp.sum(w, axis=1, keepdims=True) + jnp.sum(wf, axis=1, keepdims=True)
            o = jnp.dot(w.astype(jnp.bfloat16), value_ref[:, cols], preferred_element_type=jnp.float32)
            o += jnp.dot(wf.astype(jnp.bfloat16), fresh_value_ref[:, cols], preferred_element_type=jnp.float32)
            o = o * (1.0 / total)
            for ref, to, start, count in stores:
                ref[pl.ds(to, count), cols] = o[start:start + count].astype(ref.dtype)
            highs = jnp.where(lane == h, high, highs)
            totals = jnp.where(lane == h, total, totals)
        stats = pack_stats(highs, totals)
        for ref, to, start, count in stores:
            ref[pl.ds(to, count), width:] = stats[start:start + count].astype(ref.dtype)

    if 2 * half <= 128:
        attend_rows(0, 2 * half, [(keep_ref, 0, 0, half), (send_ref, 0, half, half)])
    else:
        for ref, base in ((keep_ref, 0), (send_ref, half)):
            @pl.loop(0, half // 128)
            def _(i, ref=ref, base=base):
                to = pl.multiple_of(i * 128, 128)
                attend_rows(base + to, 128, [(ref, to, 0, 128)])


def attend(slots, target, bias, fresh_bias, fresh_key, fresh_value, key, value, gathered):
    tokens, width = key.shape
    rows = target.shape[1] * SLOT // slots
    shape = (rows // 2, width + LANES)
    return pl.pallas_call(
        attend_kernel,
        out_shape=(jax.ShapeDtypeStruct(shape, jnp.float32), jax.ShapeDtypeStruct(shape, jnp.bfloat16)),
        in_specs=[VMEM] * (7 + len(gathered)),
        out_specs=(VMEM, VMEM),
        compiler_params=pltpu.CompilerParams(vmem_limit_bytes=24 << 20),
        cost_estimate=pl.CostEstimate(
            flops=4 * rows * tokens * width, bytes_accessed=4 * tokens * width,
            transcendentals=rows * tokens * width // HEAD,
        ),
        name="attend",
    )(target, bias, fresh_bias, fresh_key, fresh_value, key, value, *gathered)


def merge_kernel(count, last, *refs):
    parts, outs = refs[:count], refs[count:]
    rows, width = parts[0].shape
    width -= LANES
    stats = [unpack_stats(ref[:, width:].astype(jnp.float32)) for ref in parts]
    top = stats[0][0]
    for high, _ in stats[1:]:
        top = jnp.maximum(top, high)
    weights = [total * jnp.exp2((high - top) * SCALE) for high, total in stats]
    total = weights[0]
    for w in weights[1:]:
        total = total + w
    used = lax.broadcasted_iota(jnp.int32, total.shape, 1) < width // HEAD
    share = 1.0 / jnp.where(used, total, 1.0)
    weights = [w * share for w in weights]
    for h in range(width // HEAD):
        cols = slice(h * HEAD, (h + 1) * HEAD)
        o = parts[0][:, cols].astype(jnp.float32) * weights[0][:, h:h + 1]
        for ref, w in zip(parts[1:], weights[1:]):
            o = o + ref[:, cols].astype(jnp.float32) * w[:, h:h + 1]
        if last:
            for s in range(STEPS):
                outs[0][s, :, cols] = o[s * SLOT:(s + 1) * SLOT].astype(jnp.bfloat16)
        else:
            step = rows // len(outs)
            for n, ref in enumerate(outs):
                ref[:, cols] = o[n * step:(n + 1) * step].astype(ref.dtype)
    if not last:
        packed = pack_stats(jnp.where(used, top, 0.0), jnp.where(used, total, 0.0))
        for n, ref in enumerate(outs):
            ref[:, width:] = packed[n * step:(n + 1) * step].astype(ref.dtype)


def merge(parts, out_count, name):
    rows, width = parts[0].shape
    last = out_count == 0
    if last:
        shapes = (jax.ShapeDtypeStruct((STEPS, SLOT, width - LANES), jnp.bfloat16),)
    else:
        shapes = tuple(
            jax.ShapeDtypeStruct((rows // out_count, width), jnp.bfloat16 if n else jnp.float32)
            for n in range(out_count)
        )

    def kernel(*refs):
        merge_kernel(len(parts), last, *refs)

    return pl.pallas_call(
        kernel,
        out_shape=shapes,
        in_specs=[VMEM] * len(parts),
        out_specs=(VMEM,) * len(shapes),
        compiler_params=pltpu.CompilerParams(vmem_limit_bytes=16 << 20),
        name=name,
    )(*parts)


def body(cache_kv, fresh_qkv, list_rows, counts):
    device_count = lax.axis_size("blk")
    me = lax.axis_index("blk")
    slot_count = list_rows.shape[1]
    bits = device_count.bit_length() - 1

    def swap(x, mask):
        return lax.ppermute(x, "blk", [(i, i ^ mask) for i in range(device_count)])

    fresh = fresh_qkv.transpose(1, 2, 0, 3)
    mine, fresh_key, fresh_value = (fresh[:, i] for i in range(3))
    table = jnp.concatenate([counts, list_rows, jnp.full((STEPS, 1), me, jnp.int32)], axis=1)
    ready = prepare(table, cache_kv, fresh_key, fresh_value)
    held = mine
    for n in range(bits - 1, 1, -1):
        held = jnp.concatenate([held, swap(held, 1 << n)])
    across, beside = swap(held, 2), swap(held, 1)
    across, ready = lax.optimization_barrier((across, ready))
    gathered = [held, across, beside, swap(across, 1)]
    key, value, fresh_key, fresh_value, target, bias, fresh_bias = ready
    keep, send = attend(slot_count, target, bias, fresh_bias, fresh_key, fresh_value, key, value, gathered)
    for n in range(bits - 1):
        keep, send = merge([keep, swap(send, 1 << n)], 2, "merge_%d" % n)
    return merge([keep, swap(send, 1 << (bits - 1))], 0, "merge_last")[0]


def solution(mesh):
    in_specs = (
        P(("groups", "blk"), None, None),
        P(None, ("groups", "blk"), None, None),
        P(None, ("groups", "blk")),
        P(None, "groups"),
    )
    out_specs = P(None, ("groups", "blk"), None)
    return jax.shard_map(body, mesh=mesh, in_specs=in_specs, out_specs=out_specs, check_vma=False)
```

```python
import jax
import jax.numpy as jnp
from jax import lax
from jax.experimental import pallas as pl
from jax.experimental.pallas import tpu as pltpu
from jax.sharding import PartitionSpec as P

HEAD = 128
SLOT = 4
STEPS = 2
PAIR = STEPS * SLOT
LOG2E = 1.4426950408889634
SCALE = HEAD ** -0.5 * LOG2E
FAR = -1e30
LANES = 128
PART = 16
SLOT_BITS = 2
VMEM = pl.BlockSpec(memory_space=pltpu.VMEM)
SMEM = pl.BlockSpec(memory_space=pltpu.SMEM)
HBM = pl.BlockSpec(memory_space=pltpu.HBM)


def mesh_digits(device_count):
    bits = (device_count // 2).bit_length() - 1
    far_bits = (bits + 1) // 2
    return 1 << far_bits, 1 << (bits - far_bits)


def place_of(mask, far, near):
    near_bits = near.bit_length() - 1
    return ((mask & 1) * near + ((mask >> 1) & (near - 1))) * far + (mask >> (1 + near_bits))


def prepare_kernel(table_ref, cache_ref, new_key_ref, new_value_ref,
                   key_ref, value_ref, fresh_key_ref, fresh_value_ref, target_ref, bias_ref, fresh_bias_ref,
                   held, sems):
    tokens, _, width = cache_ref.shape
    slots = new_key_ref.shape[0]
    device_count = table_ref.shape[1] - slots - 1
    far, near = mesh_digits(device_count)
    block = min(128, tokens)
    blocks = tokens // block

    def fetch(i):
        part = pl.ds(i * block, block)
        return pltpu.make_async_copy(cache_ref.at[part], held.at[part], sems.at[i])

    for i in range(blocks):
        fetch(i).start()

    me = table_ref[0, device_count + slots]
    col = lax.broadcasted_iota(jnp.int32, target_ref.shape, 1)

    def one_device(dev, carry):
        start0, start1, target = carry
        count0, count1 = table_ref[0, dev], table_ref[1, dev]
        local = col - place_of(dev ^ me, far, near) * (STEPS * slots)
        slot, step = local >> 1, local & 1
        rank = slot + jnp.where(step == 0, start0, start1)
        home = rank >> SLOT_BITS
        home = ((home ^ me) & 1) * (device_count // 2) + (home >> 1)
        row = home * PAIR + step * SLOT + (rank & (SLOT - 1))
        good = (local >= 0) & (slot < jnp.where(step == 0, count0, count1))
        return start0 + count0, start1 + count1, jnp.where(good, row, target)

    carry = (jnp.int32(0), jnp.int32(0), jnp.full(target_ref.shape, -1, jnp.int32))
    if device_count <= 16:
        for dev in range(device_count):
            carry = one_device(dev, carry)
    else:
        carry = lax.fori_loop(0, device_count, one_device, carry)
    target_ref[...] = carry[2]

    live0 = [i < table_ref[0, me] for i in range(slots)]
    live1 = [i < table_ref[1, me] for i in range(slots)]
    row0 = [jnp.where(live0[i], table_ref[0, device_count + i], -1) for i in range(slots)]
    row1 = [jnp.where(live1[i], table_ref[1, device_count + i], -2) for i in range(slots)]
    token = lax.broadcasted_iota(jnp.int32, bias_ref.shape, 1)
    second = lax.broadcasted_iota(jnp.int32, bias_ref.shape, 0) >= SLOT
    gone = token == row0[0]
    for i in range(1, slots):
        gone = gone | (token == row0[i])
    later = token == row1[0]
    for i in range(1, slots):
        later = later | (token == row1[i])
    bias_ref[...] = jnp.where(gone | (second & later), FAR, 0.0)
    col = lax.broadcasted_iota(jnp.int32, fresh_bias_ref.shape, 1)
    second = (lax.broadcasted_iota(jnp.int32, fresh_bias_ref.shape, 0) >= SLOT).astype(jnp.int32)
    seen = jnp.zeros(fresh_bias_ref.shape, jnp.int32)
    for i in range(slots):
        again = row1[0] == row0[i]
        for j in range(1, slots):
            again = again | (row1[j] == row0[i])
        kept = (live0[i] & jnp.logical_not(again)).astype(jnp.int32)
        early = jnp.where(second == 1, kept, live0[i].astype(jnp.int32))
        seen = jnp.where(col == 2 * i, early, seen)
        seen = jnp.where(col == 2 * i + 1, second * live1[i].astype(jnp.int32), seen)
    fresh_bias_ref[...] = jnp.where(seen == 1, 0.0, FAR)

    out = lax.broadcasted_iota(jnp.int32, (2 * block, 2 * block), 0)
    src = lax.broadcasted_iota(jnp.int32, (2 * block, 2 * block), 1)
    order = (src == jnp.where(out < block, 2 * out, 2 * (out - block) + 1)).astype(jnp.bfloat16)
    pairs = held.reshape(2 * tokens, width)
    for i in range(blocks):
        fetch(i).wait()
        rows = slice(i * block, (i + 1) * block)
        for c in range(0, width, 256):
            part = pairs[2 * i * block:2 * (i + 1) * block, c:c + 256]
            part = jnp.dot(order, part, preferred_element_type=jnp.float32).astype(jnp.bfloat16)
            key_ref[rows, c:c + 256] = part[:block]
            value_ref[rows, c:c + 256] = part[block:]
    for ref, new_ref in ((fresh_key_ref, new_key_ref), (fresh_value_ref, new_value_ref)):
        ref[...] = jnp.zeros_like(ref)
        ref[0:STEPS * slots, :] = new_ref.reshape(STEPS * slots, width)[...]


def prepare(table, cache, fresh_key, fresh_value):
    tokens, _, width = cache.shape
    slots = fresh_key.shape[0]
    device_count = table.shape[1] - slots - 1
    fresh_rows = -(-STEPS * slots // 16) * 16
    f32, bf16 = jnp.float32, jnp.bfloat16
    shapes = (
        jax.ShapeDtypeStruct((tokens, width), bf16),
        jax.ShapeDtypeStruct((tokens, width), bf16),
        jax.ShapeDtypeStruct((fresh_rows, width), bf16),
        jax.ShapeDtypeStruct((fresh_rows, width), bf16),
        jax.ShapeDtypeStruct((1, device_count * STEPS * slots), jnp.int32),
        jax.ShapeDtypeStruct((PAIR, tokens), f32),
        jax.ShapeDtypeStruct((PAIR, fresh_rows), f32),
    )
    blocks = tokens // min(128, tokens)
    return pl.pallas_call(
        prepare_kernel,
        out_shape=shapes,
        in_specs=[SMEM, HBM, VMEM, VMEM],
        out_specs=(VMEM,) * len(shapes),
        scratch_shapes=[
            pltpu.VMEM((tokens, 2, width), bf16),
            pltpu.SemaphoreType.DMA((blocks,)),
        ],
        compiler_params=pltpu.CompilerParams(vmem_limit_bytes=45 << 20),
        cost_estimate=pl.CostEstimate(
            flops=8 * 128 * tokens * width, bytes_accessed=8 * tokens * width, transcendentals=0
        ),
        name="prepare",
    )(table, cache, fresh_key, fresh_value)


def two_parts(x):
    high = x.astype(jnp.bfloat16).astype(jnp.float32)
    return high, x - high


def pack_stats(high, total):
    lane = lax.broadcasted_iota(jnp.int32, high.shape, 1)
    high = jnp.where(lane < PART, high, 0.0)
    total = jnp.where(lane < PART, total, 0.0)
    stats, rest = two_parts(high)
    second, third = two_parts(rest)
    for n, part in enumerate((second, third) + two_parts(total)):
        stats = stats + pltpu.roll(part, PART * (n + 1), 1)
    return stats


def unpack_stats(stats):
    def part(n):
        return pltpu.roll(stats, LANES - PART * n, 1)

    return stats + part(1) + part(2), part(3) + part(4)


def attend_kernel(target_ref, bias_ref, fresh_bias_ref, fresh_key_ref, fresh_value_ref, key_ref, value_ref, *rest):
    gathered_refs, (keep_ref, send_ref) = rest[:-2], rest[-2:]
    width = key_ref.shape[1]
    heads = width // HEAD
    half = keep_ref.shape[0]
    nt = (((1,), (1,)), ((), ()))

    def attend_rows(base, chunk, stores):
        row = lax.broadcasted_iota(jnp.int32, (chunk, target_ref.shape[1]), 0)
        pick = (row == target_ref[...] - base).astype(jnp.bfloat16)
        queries, at = None, 0
        for ref in gathered_refs:
            count = ref.shape[0] * STEPS
            slots = ref.reshape(count, width)[...]
            part = jnp.dot(pick[:, at:at + count], slots, preferred_element_type=jnp.float32)
            queries = part if queries is None else queries + part
            at += count
        queries = queries.astype(jnp.bfloat16)
        bias = bias_ref[...]
        fresh_bias = fresh_bias_ref[...]
        lane = lax.broadcasted_iota(jnp.int32, (chunk, LANES), 1)
        highs = jnp.zeros((chunk, LANES), jnp.float32)
        totals = jnp.zeros((chunk, LANES), jnp.float32)
        for h in range(heads):
            cols = slice(h * HEAD, (h + 1) * HEAD)
            q = queries[:, cols]
            s = lax.dot_general(q, key_ref[:, cols], nt, preferred_element_type=jnp.float32)
            sf = lax.dot_general(q, fresh_key_ref[:, cols], nt, preferred_element_type=jnp.float32)
            s = (s.reshape(chunk // PAIR, PAIR, -1) + bias[None]).reshape(chunk, -1)
            sf = (sf.reshape(chunk // PAIR, PAIR, -1) + fresh_bias[None]).reshape(chunk, -1)
            high = jnp.maximum(jnp.max(s, axis=1, keepdims=True), jnp.max(sf, axis=1, keepdims=True))
            w = jnp.exp2((s - high) * SCALE)
            wf = jnp.exp2((sf - high) * SCALE)
            total = jnp.sum(w, axis=1, keepdims=True) + jnp.sum(wf, axis=1, keepdims=True)
            o = jnp.dot(w.astype(jnp.bfloat16), value_ref[:, cols], preferred_element_type=jnp.float32)
            o += jnp.dot(wf.astype(jnp.bfloat16), fresh_value_ref[:, cols], preferred_element_type=jnp.float32)
            o = o * (1.0 / total)
            for ref, to, start, count in stores:
                ref[pl.ds(to, count), cols] = o[start:start + count].astype(ref.dtype)
            highs = jnp.where(lane == h, high, highs)
            totals = jnp.where(lane == h, total, totals)
        stats = pack_stats(highs, totals)
        for ref, to, start, count in stores:
            ref[pl.ds(to, count), width:] = stats[start:start + count].astype(ref.dtype)

    if 2 * half <= 128:
        attend_rows(0, 2 * half, [(keep_ref, 0, 0, half), (send_ref, 0, half, half)])
    else:
        for ref, base in ((keep_ref, 0), (send_ref, half)):
            @pl.loop(0, half // 128)
            def _(i, ref=ref, base=base):
                to = pl.multiple_of(i * 128, 128)
                attend_rows(base + to, 128, [(ref, to, 0, 128)])


def attend(slots, target, bias, fresh_bias, fresh_key, fresh_value, key, value, gathered):
    tokens, width = key.shape
    rows = target.shape[1] * SLOT // slots
    shape = (rows // 2, width + LANES)
    return pl.pallas_call(
        attend_kernel,
        out_shape=(jax.ShapeDtypeStruct(shape, jnp.float32), jax.ShapeDtypeStruct(shape, jnp.bfloat16)),
        in_specs=[VMEM] * (7 + len(gathered)),
        out_specs=(VMEM, VMEM),
        compiler_params=pltpu.CompilerParams(vmem_limit_bytes=24 << 20),
        cost_estimate=pl.CostEstimate(
            flops=4 * rows * tokens * width, bytes_accessed=4 * tokens * width,
            transcendentals=rows * tokens * width // HEAD,
        ),
        name="attend",
    )(target, bias, fresh_bias, fresh_key, fresh_value, key, value, *gathered)


def merged(parts):
    width = parts[0].shape[1] - LANES
    stats = [unpack_stats(part[:, width:].astype(jnp.float32)) for part in parts]
    top = stats[0][0]
    for high, _ in stats[1:]:
        top = jnp.maximum(top, high)
    weights = [total * jnp.exp2((high - top) * SCALE) for high, total in stats]
    total = weights[0]
    for w in weights[1:]:
        total = total + w
    used = lax.broadcasted_iota(jnp.int32, total.shape, 1) < width // HEAD
    share = 1.0 / jnp.where(used, total, 1.0)
    weights = [w * share for w in weights]
    for h in range(width // HEAD):
        cols = slice(h * HEAD, (h + 1) * HEAD)
        o = parts[0][:, cols].astype(jnp.float32) * weights[0][:, h:h + 1]
        for part, w in zip(parts[1:], weights[1:]):
            o = o + part[:, cols].astype(jnp.float32) * w[:, h:h + 1]
        yield cols, o
    yield slice(width, width + LANES), pack_stats(jnp.where(used, top, 0.0), jnp.where(used, total, 0.0))


def merge_cores_kernel(keep_ref, other_ref, out_ref):
    for cols, o in merged([keep_ref, other_ref]):
        out_ref[:, :, cols] = o.reshape(o.shape[0] // PAIR, PAIR, -1).astype(jnp.bfloat16)


def merge_chips_kernel(parts_ref, out_ref):
    width = out_ref.shape[2]
    for cols, o in merged([parts_ref.at[n] for n in range(parts_ref.shape[0])]):
        if cols.start < width:
            for s in range(STEPS):
                out_ref[s, :, cols] = o[s * SLOT:(s + 1) * SLOT].astype(jnp.bfloat16)


def merge(kernel, parts, shape, name):
    return pl.pallas_call(
        kernel,
        out_shape=jax.ShapeDtypeStruct(shape, jnp.bfloat16),
        in_specs=[VMEM] * len(parts),
        out_specs=VMEM,
        compiler_params=pltpu.CompilerParams(vmem_limit_bytes=16 << 20),
        name=name,
    )(*parts)


def body(cache_kv, fresh_qkv, list_rows, counts):
    device_count = lax.axis_size("blk")
    me = lax.axis_index("blk")
    slot_count = list_rows.shape[1]
    far, near = mesh_digits(device_count)
    width = cache_kv.shape[2]

    def swap(x, mask):
        return lax.ppermute(x, "blk", [(i, i ^ mask) for i in range(device_count)])

    fresh = fresh_qkv.transpose(1, 2, 0, 3)
    mine, fresh_key, fresh_value = (fresh[:, i] for i in range(3))
    table = jnp.concatenate([counts, list_rows, jnp.full((STEPS, 1), me, jnp.int32)], axis=1)
    ready = prepare(table, cache_kv, fresh_key, fresh_value)
    plane = [jnp.concatenate([mine] + [swap(mine, k * near * 2) for k in range(1, far)])]
    across = [swap(plane[0], k * 2) for k in range(1, near)]
    beside = swap(plane[0], 1)
    across, ready = lax.optimization_barrier((across, ready))
    gathered = plane + across + [beside] + [swap(x, 1) for x in across]
    key, value, fresh_key, fresh_value, target, bias, fresh_bias = ready
    keep, send = attend(slot_count, target, bias, fresh_bias, fresh_key, fresh_value, key, value, gathered)
    chips = device_count // 2
    parts = merge(merge_cores_kernel, [keep, swap(send, 1)], (chips, PAIR, width + LANES), "merge_cores")
    groups = [[chip * 2 + core for chip in range(chips)] for core in range(2)]
    parts = lax.all_to_all(parts, "blk", split_axis=0, concat_axis=0, axis_index_groups=groups, tiled=True)
    return merge(merge_chips_kernel, [parts], (STEPS, SLOT, width), "merge_chips")


def solution(mesh):
    in_specs = (
        P(("groups", "blk"), None, None),
        P(None, ("groups", "blk"), None, None),
        P(None, ("groups", "blk")),
        P(None, "groups"),
    )
    out_specs = P(None, ("groups", "blk"), None)
    return jax.shard_map(body, mesh=mesh, in_specs=in_specs, out_specs=out_specs, check_vma=False)
```

```python
import jax
import jax.numpy as jnp
from jax import lax
from jax.experimental import pallas as pl
from jax.experimental.pallas import tpu as pltpu
from jax.sharding import PartitionSpec as P

HEAD = 128
SLOT = 4
STEPS = 2
PAIR = STEPS * SLOT
LOG2E = 1.4426950408889634
SCALE = HEAD ** -0.5 * LOG2E
FAR = -1e30
LANES = 128
PART = 16
SLOT_BITS = 2
VMEM = pl.BlockSpec(memory_space=pltpu.VMEM)
SMEM = pl.BlockSpec(memory_space=pltpu.SMEM)
HBM = pl.BlockSpec(memory_space=pltpu.HBM)


def mesh_digits(device_count):
    bits = (device_count // 2).bit_length() - 1
    far_bits = (bits + 1) // 2
    return 1 << far_bits, 1 << (bits - far_bits)


def place_of(mask, far, near):
    near_bits = near.bit_length() - 1
    return ((mask & 1) * near + ((mask >> 1) & (near - 1))) * far + (mask >> (1 + near_bits))


def prepare_kernel(table_ref, cache_ref, new_key_ref, new_value_ref,
                   key_ref, value_ref, fresh_key_ref, fresh_value_ref, target_ref, bias_ref, fresh_bias_ref,
                   held, sems):
    tokens, _, width = cache_ref.shape
    slots = new_key_ref.shape[0]
    device_count = table_ref.shape[1] - slots - 1
    far, near = mesh_digits(device_count)
    block = min(128, tokens)
    blocks = tokens // block

    def fetch(i):
        part = pl.ds(i * block, block)
        return pltpu.make_async_copy(cache_ref.at[part], held.at[part, :, pl.ds(0, width)], sems.at[i])

    for i in range(blocks):
        fetch(i).start()

    me = table_ref[0, device_count + slots]
    col = lax.broadcasted_iota(jnp.int32, target_ref.shape, 1)

    def one_device(dev, carry):
        start0, start1, target = carry
        count0, count1 = table_ref[0, dev], table_ref[1, dev]
        local = col - place_of(dev ^ me, far, near) * (STEPS * slots)
        slot, step = local >> 1, local & 1
        rank = slot + jnp.where(step == 0, start0, start1)
        home = rank >> SLOT_BITS
        home = ((home ^ me) & 1) * (device_count // 2) + (home >> 1)
        row = home * PAIR + step * SLOT + (rank & (SLOT - 1))
        good = (local >= 0) & (slot < jnp.where(step == 0, count0, count1))
        return start0 + count0, start1 + count1, jnp.where(good, row, target)

    carry = (jnp.int32(0), jnp.int32(0), jnp.full(target_ref.shape, -1, jnp.int32))
    if device_count <= 16:
        for dev in range(device_count):
            carry = one_device(dev, carry)
    else:
        carry = lax.fori_loop(0, device_count, one_device, carry)
    target_ref[...] = carry[2]

    live0 = [i < table_ref[0, me] for i in range(slots)]
    live1 = [i < table_ref[1, me] for i in range(slots)]
    row0 = [jnp.where(live0[i], table_ref[0, device_count + i], -1) for i in range(slots)]
    row1 = [jnp.where(live1[i], table_ref[1, device_count + i], -2) for i in range(slots)]
    token = lax.broadcasted_iota(jnp.int32, bias_ref.shape, 1)
    second = lax.broadcasted_iota(jnp.int32, bias_ref.shape, 0) >= SLOT
    gone = token == row0[0]
    for i in range(1, slots):
        gone = gone | (token == row0[i])
    later = token == row1[0]
    for i in range(1, slots):
        later = later | (token == row1[i])
    bias_ref[...] = jnp.where(gone | (second & later), FAR, 0.0)
    col = lax.broadcasted_iota(jnp.int32, fresh_bias_ref.shape, 1)
    second = (lax.broadcasted_iota(jnp.int32, fresh_bias_ref.shape, 0) >= SLOT).astype(jnp.int32)
    seen = jnp.zeros(fresh_bias_ref.shape, jnp.int32)
    for i in range(slots):
        again = row1[0] == row0[i]
        for j in range(1, slots):
            again = again | (row1[j] == row0[i])
        kept = (live0[i] & jnp.logical_not(again)).astype(jnp.int32)
        early = jnp.where(second == 1, kept, live0[i].astype(jnp.int32))
        seen = jnp.where(col == 2 * i, early, seen)
        seen = jnp.where(col == 2 * i + 1, second * live1[i].astype(jnp.int32), seen)
    fresh_bias_ref[...] = jnp.where(seen == 1, 0.0, FAR)

    out = lax.broadcasted_iota(jnp.int32, (2 * block, 2 * block), 0)
    src = lax.broadcasted_iota(jnp.int32, (2 * block, 2 * block), 1)
    order = (src == jnp.where(out < block, 2 * out, 2 * (out - block) + 1)).astype(jnp.bfloat16)
    pairs = held.reshape(2 * tokens, held.shape[2])
    for i in range(blocks):
        fetch(i).wait()
        rows = slice(i * block, (i + 1) * block)
        for c in range(0, width, 256):
            part = pairs[2 * i * block:2 * (i + 1) * block, c:c + 256]
            part = jnp.dot(order, part, preferred_element_type=jnp.float32).astype(jnp.bfloat16)
            key_ref[rows, c:c + 256] = part[:block]
            value_ref[rows, c:c + 256] = part[block:]
    for ref, new_ref in ((fresh_key_ref, new_key_ref), (fresh_value_ref, new_value_ref)):
        ref[...] = jnp.zeros_like(ref)
        ref[0:STEPS * slots, :] = new_ref.reshape(STEPS * slots, width)[...]


def prepare(table, cache, fresh_key, fresh_value):
    tokens, _, width = cache.shape
    slots = fresh_key.shape[0]
    device_count = table.shape[1] - slots - 1
    fresh_rows = -(-STEPS * slots // 16) * 16
    f32, bf16 = jnp.float32, jnp.bfloat16
    shapes = (
        jax.ShapeDtypeStruct((tokens, width), bf16),
        jax.ShapeDtypeStruct((tokens, width), bf16),
        jax.ShapeDtypeStruct((fresh_rows, width), bf16),
        jax.ShapeDtypeStruct((fresh_rows, width), bf16),
        jax.ShapeDtypeStruct((1, device_count * STEPS * slots), jnp.int32),
        jax.ShapeDtypeStruct((PAIR, tokens), f32),
        jax.ShapeDtypeStruct((PAIR, fresh_rows), f32),
    )
    blocks = tokens // min(128, tokens)
    return pl.pallas_call(
        prepare_kernel,
        out_shape=shapes,
        in_specs=[SMEM, HBM, VMEM, VMEM],
        out_specs=(VMEM,) * len(shapes),
        scratch_shapes=[
            pltpu.VMEM((tokens, 2, width + LANES), bf16),
            pltpu.SemaphoreType.DMA((blocks,)),
        ],
        compiler_params=pltpu.CompilerParams(vmem_limit_bytes=45 << 20),
        cost_estimate=pl.CostEstimate(
            flops=8 * 128 * tokens * width, bytes_accessed=8 * tokens * width, transcendentals=0
        ),
        name="prepare",
    )(table, cache, fresh_key, fresh_value)


def two_parts(x):
    high = x.astype(jnp.bfloat16).astype(jnp.float32)
    return high, x - high


def pack_stats(high, total):
    lane = lax.broadcasted_iota(jnp.int32, high.shape, 1)
    high = jnp.where(lane < PART, high, 0.0)
    total = jnp.where(lane < PART, total, 0.0)
    stats, rest = two_parts(high)
    second, third = two_parts(rest)
    for n, part in enumerate((second, third) + two_parts(total)):
        stats = stats + pltpu.roll(part, PART * (n + 1), 1)
    return stats


def unpack_stats(stats):
    def part(n):
        return pltpu.roll(stats, LANES - PART * n, 1)

    return stats + part(1) + part(2), part(3) + part(4)


def attend_kernel(target_ref, bias_ref, fresh_bias_ref, fresh_key_ref, fresh_value_ref, key_ref, value_ref, *rest):
    gathered_refs, (keep_ref, send_ref) = rest[:-2], rest[-2:]
    width = key_ref.shape[1]
    heads = width // HEAD
    half = keep_ref.shape[0]
    nt = (((1,), (1,)), ((), ()))

    def attend_rows(base, chunk, stores):
        row = lax.broadcasted_iota(jnp.int32, (chunk, target_ref.shape[1]), 0)
        pick = (row == target_ref[...] - base).astype(jnp.bfloat16)
        queries, at = None, 0
        for ref in gathered_refs:
            count = ref.shape[0] * STEPS
            slots = ref.reshape(count, width)[...]
            part = jnp.dot(pick[:, at:at + count], slots, preferred_element_type=jnp.float32)
            queries = part if queries is None else queries + part
            at += count
        queries = queries.astype(jnp.bfloat16)
        bias = bias_ref[...]
        fresh_bias = fresh_bias_ref[...]
        lane = lax.broadcasted_iota(jnp.int32, (chunk, LANES), 1)
        highs = jnp.zeros((chunk, LANES), jnp.float32)
        totals = jnp.zeros((chunk, LANES), jnp.float32)
        ones = jnp.ones((key_ref.shape[0], LANES), jnp.bfloat16)

        def score(h):
            cols = slice(h * HEAD, (h + 1) * HEAD)
            q = queries[:, cols]
            s = lax.dot_general(q, key_ref[:, cols], nt, preferred_element_type=jnp.float32)
            sf = lax.dot_general(q, fresh_key_ref[:, cols], nt, preferred_element_type=jnp.float32)
            s = (s.reshape(chunk // PAIR, PAIR, -1) + bias[None]).reshape(chunk, -1)
            sf = (sf.reshape(chunk // PAIR, PAIR, -1) + fresh_bias[None]).reshape(chunk, -1)
            return s, sf

        following = score(0)
        for h in range(heads):
            cols = slice(h * HEAD, (h + 1) * HEAD)
            s, sf = following
            if h + 1 < heads:
                following = score(h + 1)
            high = jnp.maximum(jnp.max(s, axis=1, keepdims=True), jnp.max(sf, axis=1, keepdims=True))
            w = jnp.exp2((s - high) * SCALE).astype(jnp.bfloat16)
            wf = jnp.exp2((sf - high) * SCALE).astype(jnp.bfloat16)
            value = jnp.concatenate([value_ref[:, cols], ones], axis=1)
            fresh_value = jnp.concatenate([fresh_value_ref[:, cols], ones[:fresh_value_ref.shape[0]]], axis=1)
            o = jnp.dot(w, value, preferred_element_type=jnp.float32)
            o += jnp.dot(wf, fresh_value, preferred_element_type=jnp.float32)
            total = o[:, HEAD:]
            o = o[:, :HEAD] * (1.0 / total)
            for ref, to, start, count in stores:
                ref[pl.ds(to, count), cols] = o[start:start + count].astype(ref.dtype)
            highs = jnp.where(lane == h, high, highs)
            totals = jnp.where(lane == h, total, totals)
        stats = pack_stats(highs, totals)
        for ref, to, start, count in stores:
            ref[pl.ds(to, count), width:] = stats[start:start + count].astype(ref.dtype)

    if 2 * half <= 128:
        attend_rows(0, 2 * half, [(keep_ref, 0, 0, half), (send_ref, 0, half, half)])
    else:
        for ref, base in ((keep_ref, 0), (send_ref, half)):
            @pl.loop(0, half // 128)
            def _(i, ref=ref, base=base):
                to = pl.multiple_of(i * 128, 128)
                attend_rows(base + to, 128, [(ref, to, 0, 128)])


def attend(slots, target, bias, fresh_bias, fresh_key, fresh_value, key, value, gathered):
    tokens, width = key.shape
    rows = target.shape[1] * SLOT // slots
    shape = (rows // 2, width + LANES)
    return pl.pallas_call(
        attend_kernel,
        out_shape=(jax.ShapeDtypeStruct(shape, jnp.float32), jax.ShapeDtypeStruct(shape, jnp.bfloat16)),
        in_specs=[VMEM] * (7 + len(gathered)),
        out_specs=(VMEM, VMEM),
        compiler_params=pltpu.CompilerParams(vmem_limit_bytes=24 << 20),
        cost_estimate=pl.CostEstimate(
            flops=4 * rows * tokens * width, bytes_accessed=4 * tokens * width,
            transcendentals=rows * tokens * width // HEAD,
        ),
        name="attend",
    )(target, bias, fresh_bias, fresh_key, fresh_value, key, value, *gathered)


def merged(parts):
    width = parts[0].shape[1] - LANES
    stats = [unpack_stats(part[:, width:].astype(jnp.float32)) for part in parts]
    top = stats[0][0]
    for high, _ in stats[1:]:
        top = jnp.maximum(top, high)
    weights = [total * jnp.exp2((high - top) * SCALE) for high, total in stats]
    total = weights[0]
    for w in weights[1:]:
        total = total + w
    used = lax.broadcasted_iota(jnp.int32, total.shape, 1) < width // HEAD
    share = 1.0 / jnp.where(used, total, 1.0)
    weights = [w * share for w in weights]
    for h in range(width // HEAD):
        cols = slice(h * HEAD, (h + 1) * HEAD)
        o = parts[0][:, cols].astype(jnp.float32) * weights[0][:, h:h + 1]
        for part, w in zip(parts[1:], weights[1:]):
            o = o + part[:, cols].astype(jnp.float32) * w[:, h:h + 1]
        yield cols, o
    yield slice(width, width + LANES), pack_stats(jnp.where(used, top, 0.0), jnp.where(used, total, 0.0))


def merge_cores_kernel(keep_ref, other_ref, out_ref):
    for cols, o in merged([keep_ref, other_ref]):
        out_ref[:, :, cols] = o.reshape(o.shape[0] // PAIR, PAIR, -1).astype(jnp.bfloat16)


def merge_chips_kernel(parts_ref, out_ref):
    width = out_ref.shape[2]
    for cols, o in merged([parts_ref.at[n] for n in range(parts_ref.shape[0])]):
        if cols.start < width:
            for s in range(STEPS):
                out_ref[s, :, cols] = o[s * SLOT:(s + 1) * SLOT].astype(jnp.bfloat16)


def merge(kernel, parts, shape, name):
    return pl.pallas_call(
        kernel,
        out_shape=jax.ShapeDtypeStruct(shape, jnp.bfloat16),
        in_specs=[VMEM] * len(parts),
        out_specs=VMEM,
        compiler_params=pltpu.CompilerParams(vmem_limit_bytes=16 << 20),
        name=name,
    )(*parts)


def body(cache_kv, fresh_qkv, list_rows, counts):
    device_count = lax.axis_size("blk")
    me = lax.axis_index("blk")
    slot_count = list_rows.shape[1]
    far, near = mesh_digits(device_count)
    width = cache_kv.shape[2]

    def swap(x, mask):
        return lax.ppermute(x, "blk", [(i, i ^ mask) for i in range(device_count)])

    fresh = fresh_qkv.transpose(1, 2, 0, 3)
    mine, fresh_key, fresh_value = (fresh[:, i] for i in range(3))
    table = jnp.concatenate([counts, list_rows, jnp.full((STEPS, 1), me, jnp.int32)], axis=1)
    ready = prepare(table, cache_kv, fresh_key, fresh_value)
    plane = [jnp.concatenate([mine] + [swap(mine, k * near * 2) for k in range(1, far)])]
    across = [swap(plane[0], k * 2) for k in range(1, near)]
    beside = swap(plane[0], 1)
    across, ready = lax.optimization_barrier((across, ready))
    gathered = plane + across + [beside] + [swap(x, 1) for x in across]
    key, value, fresh_key, fresh_value, target, bias, fresh_bias = ready
    keep, send = attend(slot_count, target, bias, fresh_bias, fresh_key, fresh_value, key, value, gathered)
    chips = device_count // 2
    parts = merge(merge_cores_kernel, [keep, swap(send, 1)], (chips, PAIR, width + LANES), "merge_cores")
    groups = [[chip * 2 + core for chip in range(chips)] for core in range(2)]
    parts = lax.all_to_all(parts, "blk", split_axis=0, concat_axis=0, axis_index_groups=groups, tiled=True)
    return merge(merge_chips_kernel, [parts], (STEPS, SLOT, width), "merge_chips")


def solution(mesh):
    in_specs = (
        P(("groups", "blk"), None, None),
        P(None, ("groups", "blk"), None, None),
        P(None, ("groups", "blk")),
        P(None, "groups"),
    )
    out_specs = P(None, ("groups", "blk"), None)
    return jax.shard_map(body, mesh=mesh, in_specs=in_specs, out_specs=out_specs, check_vma=False)
```

```python
import jax
import jax.numpy as jnp
from jax import lax
from jax.experimental import pallas as pl
from jax.experimental.pallas import tpu as pltpu
from jax.sharding import PartitionSpec as P

HEAD = 128
SLOT = 4
STEPS = 2
PAIR = STEPS * SLOT
LOG2E = 1.4426950408889634
SCALE = HEAD ** -0.5 * LOG2E
FAR = -1e30
LANES = 128
PART = 16
SLOT_BITS = 2
WAITS = 4
VMEM = pl.BlockSpec(memory_space=pltpu.VMEM)
SMEM = pl.BlockSpec(memory_space=pltpu.SMEM)
HBM = pl.BlockSpec(memory_space=pltpu.HBM)


def turned(mask, bits):
    place = 0
    for n in range(bits):
        place = place + (((mask >> n) & 1) << (bits - 1 - n))
    return place


def prepare_kernel(table_ref, cache_ref, new_key_ref, new_value_ref,
                   key_ref, value_ref, fresh_key_ref, fresh_value_ref, target_ref, bias_ref, fresh_bias_ref,
                   held, sems):
    tokens, _, width = cache_ref.shape
    slots = new_key_ref.shape[0]
    device_count = table_ref.shape[1] - slots - 1
    bits = device_count.bit_length() - 1
    block = min(128, tokens)
    blocks = tokens // block

    def fetch(i):
        part = pl.ds(i * block, block)
        return pltpu.make_async_copy(cache_ref.at[part], held.at[part, :, pl.ds(0, width)], sems.at[i])

    for i in range(blocks):
        fetch(i).start()

    me = table_ref[0, device_count + slots]
    col = lax.broadcasted_iota(jnp.int32, target_ref.shape, 1)

    def one_device(dev, carry):
        start0, start1, target = carry
        count0, count1 = table_ref[0, dev], table_ref[1, dev]
        local = col - turned(dev ^ me, bits) * (STEPS * slots)
        slot, step = local >> 1, local & 1
        rank = slot + jnp.where(step == 0, start0, start1)
        home = rank >> SLOT_BITS
        home = (((home ^ me) & 1) * 4 + ((home >> 1) & 3)) * (device_count // 8) + turned((home ^ me) >> 3, bits - 3)
        row = home * PAIR + step * SLOT + (rank & (SLOT - 1))
        good = (local >= 0) & (slot < jnp.where(step == 0, count0, count1))
        return start0 + count0, start1 + count1, jnp.where(good, row, target)

    carry = (jnp.int32(0), jnp.int32(0), jnp.full(target_ref.shape, -1, jnp.int32))
    if device_count <= 16:
        for dev in range(device_count):
            carry = one_device(dev, carry)
    else:
        carry = lax.fori_loop(0, device_count, one_device, carry)
    target_ref[...] = carry[2]

    live0 = [i < table_ref[0, me] for i in range(slots)]
    live1 = [i < table_ref[1, me] for i in range(slots)]
    row0 = [jnp.where(live0[i], table_ref[0, device_count + i], -1) for i in range(slots)]
    row1 = [jnp.where(live1[i], table_ref[1, device_count + i], -2) for i in range(slots)]
    token = lax.broadcasted_iota(jnp.int32, bias_ref.shape, 1)
    second = lax.broadcasted_iota(jnp.int32, bias_ref.shape, 0) >= SLOT
    gone = token == row0[0]
    for i in range(1, slots):
        gone = gone | (token == row0[i])
    later = token == row1[0]
    for i in range(1, slots):
        later = later | (token == row1[i])
    bias_ref[...] = jnp.where(gone | (second & later), FAR, 0.0)
    col = lax.broadcasted_iota(jnp.int32, fresh_bias_ref.shape, 1)
    second = (lax.broadcasted_iota(jnp.int32, fresh_bias_ref.shape, 0) >= SLOT).astype(jnp.int32)
    seen = jnp.zeros(fresh_bias_ref.shape, jnp.int32)
    for i in range(slots):
        again = row1[0] == row0[i]
        for j in range(1, slots):
            again = again | (row1[j] == row0[i])
        kept = (live0[i] & jnp.logical_not(again)).astype(jnp.int32)
        early = jnp.where(second == 1, kept, live0[i].astype(jnp.int32))
        seen = jnp.where(col == 2 * i, early, seen)
        seen = jnp.where(col == 2 * i + 1, second * live1[i].astype(jnp.int32), seen)
    fresh_bias_ref[...] = jnp.where(seen == 1, 0.0, FAR)

    out = lax.broadcasted_iota(jnp.int32, (2 * block, 2 * block), 0)
    src = lax.broadcasted_iota(jnp.int32, (2 * block, 2 * block), 1)
    order = (src == jnp.where(out < block, 2 * out, 2 * (out - block) + 1)).astype(jnp.bfloat16)
    pairs = held.reshape(2 * tokens, held.shape[2])
    for i in range(blocks):
        if i % WAITS == 0:
            for j in range(i, min(i + WAITS, blocks)):
                fetch(j).wait()
        rows = slice(i * block, (i + 1) * block)
        for c in range(0, width, 256):
            part = pairs[2 * i * block:2 * (i + 1) * block, c:c + 256]
            part = jnp.dot(order, part, preferred_element_type=jnp.float32).astype(jnp.bfloat16)
            key_ref[rows, c:c + 256] = part[:block]
            value_ref[rows, c:c + 256] = part[block:]
    for ref, new_ref in ((fresh_key_ref, new_key_ref), (fresh_value_ref, new_value_ref)):
        ref[...] = jnp.zeros_like(ref)
        ref[0:STEPS * slots, :] = new_ref.reshape(STEPS * slots, width)[...]


def prepare(table, cache, fresh_key, fresh_value):
    tokens, _, width = cache.shape
    slots = fresh_key.shape[0]
    device_count = table.shape[1] - slots - 1
    fresh_rows = -(-STEPS * slots // 16) * 16
    f32, bf16 = jnp.float32, jnp.bfloat16
    shapes = (
        jax.ShapeDtypeStruct((tokens, width), bf16),
        jax.ShapeDtypeStruct((tokens, width), bf16),
        jax.ShapeDtypeStruct((fresh_rows, width), bf16),
        jax.ShapeDtypeStruct((fresh_rows, width), bf16),
        jax.ShapeDtypeStruct((1, device_count * STEPS * slots), jnp.int32),
        jax.ShapeDtypeStruct((PAIR, tokens), f32),
        jax.ShapeDtypeStruct((PAIR, fresh_rows), f32),
    )
    blocks = tokens // min(128, tokens)
    return pl.pallas_call(
        prepare_kernel,
        out_shape=shapes,
        in_specs=[SMEM, HBM, VMEM, VMEM],
        out_specs=(VMEM,) * len(shapes),
        scratch_shapes=[
            pltpu.VMEM((tokens, 2, width + LANES), bf16),
            pltpu.SemaphoreType.DMA((blocks,)),
        ],
        compiler_params=pltpu.CompilerParams(vmem_limit_bytes=45 << 20),
        cost_estimate=pl.CostEstimate(
            flops=8 * 128 * tokens * width, bytes_accessed=8 * tokens * width, transcendentals=0
        ),
        name="prepare",
    )(table, cache, fresh_key, fresh_value)


def two_parts(x):
    high = x.astype(jnp.bfloat16).astype(jnp.float32)
    return high, x - high


def pack_stats(high, total):
    lane = lax.broadcasted_iota(jnp.int32, high.shape, 1)
    high = jnp.where(lane < PART, high, 0.0)
    total = jnp.where(lane < PART, total, 0.0)
    stats, rest = two_parts(high)
    second, third = two_parts(rest)
    for n, part in enumerate((second, third) + two_parts(total)):
        stats = stats + pltpu.roll(part, PART * (n + 1), 1)
    return stats


def unpack_stats(stats):
    def part(n):
        return pltpu.roll(stats, LANES - PART * n, 1)

    return stats + part(1) + part(2), part(3) + part(4)


def attend_kernel(target_ref, bias_ref, fresh_bias_ref, fresh_key_ref, fresh_value_ref, key_ref, value_ref, *rest):
    gathered_refs, (keep_ref, send_ref) = rest[:-2], rest[-2:]
    width = key_ref.shape[1]
    heads = width // HEAD
    half = keep_ref.shape[0]
    nt = (((1,), (1,)), ((), ()))

    def attend_rows(base, chunk, stores):
        row = lax.broadcasted_iota(jnp.int32, (chunk, target_ref.shape[1]), 0)
        pick = (row == target_ref[...] - base).astype(jnp.bfloat16)
        slots = [ref.reshape(ref.shape[0] * STEPS, width)[...].astype(jnp.float32) for ref in gathered_refs]
        slots = jnp.concatenate(slots).astype(jnp.bfloat16)
        queries = jnp.dot(pick, slots, preferred_element_type=jnp.float32).astype(jnp.bfloat16)
        bias = bias_ref[...]
        fresh_bias = fresh_bias_ref[...]
        lane = lax.broadcasted_iota(jnp.int32, (chunk, LANES), 1)
        highs = jnp.zeros((chunk, LANES), jnp.float32)
        totals = jnp.zeros((chunk, LANES), jnp.float32)
        ones = jnp.ones((key_ref.shape[0], LANES), jnp.bfloat16)

        def score(h):
            cols = slice(h * HEAD, (h + 1) * HEAD)
            q = queries[:, cols]
            s = lax.dot_general(q, key_ref[:, cols], nt, preferred_element_type=jnp.float32)
            sf = lax.dot_general(q, fresh_key_ref[:, cols], nt, preferred_element_type=jnp.float32)
            s = (s.reshape(chunk // PAIR, PAIR, -1) + bias[None]).reshape(chunk, -1)
            sf = (sf.reshape(chunk // PAIR, PAIR, -1) + fresh_bias[None]).reshape(chunk, -1)
            return s, sf

        following = score(0)
        for h in range(heads):
            cols = slice(h * HEAD, (h + 1) * HEAD)
            s, sf = following
            if h + 1 < heads:
                following = score(h + 1)
            high = jnp.maximum(jnp.max(s, axis=1, keepdims=True), jnp.max(sf, axis=1, keepdims=True))
            w = jnp.exp2((s - high) * SCALE).astype(jnp.bfloat16)
            wf = jnp.exp2((sf - high) * SCALE).astype(jnp.bfloat16)
            value = jnp.concatenate([value_ref[:, cols], ones], axis=1)
            fresh_value = jnp.concatenate([fresh_value_ref[:, cols], ones[:fresh_value_ref.shape[0]]], axis=1)
            o = jnp.dot(w, value, preferred_element_type=jnp.float32)
            o += jnp.dot(wf, fresh_value, preferred_element_type=jnp.float32)
            total = o[:, HEAD:]
            o = o[:, :HEAD] * (1.0 / total)
            for ref, to, start, count in stores:
                ref[pl.ds(to, count), cols] = o[start:start + count].astype(ref.dtype)
            highs = jnp.where(lane == h, high, highs)
            totals = jnp.where(lane == h, total, totals)
        stats = pack_stats(highs, totals)
        for ref, to, start, count in stores:
            ref[pl.ds(to, count), width:] = stats[start:start + count].astype(ref.dtype)

    if 2 * half <= 128:
        attend_rows(0, 2 * half, [(keep_ref, 0, 0, half), (send_ref, 0, half, half)])
    else:
        for ref, base in ((keep_ref, 0), (send_ref, half)):
            @pl.loop(0, half // 128)
            def _(i, ref=ref, base=base):
                to = pl.multiple_of(i * 128, 128)
                attend_rows(base + to, 128, [(ref, to, 0, 128)])


def attend(slots, target, bias, fresh_bias, fresh_key, fresh_value, key, value, gathered):
    tokens, width = key.shape
    rows = target.shape[1] * SLOT // slots
    shape = (rows // 2, width + LANES)
    return pl.pallas_call(
        attend_kernel,
        out_shape=(jax.ShapeDtypeStruct(shape, jnp.float32), jax.ShapeDtypeStruct(shape, jnp.bfloat16)),
        in_specs=[VMEM] * (7 + len(gathered)),
        out_specs=(VMEM, VMEM),
        compiler_params=pltpu.CompilerParams(vmem_limit_bytes=24 << 20),
        cost_estimate=pl.CostEstimate(
            flops=4 * rows * tokens * width, bytes_accessed=4 * tokens * width,
            transcendentals=rows * tokens * width // HEAD,
        ),
        name="attend",
    )(target, bias, fresh_bias, fresh_key, fresh_value, key, value, *gathered)


def merged(parts):
    width = parts[0].shape[1] - LANES
    stats = [unpack_stats(part[:, width:].astype(jnp.float32)) for part in parts]
    top = stats[0][0]
    for high, _ in stats[1:]:
        top = jnp.maximum(top, high)
    weights = [total * jnp.exp2((high - top) * SCALE) for high, total in stats]
    total = weights[0]
    for w in weights[1:]:
        total = total + w
    used = lax.broadcasted_iota(jnp.int32, total.shape, 1) < width // HEAD
    share = 1.0 / jnp.where(used, total, 1.0)
    weights = [w * share for w in weights]
    for h in range(width // HEAD):
        cols = slice(h * HEAD, (h + 1) * HEAD)
        o = parts[0][:, cols].astype(jnp.float32) * weights[0][:, h:h + 1]
        for part, w in zip(parts[1:], weights[1:]):
            o = o + part[:, cols].astype(jnp.float32) * w[:, h:h + 1]
        yield cols, o
    yield slice(width, width + LANES), pack_stats(jnp.where(used, top, 0.0), jnp.where(used, total, 0.0))


def merge_cores_kernel(keep_ref, other_ref, out_ref):
    for cols, o in merged([keep_ref, other_ref]):
        out_ref[:, :, cols] = o.reshape(out_ref.shape[0], out_ref.shape[1], -1).astype(jnp.bfloat16)


def merge_four_kernel(parts_ref, *out_refs):
    store_merged([parts_ref.at[n] for n in range(parts_ref.shape[0])], out_refs)


def merge_two_kernel(keep_ref, other_ref, *out_refs):
    store_merged([keep_ref, other_ref], out_refs)


def store_merged(parts, out_refs):
    rows, width = parts[0].shape
    for cols, o in merged(parts):
        if len(out_refs) == 2:
            for n, ref in enumerate(out_refs):
                ref[:, cols] = o[n * rows // 2:(n + 1) * rows // 2].astype(ref.dtype)
        elif cols.start < width - LANES:
            for s in range(STEPS):
                out_refs[0][s, :, cols] = o[s * SLOT:(s + 1) * SLOT].astype(jnp.bfloat16)


def merge(kernel, parts, shapes, name):
    return pl.pallas_call(
        kernel,
        out_shape=shapes,
        in_specs=[VMEM] * len(parts),
        out_specs=jax.tree.map(lambda _: VMEM, shapes),
        compiler_params=pltpu.CompilerParams(vmem_limit_bytes=16 << 20),
        name=name,
    )(*parts)


def body(cache_kv, fresh_qkv, list_rows, counts):
    device_count = lax.axis_size("blk")
    me = lax.axis_index("blk")
    slot_count = list_rows.shape[1]
    bits = device_count.bit_length() - 1
    width = cache_kv.shape[2]

    def swap(x, mask):
        return lax.ppermute(x, "blk", [(i, i ^ mask) for i in range(device_count)])

    fresh = fresh_qkv.transpose(1, 2, 0, 3)
    mine, fresh_key, fresh_value = (fresh[:, i] for i in range(3))
    table = jnp.concatenate([counts, list_rows, jnp.full((STEPS, 1), me, jnp.int32)], axis=1)
    ready = prepare(table, cache_kv, fresh_key, fresh_value)
    column = mine
    for n in range(bits - 1, 2, -1):
        column = jnp.concatenate([column, swap(column, 1 << n)])
    others = [swap(column, mask) for mask in (4, 2, 6)]
    beside = swap(column, 1)
    others, beside, ready = lax.optimization_barrier((others, beside, ready))
    others = jnp.concatenate(others)
    gathered = [column, others, beside, swap(others, 1)]
    key, value, fresh_key, fresh_value, target, bias, fresh_bias = ready
    keep, send = attend(slot_count, target, bias, fresh_bias, fresh_key, fresh_value, key, value, gathered)
    rows = device_count // 8 * PAIR
    lanes = width + LANES
    bf16 = jnp.bfloat16
    parts = merge(merge_cores_kernel, [keep, swap(send, 1)], jax.ShapeDtypeStruct((4, rows, lanes), bf16), "merge_cores")
    fours = [[(first * 4 + chip) * 2 + core for chip in range(4)] for first in range(device_count // 8) for core in range(2)]
    parts = [lax.all_to_all(parts, "blk", split_axis=0, concat_axis=0, axis_index_groups=fours, tiled=True)]
    kernel, name = merge_four_kernel, "merge_four"
    for n in range(3, bits):
        rows //= 2
        shapes = (jax.ShapeDtypeStruct((rows, lanes), jnp.float32), jax.ShapeDtypeStruct((rows, lanes), bf16))
        keep, send = merge(kernel, parts, shapes, name)
        parts = [keep, swap(send, 1 << n)]
        kernel, name = merge_two_kernel, "merge_two"
    return merge(kernel, parts, jax.ShapeDtypeStruct((STEPS, SLOT, width), bf16), name)


def solution(mesh):
    in_specs = (
        P(("groups", "blk"), None, None),
        P(None, ("groups", "blk"), None, None),
        P(None, ("groups", "blk")),
        P(None, "groups"),
    )
    out_specs = P(None, ("groups", "blk"), None)
    return jax.shard_map(body, mesh=mesh, in_specs=in_specs, out_specs=out_specs, check_vma=False)
```

```python
import jax
import jax.numpy as jnp
from jax import lax
from jax.experimental import pallas as pl
from jax.experimental.pallas import tpu as pltpu
from jax.sharding import PartitionSpec as P

HEAD = 128
SLOT = 4
STEPS = 2
PAIR = STEPS * SLOT
LOG2E = 1.4426950408889634
SCALE = HEAD ** -0.5 * LOG2E
FAR = -1e30
LANES = 128
PART = 16
SLOT_BITS = 2
WAITS = 4
SORT_VMEM = 48
VMEM = pl.BlockSpec(memory_space=pltpu.VMEM)
SMEM = pl.BlockSpec(memory_space=pltpu.SMEM)
HBM = pl.BlockSpec(memory_space=pltpu.HBM)


def turned(mask, bits):
    place = 0
    for n in range(bits):
        place = place + (((mask >> n) & 1) << (bits - 1 - n))
    return place


def plan_kernel_part(table_ref, slots, target_ref, bias_ref, fresh_bias_ref):
    device_count = table_ref.shape[1] - slots - 1
    bits = device_count.bit_length() - 1
    me = table_ref[0, device_count + slots]
    col = lax.broadcasted_iota(jnp.int32, target_ref.shape, 1)

    def one_device(dev, carry):
        start0, start1, target = carry
        count0, count1 = table_ref[0, dev], table_ref[1, dev]
        local = col - turned(dev ^ me, bits) * (STEPS * slots)
        slot, step = local >> 1, local & 1
        rank = slot + jnp.where(step == 0, start0, start1)
        home = rank >> SLOT_BITS
        home = ((home ^ me) & 1) * (device_count // 2) + (home >> 1)
        row = home * PAIR + step * SLOT + (rank & (SLOT - 1))
        good = (local >= 0) & (slot < jnp.where(step == 0, count0, count1))
        return start0 + count0, start1 + count1, jnp.where(good, row, target)

    carry = (jnp.int32(0), jnp.int32(0), jnp.full(target_ref.shape, -1, jnp.int32))
    if device_count <= 16:
        for dev in range(device_count):
            carry = one_device(dev, carry)
    else:
        carry = lax.fori_loop(0, device_count, one_device, carry)
    target_ref[...] = carry[2]

    live0 = [i < table_ref[0, me] for i in range(slots)]
    live1 = [i < table_ref[1, me] for i in range(slots)]
    row0 = [jnp.where(live0[i], table_ref[0, device_count + i], -1) for i in range(slots)]
    row1 = [jnp.where(live1[i], table_ref[1, device_count + i], -2) for i in range(slots)]
    token = lax.broadcasted_iota(jnp.int32, bias_ref.shape, 1)
    second = lax.broadcasted_iota(jnp.int32, bias_ref.shape, 0) >= SLOT
    gone = token == row0[0]
    for i in range(1, slots):
        gone = gone | (token == row0[i])
    later = token == row1[0]
    for i in range(1, slots):
        later = later | (token == row1[i])
    bias_ref[...] = jnp.where(gone | (second & later), FAR, 0.0)
    col = lax.broadcasted_iota(jnp.int32, fresh_bias_ref.shape, 1)
    second = (lax.broadcasted_iota(jnp.int32, fresh_bias_ref.shape, 0) >= SLOT).astype(jnp.int32)
    seen = jnp.zeros(fresh_bias_ref.shape, jnp.int32)
    for i in range(slots):
        again = row1[0] == row0[i]
        for j in range(1, slots):
            again = again | (row1[j] == row0[i])
        kept = (live0[i] & jnp.logical_not(again)).astype(jnp.int32)
        early = jnp.where(second == 1, kept, live0[i].astype(jnp.int32))
        seen = jnp.where(col == 2 * i, early, seen)
        seen = jnp.where(col == 2 * i + 1, second * live1[i].astype(jnp.int32), seen)
    fresh_bias_ref[...] = jnp.where(seen == 1, 0.0, FAR)


def sort_kernel(first, planned, *refs):
    refs = list(refs)
    table_ref = refs.pop(0) if planned else None
    cache_ref = refs.pop(0)
    new_refs = [refs.pop(0) for _ in range(2)] if planned else []
    key_ref, value_ref, *small_refs, held, sems = refs
    tokens, width = key_ref.shape
    block = min(128, tokens)
    blocks = tokens // block

    def fetch(i):
        part = pl.ds(i * block, block)
        return pltpu.make_async_copy(
            cache_ref.at[part, :, pl.ds(first, width)], held.at[part, :, pl.ds(0, width)], sems.at[i]
        )

    for i in range(blocks):
        fetch(i).start()
    if planned:
        slots = new_refs[0].shape[0]
        for ref, new_ref in zip(small_refs[:2], new_refs):
            ref[...] = jnp.zeros_like(ref)
            ref[0:STEPS * slots, :] = new_ref.reshape(STEPS * slots, ref.shape[1])[...]
        plan_kernel_part(table_ref, slots, *small_refs[2:])
    out = lax.broadcasted_iota(jnp.int32, (2 * block, 2 * block), 0)
    src = lax.broadcasted_iota(jnp.int32, (2 * block, 2 * block), 1)
    order = (src == jnp.where(out < block, 2 * out, 2 * (out - block) + 1)).astype(jnp.bfloat16)
    pairs = held.reshape(2 * tokens, held.shape[2])
    for i in range(blocks):
        if i % WAITS == 0:
            for j in range(i, min(i + WAITS, blocks)):
                fetch(j).wait()
        rows = slice(i * block, (i + 1) * block)
        for c in range(0, width, 256):
            part = pairs[2 * i * block:2 * (i + 1) * block, c:c + 256]
            part = jnp.dot(order, part, preferred_element_type=jnp.float32).astype(jnp.bfloat16)
            key_ref[rows, c:c + 256] = part[:block]
            value_ref[rows, c:c + 256] = part[block:]


def sort_cache(cache, first, width, plan, name):
    tokens, _, full = cache.shape
    f32, bf16 = jnp.float32, jnp.bfloat16
    shapes = [jax.ShapeDtypeStruct((tokens, width), bf16)] * 2
    inputs, specs = [cache], [HBM]
    if plan:
        table, fresh_key, fresh_value = plan
        slots = fresh_key.shape[0]
        device_count = table.shape[1] - slots - 1
        fresh_rows = -(-STEPS * slots // 16) * 16
        shapes += [jax.ShapeDtypeStruct((fresh_rows, full), bf16)] * 2
        shapes += [
            jax.ShapeDtypeStruct((1, device_count * STEPS * slots), jnp.int32),
            jax.ShapeDtypeStruct((PAIR, tokens), f32),
            jax.ShapeDtypeStruct((PAIR, fresh_rows), f32),
        ]
        inputs, specs = [table, cache, fresh_key, fresh_value], [SMEM, HBM, VMEM, VMEM]

    def kernel(*refs):
        sort_kernel(first, bool(plan), *refs)

    blocks = tokens // min(128, tokens)
    return pl.pallas_call(
        kernel,
        out_shape=tuple(shapes),
        in_specs=specs,
        out_specs=(VMEM,) * len(shapes),
        scratch_shapes=[
            pltpu.VMEM((tokens, 2, width + LANES), bf16),
            pltpu.SemaphoreType.DMA((blocks,)),
        ],
        compiler_params=pltpu.CompilerParams(vmem_limit_bytes=SORT_VMEM << 20),
        cost_estimate=pl.CostEstimate(
            flops=8 * 128 * tokens * width, bytes_accessed=8 * tokens * width, transcendentals=0
        ),
        name=name,
    )(*inputs)


def two_parts(x):
    high = x.astype(jnp.bfloat16).astype(jnp.float32)
    return high, x - high


def pack_stats(high, total):
    lane = lax.broadcasted_iota(jnp.int32, high.shape, 1)
    high = jnp.where(lane < PART, high, 0.0)
    total = jnp.where(lane < PART, total, 0.0)
    stats, rest = two_parts(high)
    second, third = two_parts(rest)
    for n, part in enumerate((second, third) + two_parts(total)):
        stats = stats + pltpu.roll(part, PART * (n + 1), 1)
    return stats


def unpack_stats(stats):
    def part(n):
        return pltpu.roll(stats, LANES - PART * n, 1)

    return stats + part(1) + part(2), part(3) + part(4)


def attend_kernel(target_ref, bias_ref, fresh_bias_ref, fresh_key_ref, fresh_value_ref, *rest):
    key_refs, value_refs, gathered_refs, (keep_ref, send_ref) = rest[0:4:2], rest[1:4:2], rest[4:-2], rest[-2:]
    width = fresh_key_ref.shape[1]
    part_heads = key_refs[0].shape[1] // HEAD
    tokens = key_refs[0].shape[0]
    heads = width // HEAD
    half = keep_ref.shape[0]
    nt = (((1,), (1,)), ((), ()))

    def attend_rows(base, chunk, stores):
        row = lax.broadcasted_iota(jnp.int32, (chunk, target_ref.shape[1]), 0)
        pick = (row == target_ref[...] - base).astype(jnp.bfloat16)
        slots = [ref.reshape(ref.shape[0] * STEPS, width)[...].astype(jnp.float32) for ref in gathered_refs]
        slots = jnp.concatenate(slots).astype(jnp.bfloat16)
        queries = jnp.dot(pick, slots, preferred_element_type=jnp.float32).astype(jnp.bfloat16)
        bias = bias_ref[...]
        fresh_bias = fresh_bias_ref[...]
        lane = lax.broadcasted_iota(jnp.int32, (chunk, LANES), 1)
        highs = jnp.zeros((chunk, LANES), jnp.float32)
        totals = jnp.zeros((chunk, LANES), jnp.float32)
        ones = jnp.ones((tokens, LANES), jnp.bfloat16)

        def block_of(refs, h):
            at = h % part_heads * HEAD
            return refs[h // part_heads][:, at:at + HEAD]

        def score(h):
            cols = slice(h * HEAD, (h + 1) * HEAD)
            q = queries[:, cols]
            s = lax.dot_general(q, block_of(key_refs, h), nt, preferred_element_type=jnp.float32)
            sf = lax.dot_general(q, fresh_key_ref[:, cols], nt, preferred_element_type=jnp.float32)
            s = (s.reshape(chunk // PAIR, PAIR, -1) + bias[None]).reshape(chunk, -1)
            sf = (sf.reshape(chunk // PAIR, PAIR, -1) + fresh_bias[None]).reshape(chunk, -1)
            return s, sf

        following = score(0)
        for h in range(heads):
            cols = slice(h * HEAD, (h + 1) * HEAD)
            s, sf = following
            if h + 1 < heads:
                following = score(h + 1)
            high = jnp.maximum(jnp.max(s, axis=1, keepdims=True), jnp.max(sf, axis=1, keepdims=True))
            w = jnp.exp2((s - high) * SCALE).astype(jnp.bfloat16)
            wf = jnp.exp2((sf - high) * SCALE).astype(jnp.bfloat16)
            value = jnp.concatenate([block_of(value_refs, h), ones], axis=1)
            fresh_value = jnp.concatenate([fresh_value_ref[:, cols], ones[:fresh_value_ref.shape[0]]], axis=1)
            o = jnp.dot(w, value, preferred_element_type=jnp.float32)
            o += jnp.dot(wf, fresh_value, preferred_element_type=jnp.float32)
            total = o[:, HEAD:]
            o = o[:, :HEAD] * (1.0 / total)
            for ref, to, start, count in stores:
                ref[pl.ds(to, count), cols] = o[start:start + count].astype(ref.dtype)
            highs = jnp.where(lane == h, high, highs)
            totals = jnp.where(lane == h, total, totals)
        stats = pack_stats(highs, totals)
        for ref, to, start, count in stores:
            ref[pl.ds(to, count), width:] = stats[start:start + count].astype(ref.dtype)

    if 2 * half <= 128:
        attend_rows(0, 2 * half, [(keep_ref, 0, 0, half), (send_ref, 0, half, half)])
    else:
        for ref, base in ((keep_ref, 0), (send_ref, half)):
            @pl.loop(0, half // 128)
            def _(i, ref=ref, base=base):
                to = pl.multiple_of(i * 128, 128)
                attend_rows(base + to, 128, [(ref, to, 0, 128)])


def attend(slots, target, bias, fresh_bias, fresh_key, fresh_value, sorted_parts, gathered):
    tokens, width = sorted_parts[0].shape[0], fresh_key.shape[1]
    rows = target.shape[1] * SLOT // slots
    shape = (rows // 2, width + LANES)
    return pl.pallas_call(
        attend_kernel,
        out_shape=(jax.ShapeDtypeStruct(shape, jnp.float32), jax.ShapeDtypeStruct(shape, jnp.bfloat16)),
        in_specs=[VMEM] * (5 + len(sorted_parts) + len(gathered)),
        out_specs=(VMEM, VMEM),
        compiler_params=pltpu.CompilerParams(vmem_limit_bytes=24 << 20),
        cost_estimate=pl.CostEstimate(
            flops=4 * rows * tokens * width, bytes_accessed=4 * tokens * width,
            transcendentals=rows * tokens * width // HEAD,
        ),
        name="attend",
    )(target, bias, fresh_bias, fresh_key, fresh_value, *sorted_parts, *gathered)


def merged(parts):
    width = parts[0].shape[1] - LANES
    stats = [unpack_stats(part[:, width:].astype(jnp.float32)) for part in parts]
    top = stats[0][0]
    for high, _ in stats[1:]:
        top = jnp.maximum(top, high)
    weights = [total * jnp.exp2((high - top) * SCALE) for high, total in stats]
    total = weights[0]
    for w in weights[1:]:
        total = total + w
    used = lax.broadcasted_iota(jnp.int32, total.shape, 1) < width // HEAD
    share = 1.0 / jnp.where(used, total, 1.0)
    weights = [w * share for w in weights]
    for h in range(width // HEAD):
        cols = slice(h * HEAD, (h + 1) * HEAD)
        o = parts[0][:, cols].astype(jnp.float32) * weights[0][:, h:h + 1]
        for part, w in zip(parts[1:], weights[1:]):
            o = o + part[:, cols].astype(jnp.float32) * w[:, h:h + 1]
        yield cols, o
    yield slice(width, width + LANES), pack_stats(jnp.where(used, top, 0.0), jnp.where(used, total, 0.0))


def merge_cores_kernel(keep_ref, other_ref, out_ref):
    for cols, o in merged([keep_ref, other_ref]):
        out_ref[:, :, cols] = o.reshape(o.shape[0] // PAIR, PAIR, -1).astype(jnp.bfloat16)


def merge_chips_kernel(parts_ref, out_ref):
    width = out_ref.shape[2]
    for cols, o in merged([parts_ref.at[n] for n in range(parts_ref.shape[0])]):
        if cols.start < width:
            for s in range(STEPS):
                out_ref[s, :, cols] = o[s * SLOT:(s + 1) * SLOT].astype(jnp.bfloat16)


def merge(kernel, parts, shape, name):
    return pl.pallas_call(
        kernel,
        out_shape=jax.ShapeDtypeStruct(shape, jnp.bfloat16),
        in_specs=[VMEM] * len(parts),
        out_specs=VMEM,
        compiler_params=pltpu.CompilerParams(vmem_limit_bytes=16 << 20),
        name=name,
    )(*parts)


def body(cache_kv, fresh_qkv, list_rows, counts):
    device_count = lax.axis_size("blk")
    me = lax.axis_index("blk")
    slot_count = list_rows.shape[1]
    bits = device_count.bit_length() - 1
    width = cache_kv.shape[2]

    def swap(x, mask):
        return lax.ppermute(x, "blk", [(i, i ^ mask) for i in range(device_count)])

    fresh = fresh_qkv.transpose(1, 2, 0, 3)
    mine, fresh_key, fresh_value = (fresh[:, i] for i in range(3))
    half = width // 2
    early = sort_cache(cache_kv, 0, half, None, "sort_first")
    column = mine
    for n in range(bits - 1, 2, -1):
        other = swap(column, 1 << n)
        if n == bits - 1:
            other, early, counts, list_rows = lax.optimization_barrier((other, early, counts, list_rows))
        column = jnp.concatenate([column, other])
    table = jnp.concatenate([counts, list_rows, jnp.full((STEPS, 1), me, jnp.int32)], axis=1)
    late = sort_cache(cache_kv, half, half, (table, fresh_key, fresh_value), "sort_second")
    others = [swap(column, mask) for mask in (4, 2, 6)]
    beside = swap(column, 1)
    others, beside, late = lax.optimization_barrier((others, beside, late))
    others = jnp.concatenate(others)
    gathered = [column, others, beside, swap(others, 1)]
    key, value, fresh_key, fresh_value, target, bias, fresh_bias = late
    keep, send = attend(slot_count, target, bias, fresh_bias, fresh_key, fresh_value, [*early, key, value], gathered)
    chips = device_count // 2
    parts = merge(merge_cores_kernel, [keep, swap(send, 1)], (chips, PAIR, width + LANES), "merge_cores")
    groups = [[chip * 2 + core for chip in range(chips)] for core in range(2)]
    parts = lax.all_to_all(parts, "blk", split_axis=0, concat_axis=0, axis_index_groups=groups, tiled=True)
    return merge(merge_chips_kernel, [parts], (STEPS, SLOT, width), "merge_chips")


def solution(mesh):
    in_specs = (
        P(("groups", "blk"), None, None),
        P(None, ("groups", "blk"), None, None),
        P(None, ("groups", "blk")),
        P(None, "groups"),
    )
    out_specs = P(None, ("groups", "blk"), None)
    return jax.shard_map(body, mesh=mesh, in_specs=in_specs, out_specs=out_specs, check_vma=False)
```

```python
import jax
import jax.numpy as jnp
from jax import lax
from jax.experimental import pallas as pl
from jax.experimental.pallas import tpu as pltpu
from jax.sharding import PartitionSpec as P

HEAD = 128
SLOT = 4
STEPS = 2
PAIR = STEPS * SLOT
LOG2E = 1.4426950408889634
SCALE = HEAD ** -0.5 * LOG2E
FAR = -1e30
LANES = 128
PART = 16
SLOT_BITS = 2
WAITS = 4
SORT_VMEM = 48
VMEM = pl.BlockSpec(memory_space=pltpu.VMEM)
SMEM = pl.BlockSpec(memory_space=pltpu.SMEM)
HBM = pl.BlockSpec(memory_space=pltpu.HBM)


def turned(mask, bits):
    place = 0
    for n in range(bits):
        place = place + (((mask >> n) & 1) << (bits - 1 - n))
    return place


def plan_kernel_part(table_ref, slots, target_ref, bias_ref, fresh_bias_ref):
    device_count = table_ref.shape[1] - slots - 1
    bits = device_count.bit_length() - 1
    me = table_ref[0, device_count + slots]
    col = lax.broadcasted_iota(jnp.int32, target_ref.shape, 1)

    def one_device(dev, carry):
        start0, start1, target = carry
        count0, count1 = table_ref[0, dev], table_ref[1, dev]
        local = col - turned(dev ^ me, bits) * (STEPS * slots)
        slot, step = local >> 1, local & 1
        rank = slot + jnp.where(step == 0, start0, start1)
        home = rank >> SLOT_BITS
        home = ((home ^ me) & 1) * (device_count // 2) + (home >> 1)
        row = home * PAIR + step * SLOT + (rank & (SLOT - 1))
        good = (local >= 0) & (slot < jnp.where(step == 0, count0, count1))
        return start0 + count0, start1 + count1, jnp.where(good, row, target)

    carry = (jnp.int32(0), jnp.int32(0), jnp.full(target_ref.shape, -1, jnp.int32))
    if device_count <= 16:
        for dev in range(device_count):
            carry = one_device(dev, carry)
    else:
        carry = lax.fori_loop(0, device_count, one_device, carry)
    target_ref[...] = carry[2]

    live0 = [i < table_ref[0, me] for i in range(slots)]
    live1 = [i < table_ref[1, me] for i in range(slots)]
    row0 = [jnp.where(live0[i], table_ref[0, device_count + i], -1) for i in range(slots)]
    row1 = [jnp.where(live1[i], table_ref[1, device_count + i], -2) for i in range(slots)]
    token = lax.broadcasted_iota(jnp.int32, bias_ref.shape, 1)
    second = lax.broadcasted_iota(jnp.int32, bias_ref.shape, 0) >= SLOT
    gone = token == row0[0]
    for i in range(1, slots):
        gone = gone | (token == row0[i])
    later = token == row1[0]
    for i in range(1, slots):
        later = later | (token == row1[i])
    bias_ref[...] = jnp.where(gone | (second & later), FAR, 0.0)
    col = lax.broadcasted_iota(jnp.int32, fresh_bias_ref.shape, 1)
    second = (lax.broadcasted_iota(jnp.int32, fresh_bias_ref.shape, 0) >= SLOT).astype(jnp.int32)
    seen = jnp.zeros(fresh_bias_ref.shape, jnp.int32)
    for i in range(slots):
        again = row1[0] == row0[i]
        for j in range(1, slots):
            again = again | (row1[j] == row0[i])
        kept = (live0[i] & jnp.logical_not(again)).astype(jnp.int32)
        early = jnp.where(second == 1, kept, live0[i].astype(jnp.int32))
        seen = jnp.where(col == 2 * i, early, seen)
        seen = jnp.where(col == 2 * i + 1, second * live1[i].astype(jnp.int32), seen)
    fresh_bias_ref[...] = jnp.where(seen == 1, 0.0, FAR)


def sort_kernel(first, planned, *refs):
    refs = list(refs)
    table_ref = refs.pop(0) if planned else None
    cache_ref = refs.pop(0)
    new_refs = [refs.pop(0) for _ in range(2)] if planned else []
    key_ref, value_ref, *small_refs, held, sems = refs
    tokens, width = key_ref.shape
    block = min(128, tokens)
    blocks = tokens // block

    def fetch(i):
        part = pl.ds(i * block, block)
        return pltpu.make_async_copy(
            cache_ref.at[part, :, pl.ds(first, width)], held.at[part, :, pl.ds(0, width)], sems.at[i]
        )

    for i in range(blocks):
        fetch(i).start()
    if planned:
        slots = new_refs[0].shape[0]
        for ref, new_ref in zip(small_refs[:2], new_refs):
            ref[...] = jnp.zeros_like(ref)
            ref[0:STEPS * slots, :] = new_ref.reshape(STEPS * slots, ref.shape[1])[...]
        plan_kernel_part(table_ref, slots, *small_refs[2:])
    out = lax.broadcasted_iota(jnp.int32, (2 * block, 2 * block), 0)
    src = lax.broadcasted_iota(jnp.int32, (2 * block, 2 * block), 1)
    order = (src == jnp.where(out < block, 2 * out, 2 * (out - block) + 1)).astype(jnp.bfloat16)
    pairs = held.reshape(2 * tokens, held.shape[2])
    for i in range(blocks):
        if i % WAITS == 0:
            for j in range(i, min(i + WAITS, blocks)):
                fetch(j).wait()
        rows = slice(i * block, (i + 1) * block)
        for c in range(0, width, 256):
            part = pairs[2 * i * block:2 * (i + 1) * block, c:c + 256]
            part = jnp.dot(order, part, preferred_element_type=jnp.float32).astype(jnp.bfloat16)
            key_ref[rows, c:c + 256] = part[:block]
            value_ref[rows, c:c + 256] = part[block:]


def sort_cache(cache, first, width, plan, name):
    tokens, _, full = cache.shape
    f32, bf16 = jnp.float32, jnp.bfloat16
    shapes = [jax.ShapeDtypeStruct((tokens, width), bf16)] * 2
    inputs, specs = [cache], [HBM]
    if plan:
        table, fresh_key, fresh_value = plan
        slots = fresh_key.shape[0]
        device_count = table.shape[1] - slots - 1
        fresh_rows = -(-STEPS * slots // 16) * 16
        shapes += [jax.ShapeDtypeStruct((fresh_rows, full), bf16)] * 2
        shapes += [
            jax.ShapeDtypeStruct((1, device_count * STEPS * slots), jnp.int32),
            jax.ShapeDtypeStruct((PAIR, tokens), f32),
            jax.ShapeDtypeStruct((PAIR, fresh_rows), f32),
        ]
        inputs, specs = [table, cache, fresh_key, fresh_value], [SMEM, HBM, VMEM, VMEM]

    def kernel(*refs):
        sort_kernel(first, bool(plan), *refs)

    blocks = tokens // min(128, tokens)
    return pl.pallas_call(
        kernel,
        out_shape=tuple(shapes),
        in_specs=specs,
        out_specs=(VMEM,) * len(shapes),
        scratch_shapes=[
            pltpu.VMEM((tokens, 2, width + LANES), bf16),
            pltpu.SemaphoreType.DMA((blocks,)),
        ],
        compiler_params=pltpu.CompilerParams(vmem_limit_bytes=SORT_VMEM << 20),
        cost_estimate=pl.CostEstimate(
            flops=8 * 128 * tokens * width, bytes_accessed=8 * tokens * width, transcendentals=0
        ),
        name=name,
    )(*inputs)


def two_parts(x):
    high = x.astype(jnp.bfloat16).astype(jnp.float32)
    return high, x - high


def pack_stats(high, total):
    lane = lax.broadcasted_iota(jnp.int32, high.shape, 1)
    high = jnp.where(lane < PART, high, 0.0)
    total = jnp.where(lane < PART, total, 0.0)
    stats, rest = two_parts(high)
    second, third = two_parts(rest)
    for n, part in enumerate((second, third) + two_parts(total)):
        stats = stats + pltpu.roll(part, PART * (n + 1), 1)
    return stats


def unpack_stats(stats):
    def part(n):
        return pltpu.roll(stats, LANES - PART * n, 1)

    return stats + part(1) + part(2), part(3) + part(4)


def attend_kernel(target_ref, bias_ref, fresh_bias_ref, fresh_key_ref, fresh_value_ref, *rest):
    key_refs, value_refs, gathered_refs, (keep_ref, send_ref) = rest[0:4:2], rest[1:4:2], rest[4:-2], rest[-2:]
    width = fresh_key_ref.shape[1]
    part_heads = key_refs[0].shape[1] // HEAD
    tokens = key_refs[0].shape[0]
    heads = width // HEAD
    half = keep_ref.shape[0]
    nt = (((1,), (1,)), ((), ()))

    def attend_rows(base, chunk, stores):
        row = lax.broadcasted_iota(jnp.int32, (chunk, target_ref.shape[1]), 0)
        pick = (row == target_ref[...] - base).astype(jnp.bfloat16)
        slots = [ref.reshape(ref.shape[0] * STEPS, width)[...].astype(jnp.float32) for ref in gathered_refs]
        slots = jnp.concatenate(slots).astype(jnp.bfloat16)
        queries = jnp.dot(pick, slots, preferred_element_type=jnp.float32).astype(jnp.bfloat16)
        bias = bias_ref[...]
        fresh_bias = fresh_bias_ref[...]
        lane = lax.broadcasted_iota(jnp.int32, (chunk, LANES), 1)
        highs = jnp.zeros((chunk, LANES), jnp.float32)
        totals = jnp.zeros((chunk, LANES), jnp.float32)
        ones = jnp.ones((tokens, LANES), jnp.bfloat16)

        def block_of(refs, h):
            at = h % part_heads * HEAD
            return refs[h // part_heads][:, at:at + HEAD]

        def score(h):
            cols = slice(h * HEAD, (h + 1) * HEAD)
            q = queries[:, cols]
            s = lax.dot_general(q, block_of(key_refs, h), nt, preferred_element_type=jnp.float32)
            sf = lax.dot_general(q, fresh_key_ref[:, cols], nt, preferred_element_type=jnp.float32)
            s = (s.reshape(chunk // PAIR, PAIR, -1) + bias[None]).reshape(chunk, -1)
            sf = (sf.reshape(chunk // PAIR, PAIR, -1) + fresh_bias[None]).reshape(chunk, -1)
            return s, sf

        following = score(0)
        for h in range(heads):
            cols = slice(h * HEAD, (h + 1) * HEAD)
            s, sf = following
            if h + 1 < heads:
                following = score(h + 1)
            high = jnp.maximum(jnp.max(s, axis=1, keepdims=True), jnp.max(sf, axis=1, keepdims=True))
            w = jnp.exp2((s - high) * SCALE).astype(jnp.bfloat16)
            wf = jnp.exp2((sf - high) * SCALE).astype(jnp.bfloat16)
            value = jnp.concatenate([block_of(value_refs, h), ones], axis=1)
            fresh_value = jnp.concatenate([fresh_value_ref[:, cols], ones[:fresh_value_ref.shape[0]]], axis=1)
            o = jnp.dot(w, value, preferred_element_type=jnp.float32)
            o += jnp.dot(wf, fresh_value, preferred_element_type=jnp.float32)
            total = o[:, HEAD:]
            o = o[:, :HEAD] * (1.0 / total)
            for ref, to, start, count in stores:
                ref[pl.ds(to, count), cols] = o[start:start + count].astype(ref.dtype)
            highs = jnp.where(lane == h, high, highs)
            totals = jnp.where(lane == h, total, totals)
        stats = pack_stats(highs, totals)
        for ref, to, start, count in stores:
            ref[pl.ds(to, count), width:] = stats[start:start + count].astype(ref.dtype)

    if 2 * half <= 128:
        attend_rows(0, 2 * half, [(keep_ref, 0, 0, half), (send_ref, 0, half, half)])
    else:
        for ref, base in ((keep_ref, 0), (send_ref, half)):
            @pl.loop(0, half // 128)
            def _(i, ref=ref, base=base):
                to = pl.multiple_of(i * 128, 128)
                attend_rows(base + to, 128, [(ref, to, 0, 128)])


def attend(slots, target, bias, fresh_bias, fresh_key, fresh_value, sorted_parts, gathered):
    tokens, width = sorted_parts[0].shape[0], fresh_key.shape[1]
    rows = target.shape[1] * SLOT // slots
    shape = (rows // 2, width + LANES)
    return pl.pallas_call(
        attend_kernel,
        out_shape=(jax.ShapeDtypeStruct(shape, jnp.float32), jax.ShapeDtypeStruct(shape, jnp.bfloat16)),
        in_specs=[VMEM] * (5 + len(sorted_parts) + len(gathered)),
        out_specs=(VMEM, VMEM),
        compiler_params=pltpu.CompilerParams(vmem_limit_bytes=24 << 20),
        cost_estimate=pl.CostEstimate(
            flops=4 * rows * tokens * width, bytes_accessed=4 * tokens * width,
            transcendentals=rows * tokens * width // HEAD,
        ),
        name="attend",
    )(target, bias, fresh_bias, fresh_key, fresh_value, *sorted_parts, *gathered)


def merged(parts):
    width = parts[0].shape[1] - LANES
    stats = [unpack_stats(part[:, width:].astype(jnp.float32)) for part in parts]
    top = stats[0][0]
    for high, _ in stats[1:]:
        top = jnp.maximum(top, high)
    weights = [total * jnp.exp2((high - top) * SCALE) for high, total in stats]
    total = weights[0]
    for w in weights[1:]:
        total = total + w
    used = lax.broadcasted_iota(jnp.int32, total.shape, 1) < width // HEAD
    share = 1.0 / jnp.where(used, total, 1.0)
    weights = [w * share for w in weights]
    for h in range(width // HEAD):
        cols = slice(h * HEAD, (h + 1) * HEAD)
        o = parts[0][:, cols].astype(jnp.float32) * weights[0][:, h:h + 1]
        for part, w in zip(parts[1:], weights[1:]):
            o = o + part[:, cols].astype(jnp.float32) * w[:, h:h + 1]
        yield cols, o
    yield slice(width, width + LANES), pack_stats(jnp.where(used, top, 0.0), jnp.where(used, total, 0.0))


def merge_cores_kernel(keep_ref, other_ref, out_ref):
    for cols, o in merged([keep_ref, other_ref]):
        out_ref[:, :, cols] = o.reshape(o.shape[0] // PAIR, PAIR, -1).astype(jnp.bfloat16)


def merge_chips_kernel(parts_ref, out_ref):
    width = out_ref.shape[2]
    for cols, o in merged([parts_ref.at[n] for n in range(parts_ref.shape[0])]):
        if cols.start < width:
            for s in range(STEPS):
                out_ref[s, :, cols] = o[s * SLOT:(s + 1) * SLOT].astype(jnp.bfloat16)


def merge(kernel, parts, shape, name):
    return pl.pallas_call(
        kernel,
        out_shape=jax.ShapeDtypeStruct(shape, jnp.bfloat16),
        in_specs=[VMEM] * len(parts),
        out_specs=VMEM,
        compiler_params=pltpu.CompilerParams(vmem_limit_bytes=16 << 20),
        name=name,
    )(*parts)


def body(cache_kv, fresh_qkv, list_rows, counts):
    device_count = lax.axis_size("blk")
    me = lax.axis_index("blk")
    slot_count = list_rows.shape[1]
    bits = device_count.bit_length() - 1
    width = cache_kv.shape[2]

    def swap(x, mask):
        return lax.ppermute(x, "blk", [(i, i ^ mask) for i in range(device_count)])

    fresh = fresh_qkv.transpose(1, 2, 0, 3)
    mine, fresh_key, fresh_value = (fresh[:, i] for i in range(3))
    half = width // 2
    early = sort_cache(cache_kv, 0, half, None, "sort_first")
    column = mine
    for n in range(bits - 1, 2, -1):
        other = swap(column, 1 << n)
        if n == bits - 1:
            other, early, counts, list_rows = lax.optimization_barrier((other, early, counts, list_rows))
        column = jnp.concatenate([column, other])
    table = jnp.concatenate([counts, list_rows, jnp.full((STEPS, 1), me, jnp.int32)], axis=1)
    late = sort_cache(cache_kv, half, half, (table, fresh_key, fresh_value), "sort_second")
    others = [swap(column, mask) for mask in (4, 2, 6)]
    others, column, late = lax.optimization_barrier((others, column, late))
    beside = swap(column, 1)
    others = jnp.concatenate(others)
    gathered = [column, others, beside, swap(others, 1)]
    key, value, fresh_key, fresh_value, target, bias, fresh_bias = late
    keep, send = attend(slot_count, target, bias, fresh_bias, fresh_key, fresh_value, [*early, key, value], gathered)
    chips = device_count // 2
    parts = merge(merge_cores_kernel, [keep, swap(send, 1)], (chips, PAIR, width + LANES), "merge_cores")
    groups = [[chip * 2 + core for chip in range(chips)] for core in range(2)]
    parts = lax.all_to_all(parts, "blk", split_axis=0, concat_axis=0, axis_index_groups=groups, tiled=True)
    return merge(merge_chips_kernel, [parts], (STEPS, SLOT, width), "merge_chips")


def solution(mesh):
    in_specs = (
        P(("groups", "blk"), None, None),
        P(None, ("groups", "blk"), None, None),
        P(None, ("groups", "blk")),
        P(None, "groups"),
    )
    out_specs = P(None, ("groups", "blk"), None)
    return jax.shard_map(body, mesh=mesh, in_specs=in_specs, out_specs=out_specs, check_vma=False)
```

```python
import jax
import jax.numpy as jnp
from jax import lax
from jax.experimental import pallas as pl
from jax.experimental.pallas import tpu as pltpu
from jax.sharding import PartitionSpec as P

HEAD = 128
SLOT = 4
STEPS = 2
PAIR = STEPS * SLOT
LOG2E = 1.4426950408889634
SCALE = HEAD ** -0.5 * LOG2E
FAR = -1e30
LANES = 128
PART = 16
SLOT_BITS = 2
WAITS = 4
SORT_VMEM = 48
VMEM = pl.BlockSpec(memory_space=pltpu.VMEM)
SMEM = pl.BlockSpec(memory_space=pltpu.SMEM)
HBM = pl.BlockSpec(memory_space=pltpu.HBM)


def exchange_order(bits):
    first = list(range(bits - 1, 0, -1))
    return first, first[:-3] + [first[-2], first[-1], first[-3]]


def place_of(dev, me, bits):
    mask = dev ^ me
    first, second = exchange_order(bits)
    places = [sum(((mask >> n) & 1) << e for e, n in enumerate(order)) for order in (first, second)]
    return jnp.where((dev & 1) == 1, places[1], places[0]) + ((mask & 1) << (bits - 1))


def plan_kernel_part(table_ref, slots, target_ref, bias_ref, fresh_bias_ref):
    device_count = table_ref.shape[1] - slots - 1
    bits = device_count.bit_length() - 1
    me = table_ref[0, device_count + slots]
    col = lax.broadcasted_iota(jnp.int32, target_ref.shape, 1)

    def one_device(dev, carry):
        start0, start1, target = carry
        count0, count1 = table_ref[0, dev], table_ref[1, dev]
        local = col - place_of(dev, me, bits) * (STEPS * slots)
        slot, step = local >> 1, local & 1
        rank = slot + jnp.where(step == 0, start0, start1)
        home = rank >> SLOT_BITS
        home = ((home ^ me) & 1) * (device_count // 2) + (home >> 1)
        row = home * PAIR + step * SLOT + (rank & (SLOT - 1))
        good = (local >= 0) & (slot < jnp.where(step == 0, count0, count1))
        return start0 + count0, start1 + count1, jnp.where(good, row, target)

    carry = (jnp.int32(0), jnp.int32(0), jnp.full(target_ref.shape, -1, jnp.int32))
    if device_count <= 16:
        for dev in range(device_count):
            carry = one_device(dev, carry)
    else:
        carry = lax.fori_loop(0, device_count, one_device, carry)
    target_ref[...] = carry[2]

    live0 = [i < table_ref[0, me] for i in range(slots)]
    live1 = [i < table_ref[1, me] for i in range(slots)]
    row0 = [jnp.where(live0[i], table_ref[0, device_count + i], -1) for i in range(slots)]
    row1 = [jnp.where(live1[i], table_ref[1, device_count + i], -2) for i in range(slots)]
    token = lax.broadcasted_iota(jnp.int32, bias_ref.shape, 1)
    second = lax.broadcasted_iota(jnp.int32, bias_ref.shape, 0) >= SLOT
    gone = token == row0[0]
    for i in range(1, slots):
        gone = gone | (token == row0[i])
    later = token == row1[0]
    for i in range(1, slots):
        later = later | (token == row1[i])
    bias_ref[...] = jnp.where(gone | (second & later), FAR, 0.0)
    col = lax.broadcasted_iota(jnp.int32, fresh_bias_ref.shape, 1)
    second = (lax.broadcasted_iota(jnp.int32, fresh_bias_ref.shape, 0) >= SLOT).astype(jnp.int32)
    seen = jnp.zeros(fresh_bias_ref.shape, jnp.int32)
    for i in range(slots):
        again = row1[0] == row0[i]
        for j in range(1, slots):
            again = again | (row1[j] == row0[i])
        kept = (live0[i] & jnp.logical_not(again)).astype(jnp.int32)
        early = jnp.where(second == 1, kept, live0[i].astype(jnp.int32))
        seen = jnp.where(col == 2 * i, early, seen)
        seen = jnp.where(col == 2 * i + 1, second * live1[i].astype(jnp.int32), seen)
    fresh_bias_ref[...] = jnp.where(seen == 1, 0.0, FAR)


def sort_kernel(first, planned, *refs):
    refs = list(refs)
    table_ref = refs.pop(0) if planned else None
    cache_ref = refs.pop(0)
    new_refs = [refs.pop(0) for _ in range(2)] if planned else []
    key_ref, value_ref, *small_refs, held, sems = refs
    tokens, width = key_ref.shape
    block = min(128, tokens)
    blocks = tokens // block

    def fetch(i):
        part = pl.ds(i * block, block)
        return pltpu.make_async_copy(
            cache_ref.at[part, :, pl.ds(first, width)], held.at[part, :, pl.ds(0, width)], sems.at[i]
        )

    for i in range(blocks):
        fetch(i).start()
    if planned:
        slots = new_refs[0].shape[0]
        for ref, new_ref in zip(small_refs[:2], new_refs):
            ref[...] = jnp.zeros_like(ref)
            ref[0:STEPS * slots, :] = new_ref.reshape(STEPS * slots, ref.shape[1])[...]
        plan_kernel_part(table_ref, slots, *small_refs[2:])
    out = lax.broadcasted_iota(jnp.int32, (2 * block, 2 * block), 0)
    src = lax.broadcasted_iota(jnp.int32, (2 * block, 2 * block), 1)
    order = (src == jnp.where(out < block, 2 * out, 2 * (out - block) + 1)).astype(jnp.bfloat16)
    pairs = held.reshape(2 * tokens, held.shape[2])
    for i in range(blocks):
        if i % WAITS == 0:
            for j in range(i, min(i + WAITS, blocks)):
                fetch(j).wait()
        rows = slice(i * block, (i + 1) * block)
        for c in range(0, width, 256):
            part = pairs[2 * i * block:2 * (i + 1) * block, c:c + 256]
            part = jnp.dot(order, part, preferred_element_type=jnp.float32).astype(jnp.bfloat16)
            key_ref[rows, c:c + 256] = part[:block]
            value_ref[rows, c:c + 256] = part[block:]


def sort_cache(cache, first, width, plan, name):
    tokens, _, full = cache.shape
    f32, bf16 = jnp.float32, jnp.bfloat16
    shapes = [jax.ShapeDtypeStruct((tokens, width), bf16)] * 2
    inputs, specs = [cache], [HBM]
    if plan:
        table, fresh_key, fresh_value = plan
        slots = fresh_key.shape[0]
        device_count = table.shape[1] - slots - 1
        fresh_rows = -(-STEPS * slots // 16) * 16
        shapes += [jax.ShapeDtypeStruct((fresh_rows, full), bf16)] * 2
        shapes += [
            jax.ShapeDtypeStruct((1, device_count * STEPS * slots), jnp.int32),
            jax.ShapeDtypeStruct((PAIR, tokens), f32),
            jax.ShapeDtypeStruct((PAIR, fresh_rows), f32),
        ]
        inputs, specs = [table, cache, fresh_key, fresh_value], [SMEM, HBM, VMEM, VMEM]

    def kernel(*refs):
        sort_kernel(first, bool(plan), *refs)

    blocks = tokens // min(128, tokens)
    return pl.pallas_call(
        kernel,
        out_shape=tuple(shapes),
        in_specs=specs,
        out_specs=(VMEM,) * len(shapes),
        scratch_shapes=[
            pltpu.VMEM((tokens, 2, width + LANES), bf16),
            pltpu.SemaphoreType.DMA((blocks,)),
        ],
        compiler_params=pltpu.CompilerParams(vmem_limit_bytes=SORT_VMEM << 20),
        cost_estimate=pl.CostEstimate(
            flops=8 * 128 * tokens * width, bytes_accessed=8 * tokens * width, transcendentals=0
        ),
        name=name,
    )(*inputs)


def two_parts(x):
    high = x.astype(jnp.bfloat16).astype(jnp.float32)
    return high, x - high


def pack_stats(high, total):
    lane = lax.broadcasted_iota(jnp.int32, high.shape, 1)
    high = jnp.where(lane < PART, high, 0.0)
    total = jnp.where(lane < PART, total, 0.0)
    stats, rest = two_parts(high)
    second, third = two_parts(rest)
    for n, part in enumerate((second, third) + two_parts(total)):
        stats = stats + pltpu.roll(part, PART * (n + 1), 1)
    return stats


def unpack_stats(stats):
    def part(n):
        return pltpu.roll(stats, LANES - PART * n, 1)

    return stats + part(1) + part(2), part(3) + part(4)


def attend_kernel(target_ref, bias_ref, fresh_bias_ref, fresh_key_ref, fresh_value_ref, *rest):
    key_refs, value_refs, gathered_refs, (keep_ref, send_ref) = rest[0:4:2], rest[1:4:2], rest[4:-2], rest[-2:]
    width = fresh_key_ref.shape[1]
    part_heads = key_refs[0].shape[1] // HEAD
    tokens = key_refs[0].shape[0]
    heads = width // HEAD
    half = keep_ref.shape[0]
    nt = (((1,), (1,)), ((), ()))

    def attend_rows(base, chunk, stores):
        row = lax.broadcasted_iota(jnp.int32, (chunk, target_ref.shape[1]), 0)
        pick = (row == target_ref[...] - base).astype(jnp.bfloat16)
        slots = [ref.reshape(ref.shape[0] * STEPS, width)[...].astype(jnp.float32) for ref in gathered_refs]
        slots = jnp.concatenate(slots).astype(jnp.bfloat16)
        queries = jnp.dot(pick, slots, preferred_element_type=jnp.float32).astype(jnp.bfloat16)
        bias = bias_ref[...]
        fresh_bias = fresh_bias_ref[...]
        lane = lax.broadcasted_iota(jnp.int32, (chunk, LANES), 1)
        highs = jnp.zeros((chunk, LANES), jnp.float32)
        totals = jnp.zeros((chunk, LANES), jnp.float32)
        ones = jnp.ones((tokens, LANES), jnp.bfloat16)

        def block_of(refs, h):
            at = h % part_heads * HEAD
            return refs[h // part_heads][:, at:at + HEAD]

        def score(h):
            cols = slice(h * HEAD, (h + 1) * HEAD)
            q = queries[:, cols]
            s = lax.dot_general(q, block_of(key_refs, h), nt, preferred_element_type=jnp.float32)
            sf = lax.dot_general(q, fresh_key_ref[:, cols], nt, preferred_element_type=jnp.float32)
            s = (s.reshape(chunk // PAIR, PAIR, -1) + bias[None]).reshape(chunk, -1)
            sf = (sf.reshape(chunk // PAIR, PAIR, -1) + fresh_bias[None]).reshape(chunk, -1)
            return s, sf

        following = score(0)
        for h in range(heads):
            cols = slice(h * HEAD, (h + 1) * HEAD)
            s, sf = following
            if h + 1 < heads:
                following = score(h + 1)
            high = jnp.maximum(jnp.max(s, axis=1, keepdims=True), jnp.max(sf, axis=1, keepdims=True))
            w = jnp.exp2((s - high) * SCALE).astype(jnp.bfloat16)
            wf = jnp.exp2((sf - high) * SCALE).astype(jnp.bfloat16)
            value = jnp.concatenate([block_of(value_refs, h), ones], axis=1)
            fresh_value = jnp.concatenate([fresh_value_ref[:, cols], ones[:fresh_value_ref.shape[0]]], axis=1)
            o = jnp.dot(w, value, preferred_element_type=jnp.float32)
            o += jnp.dot(wf, fresh_value, preferred_element_type=jnp.float32)
            total = o[:, HEAD:]
            o = o[:, :HEAD] * (1.0 / total)
            for ref, to, start, count in stores:
                ref[pl.ds(to, count), cols] = o[start:start + count].astype(ref.dtype)
            highs = jnp.where(lane == h, high, highs)
            totals = jnp.where(lane == h, total, totals)
        stats = pack_stats(highs, totals)
        for ref, to, start, count in stores:
            ref[pl.ds(to, count), width:] = stats[start:start + count].astype(ref.dtype)

    if 2 * half <= 128:
        attend_rows(0, 2 * half, [(keep_ref, 0, 0, half), (send_ref, 0, half, half)])
    else:
        for ref, base in ((keep_ref, 0), (send_ref, half)):
            @pl.loop(0, half // 128)
            def _(i, ref=ref, base=base):
                to = pl.multiple_of(i * 128, 128)
                attend_rows(base + to, 128, [(ref, to, 0, 128)])


def attend(slots, target, bias, fresh_bias, fresh_key, fresh_value, sorted_parts, gathered):
    tokens, width = sorted_parts[0].shape[0], fresh_key.shape[1]
    rows = target.shape[1] * SLOT // slots
    shape = (rows // 2, width + LANES)
    return pl.pallas_call(
        attend_kernel,
        out_shape=(jax.ShapeDtypeStruct(shape, jnp.float32), jax.ShapeDtypeStruct(shape, jnp.bfloat16)),
        in_specs=[VMEM] * (5 + len(sorted_parts) + len(gathered)),
        out_specs=(VMEM, VMEM),
        compiler_params=pltpu.CompilerParams(vmem_limit_bytes=24 << 20),
        cost_estimate=pl.CostEstimate(
            flops=4 * rows * tokens * width, bytes_accessed=4 * tokens * width,
            transcendentals=rows * tokens * width // HEAD,
        ),
        name="attend",
    )(target, bias, fresh_bias, fresh_key, fresh_value, *sorted_parts, *gathered)


def merged(parts):
    width = parts[0].shape[1] - LANES
    stats = [unpack_stats(part[:, width:].astype(jnp.float32)) for part in parts]
    top = stats[0][0]
    for high, _ in stats[1:]:
        top = jnp.maximum(top, high)
    weights = [total * jnp.exp2((high - top) * SCALE) for high, total in stats]
    total = weights[0]
    for w in weights[1:]:
        total = total + w
    used = lax.broadcasted_iota(jnp.int32, total.shape, 1) < width // HEAD
    share = 1.0 / jnp.where(used, total, 1.0)
    weights = [w * share for w in weights]
    for h in range(width // HEAD):
        cols = slice(h * HEAD, (h + 1) * HEAD)
        o = parts[0][:, cols].astype(jnp.float32) * weights[0][:, h:h + 1]
        for part, w in zip(parts[1:], weights[1:]):
            o = o + part[:, cols].astype(jnp.float32) * w[:, h:h + 1]
        yield cols, o
    yield slice(width, width + LANES), pack_stats(jnp.where(used, top, 0.0), jnp.where(used, total, 0.0))


def merge_cores_kernel(keep_ref, other_ref, out_ref):
    for cols, o in merged([keep_ref, other_ref]):
        out_ref[:, :, cols] = o.reshape(o.shape[0] // PAIR, PAIR, -1).astype(jnp.bfloat16)


def merge_chips_kernel(parts_ref, out_ref):
    width = out_ref.shape[2]
    for cols, o in merged([parts_ref.at[n] for n in range(parts_ref.shape[0])]):
        if cols.start < width:
            for s in range(STEPS):
                out_ref[s, :, cols] = o[s * SLOT:(s + 1) * SLOT].astype(jnp.bfloat16)


def merge(kernel, parts, shape, name):
    return pl.pallas_call(
        kernel,
        out_shape=jax.ShapeDtypeStruct(shape, jnp.bfloat16),
        in_specs=[VMEM] * len(parts),
        out_specs=VMEM,
        compiler_params=pltpu.CompilerParams(vmem_limit_bytes=16 << 20),
        name=name,
    )(*parts)


def body(cache_kv, fresh_qkv, list_rows, counts):
    device_count = lax.axis_size("blk")
    me = lax.axis_index("blk")
    slot_count = list_rows.shape[1]
    bits = device_count.bit_length() - 1
    width = cache_kv.shape[2]

    def swap(x, *masks):
        return lax.ppermute(x, "blk", [(i, i ^ masks[i % len(masks)]) for i in range(device_count)])

    fresh = fresh_qkv.transpose(1, 2, 0, 3)
    mine, fresh_key, fresh_value = (fresh[:, i] for i in range(3))
    half = width // 2
    early = sort_cache(cache_kv, 0, half, None, "sort_first")
    column = mine
    steps = [(1 << m, 1 << n) for m, n in zip(*exchange_order(bits))]
    for e, masks in enumerate(steps[:-2]):
        other = swap(column, *masks)
        if e == 0:
            other, early, counts, list_rows = lax.optimization_barrier((other, early, counts, list_rows))
        column = jnp.concatenate([column, other])
    table = jnp.concatenate([counts, list_rows, jnp.full((STEPS, 1), me, jnp.int32)], axis=1)
    late = sort_cache(cache_kv, half, half, (table, fresh_key, fresh_value), "sort_second")
    both = [m | n for m, n in zip(*steps[-2:])]
    others = [swap(column, *masks) for masks in (*steps[-2:], both)]
    others, column, late = lax.optimization_barrier((others, column, late))
    beside = swap(column, 1)
    others = jnp.concatenate(others)
    gathered = [column, others, beside, swap(others, 1)]
    key, value, fresh_key, fresh_value, target, bias, fresh_bias = late
    keep, send = attend(slot_count, target, bias, fresh_bias, fresh_key, fresh_value, [*early, key, value], gathered)
    chips = device_count // 2
    parts = merge(merge_cores_kernel, [keep, swap(send, 1)], (chips, PAIR, width + LANES), "merge_cores")
    groups = [[chip * 2 + core for chip in range(chips)] for core in range(2)]
    parts = lax.all_to_all(parts, "blk", split_axis=0, concat_axis=0, axis_index_groups=groups, tiled=True)
    return merge(merge_chips_kernel, [parts], (STEPS, SLOT, width), "merge_chips")


def solution(mesh):
    in_specs = (
        P(("groups", "blk"), None, None),
        P(None, ("groups", "blk"), None, None),
        P(None, ("groups", "blk")),
        P(None, "groups"),
    )
    out_specs = P(None, ("groups", "blk"), None)
    return jax.shard_map(body, mesh=mesh, in_specs=in_specs, out_specs=out_specs, check_vma=False)
```

```python
import jax
import jax.numpy as jnp
from jax import lax
from jax.experimental import pallas as pl
from jax.experimental.pallas import tpu as pltpu
from jax.sharding import PartitionSpec as P

HEAD = 128
SLOT = 4
STEPS = 2
PAIR = STEPS * SLOT
LOG2E = 1.4426950408889634
SCALE = HEAD ** -0.5 * LOG2E
FAR = -1e30
LANES = 128
PART = 16
SLOT_BITS = 2
WAITS = 4
SORT_VMEM = 48
VMEM = pl.BlockSpec(memory_space=pltpu.VMEM)
SMEM = pl.BlockSpec(memory_space=pltpu.SMEM)
HBM = pl.BlockSpec(memory_space=pltpu.HBM)


def exchange_order(bits):
    first = list(range(bits - 1, 0, -1))
    return first, first[:-3] + [first[-2], first[-1], first[-3]]


def place_of(dev, me, bits):
    mask = dev ^ me
    first, second = exchange_order(bits)
    places = [sum(((mask >> n) & 1) << e for e, n in enumerate(order)) for order in (first, second)]
    return jnp.where((dev & 1) == 1, places[1], places[0]) + ((mask & 1) << (bits - 1))


def plan_kernel_part(table_ref, slots, target_ref, bias_ref, fresh_bias_ref):
    device_count = table_ref.shape[1] - slots - 1
    bits = device_count.bit_length() - 1
    me = table_ref[0, device_count + slots]
    col = lax.broadcasted_iota(jnp.int32, target_ref.shape, 1)

    def one_device(dev, carry):
        start0, start1, target = carry
        count0, count1 = table_ref[0, dev], table_ref[1, dev]
        local = col - place_of(dev, me, bits) * (STEPS * slots)
        slot, step = local >> 1, local & 1
        rank = slot + jnp.where(step == 0, start0, start1)
        home = rank >> SLOT_BITS
        home = ((home ^ me) & 1) * (device_count // 2) + (home >> 1)
        row = home * PAIR + step * SLOT + (rank & (SLOT - 1))
        good = (local >= 0) & (slot < jnp.where(step == 0, count0, count1))
        return start0 + count0, start1 + count1, jnp.where(good, row, target)

    carry = (jnp.int32(0), jnp.int32(0), jnp.full(target_ref.shape, -1, jnp.int32))
    if device_count <= 16:
        for dev in range(device_count):
            carry = one_device(dev, carry)
    else:
        carry = lax.fori_loop(0, device_count, one_device, carry)
    target_ref[...] = carry[2]

    live0 = [i < table_ref[0, me] for i in range(slots)]
    live1 = [i < table_ref[1, me] for i in range(slots)]
    row0 = [jnp.where(live0[i], table_ref[0, device_count + i], -1) for i in range(slots)]
    row1 = [jnp.where(live1[i], table_ref[1, device_count + i], -2) for i in range(slots)]
    token = lax.broadcasted_iota(jnp.int32, bias_ref.shape, 1)
    second = lax.broadcasted_iota(jnp.int32, bias_ref.shape, 0) >= SLOT
    gone = token == row0[0]
    for i in range(1, slots):
        gone = gone | (token == row0[i])
    later = token == row1[0]
    for i in range(1, slots):
        later = later | (token == row1[i])
    bias_ref[...] = jnp.where(gone | (second & later), FAR, 0.0)
    col = lax.broadcasted_iota(jnp.int32, fresh_bias_ref.shape, 1)
    second = (lax.broadcasted_iota(jnp.int32, fresh_bias_ref.shape, 0) >= SLOT).astype(jnp.int32)
    seen = jnp.zeros(fresh_bias_ref.shape, jnp.int32)
    for i in range(slots):
        again = row1[0] == row0[i]
        for j in range(1, slots):
            again = again | (row1[j] == row0[i])
        kept = (live0[i] & jnp.logical_not(again)).astype(jnp.int32)
        early = jnp.where(second == 1, kept, live0[i].astype(jnp.int32))
        seen = jnp.where(col == 2 * i, early, seen)
        seen = jnp.where(col == 2 * i + 1, second * live1[i].astype(jnp.int32), seen)
    fresh_bias_ref[...] = jnp.where(seen == 1, 0.0, FAR)


def sort_kernel(first, planned, *refs):
    refs = list(refs)
    table_ref = refs.pop(0) if planned else None
    cache_ref = refs.pop(0)
    new_refs = [refs.pop(0) for _ in range(2)] if planned else []
    key_ref, value_ref, *small_refs, held, sems = refs
    tokens, width = key_ref.shape
    block = min(128, tokens)
    blocks = tokens // block

    def fetch(i):
        part = pl.ds(i * block, block)
        return pltpu.make_async_copy(
            cache_ref.at[part, :, pl.ds(first, width)], held.at[part, :, pl.ds(0, width)], sems.at[i]
        )

    for i in range(blocks):
        fetch(i).start()
    if planned:
        slots = new_refs[0].shape[0]
        for ref, new_ref in zip(small_refs[:2], new_refs):
            ref[...] = jnp.zeros_like(ref)
            ref[0:STEPS * slots, :] = new_ref.reshape(STEPS * slots, ref.shape[1])[...]
        plan_kernel_part(table_ref, slots, *small_refs[2:])
    out = lax.broadcasted_iota(jnp.int32, (2 * block, 2 * block), 0)
    src = lax.broadcasted_iota(jnp.int32, (2 * block, 2 * block), 1)
    order = (src == jnp.where(out < block, 2 * out, 2 * (out - block) + 1)).astype(jnp.bfloat16)
    pairs = held.reshape(2 * tokens, held.shape[2])
    for i in range(blocks):
        if i % WAITS == 0:
            for j in range(i, min(i + WAITS, blocks)):
                fetch(j).wait()
        rows = slice(i * block, (i + 1) * block)
        for c in range(0, width, 256):
            part = pairs[2 * i * block:2 * (i + 1) * block, c:c + 256]
            part = jnp.dot(order, part, preferred_element_type=jnp.float32).astype(jnp.bfloat16)
            key_ref[rows, c:c + 256] = part[:block]
            value_ref[rows, c:c + 256] = part[block:]


def sort_cache(cache, first, width, plan, name):
    tokens, _, full = cache.shape
    f32, bf16 = jnp.float32, jnp.bfloat16
    shapes = [jax.ShapeDtypeStruct((tokens, width), bf16)] * 2
    inputs, specs = [cache], [HBM]
    if plan:
        table, fresh_key, fresh_value = plan
        slots = fresh_key.shape[0]
        device_count = table.shape[1] - slots - 1
        fresh_rows = -(-STEPS * slots // 16) * 16
        shapes += [jax.ShapeDtypeStruct((fresh_rows, full), bf16)] * 2
        shapes += [
            jax.ShapeDtypeStruct((1, device_count * STEPS * slots), jnp.int32),
            jax.ShapeDtypeStruct((PAIR, tokens), f32),
            jax.ShapeDtypeStruct((PAIR, fresh_rows), f32),
        ]
        inputs, specs = [table, cache, fresh_key, fresh_value], [SMEM, HBM, VMEM, VMEM]

    def kernel(*refs):
        sort_kernel(first, bool(plan), *refs)

    blocks = tokens // min(128, tokens)
    return pl.pallas_call(
        kernel,
        out_shape=tuple(shapes),
        in_specs=specs,
        out_specs=(VMEM,) * len(shapes),
        scratch_shapes=[
            pltpu.VMEM((tokens, 2, width + LANES), bf16),
            pltpu.SemaphoreType.DMA((blocks,)),
        ],
        compiler_params=pltpu.CompilerParams(vmem_limit_bytes=SORT_VMEM << 20),
        cost_estimate=pl.CostEstimate(
            flops=8 * 128 * tokens * width, bytes_accessed=8 * tokens * width, transcendentals=0
        ),
        name=name,
    )(*inputs)


def two_parts(x):
    high = x.astype(jnp.bfloat16).astype(jnp.float32)
    return high, x - high


def pack_stats(high, total):
    lane = lax.broadcasted_iota(jnp.int32, high.shape, 1)
    high = jnp.where(lane < PART, high, 0.0)
    total = jnp.where(lane < PART, total, 0.0)
    stats, rest = two_parts(high)
    second, third = two_parts(rest)
    for n, part in enumerate((second, third) + two_parts(total)):
        stats = stats + pltpu.roll(part, PART * (n + 1), 1)
    return stats


def unpack_stats(stats):
    def part(n):
        return pltpu.roll(stats, LANES - PART * n, 1)

    return stats + part(1) + part(2), part(3) + part(4)


def attend_kernel(target_ref, bias_ref, fresh_bias_ref, fresh_key_ref, fresh_value_ref, *rest):
    key_refs, value_refs, gathered_refs, (keep_ref, send_ref) = rest[0:4:2], rest[1:4:2], rest[4:-2], rest[-2:]
    width = fresh_key_ref.shape[1]
    part_heads = key_refs[0].shape[1] // HEAD
    tokens = key_refs[0].shape[0]
    heads = width // HEAD
    half = keep_ref.shape[0]
    nt = (((1,), (1,)), ((), ()))

    def attend_rows(base, chunk, stores):
        row = lax.broadcasted_iota(jnp.int32, (chunk, target_ref.shape[1]), 0)
        pick = (row == target_ref[...] - base).astype(jnp.bfloat16)
        slots = [ref.reshape(ref.shape[0] * STEPS, width)[...].astype(jnp.float32) for ref in gathered_refs]
        slots = jnp.concatenate(slots).astype(jnp.bfloat16)
        queries = jnp.dot(pick, slots, preferred_element_type=jnp.float32).astype(jnp.bfloat16)
        bias = bias_ref[...]
        fresh_bias = fresh_bias_ref[...]
        lane = lax.broadcasted_iota(jnp.int32, (chunk, LANES), 1)
        highs = jnp.zeros((chunk, LANES), jnp.float32)
        totals = jnp.zeros((chunk, LANES), jnp.float32)
        ones = jnp.ones((tokens, LANES), jnp.bfloat16)

        def block_of(refs, h):
            part, at = (0, h) if h < part_heads else (1, h - part_heads)
            return refs[part][:, at * HEAD:(at + 1) * HEAD]

        def score(h):
            cols = slice(h * HEAD, (h + 1) * HEAD)
            q = queries[:, cols]
            s = lax.dot_general(q, block_of(key_refs, h), nt, preferred_element_type=jnp.float32)
            sf = lax.dot_general(q, fresh_key_ref[:, cols], nt, preferred_element_type=jnp.float32)
            s = (s.reshape(chunk // PAIR, PAIR, -1) + bias[None]).reshape(chunk, -1)
            sf = (sf.reshape(chunk // PAIR, PAIR, -1) + fresh_bias[None]).reshape(chunk, -1)
            return s, sf

        following = score(0)
        for h in range(heads):
            cols = slice(h * HEAD, (h + 1) * HEAD)
            s, sf = following
            if h + 1 < heads:
                following = score(h + 1)
            high = jnp.maximum(jnp.max(s, axis=1, keepdims=True), jnp.max(sf, axis=1, keepdims=True))
            w = jnp.exp2((s - high) * SCALE).astype(jnp.bfloat16)
            wf = jnp.exp2((sf - high) * SCALE).astype(jnp.bfloat16)
            value = jnp.concatenate([block_of(value_refs, h), ones], axis=1)
            fresh_value = jnp.concatenate([fresh_value_ref[:, cols], ones[:fresh_value_ref.shape[0]]], axis=1)
            o = jnp.dot(w, value, preferred_element_type=jnp.float32)
            o += jnp.dot(wf, fresh_value, preferred_element_type=jnp.float32)
            total = o[:, HEAD:]
            o = o[:, :HEAD] * (1.0 / total)
            for ref, to, start, count in stores:
                ref[pl.ds(to, count), cols] = o[start:start + count].astype(ref.dtype)
            highs = jnp.where(lane == h, high, highs)
            totals = jnp.where(lane == h, total, totals)
        stats = pack_stats(highs, totals)
        for ref, to, start, count in stores:
            ref[pl.ds(to, count), width:] = stats[start:start + count].astype(ref.dtype)

    if 2 * half <= 128:
        attend_rows(0, 2 * half, [(keep_ref, 0, 0, half), (send_ref, 0, half, half)])
    else:
        for ref, base in ((keep_ref, 0), (send_ref, half)):
            @pl.loop(0, half // 128)
            def _(i, ref=ref, base=base):
                to = pl.multiple_of(i * 128, 128)
                attend_rows(base + to, 128, [(ref, to, 0, 128)])


def attend(slots, target, bias, fresh_bias, fresh_key, fresh_value, sorted_parts, gathered):
    tokens, width = sorted_parts[0].shape[0], fresh_key.shape[1]
    rows = target.shape[1] * SLOT // slots
    shape = (rows // 2, width + LANES)
    return pl.pallas_call(
        attend_kernel,
        out_shape=(jax.ShapeDtypeStruct(shape, jnp.float32), jax.ShapeDtypeStruct(shape, jnp.bfloat16)),
        in_specs=[VMEM] * (5 + len(sorted_parts) + len(gathered)),
        out_specs=(VMEM, VMEM),
        compiler_params=pltpu.CompilerParams(vmem_limit_bytes=24 << 20),
        cost_estimate=pl.CostEstimate(
            flops=4 * rows * tokens * width, bytes_accessed=4 * tokens * width,
            transcendentals=rows * tokens * width // HEAD,
        ),
        name="attend",
    )(target, bias, fresh_bias, fresh_key, fresh_value, *sorted_parts, *gathered)


def merged(parts):
    width = parts[0].shape[1] - LANES
    stats = [unpack_stats(part[:, width:].astype(jnp.float32)) for part in parts]
    top = stats[0][0]
    for high, _ in stats[1:]:
        top = jnp.maximum(top, high)
    weights = [total * jnp.exp2((high - top) * SCALE) for high, total in stats]
    total = weights[0]
    for w in weights[1:]:
        total = total + w
    used = lax.broadcasted_iota(jnp.int32, total.shape, 1) < width // HEAD
    share = 1.0 / jnp.where(used, total, 1.0)
    weights = [w * share for w in weights]
    for h in range(width // HEAD):
        cols = slice(h * HEAD, (h + 1) * HEAD)
        o = parts[0][:, cols].astype(jnp.float32) * weights[0][:, h:h + 1]
        for part, w in zip(parts[1:], weights[1:]):
            o = o + part[:, cols].astype(jnp.float32) * w[:, h:h + 1]
        yield cols, o
    yield slice(width, width + LANES), pack_stats(jnp.where(used, top, 0.0), jnp.where(used, total, 0.0))


def merge_cores_kernel(keep_ref, other_ref, out_ref):
    for cols, o in merged([keep_ref, other_ref]):
        out_ref[:, :, cols] = o.reshape(o.shape[0] // PAIR, PAIR, -1).astype(jnp.bfloat16)


def merge_chips_kernel(parts_ref, out_ref):
    width = out_ref.shape[2]
    for cols, o in merged([parts_ref.at[n] for n in range(parts_ref.shape[0])]):
        if cols.start < width:
            for s in range(STEPS):
                out_ref[s, :, cols] = o[s * SLOT:(s + 1) * SLOT].astype(jnp.bfloat16)


def merge(kernel, parts, shape, name):
    return pl.pallas_call(
        kernel,
        out_shape=jax.ShapeDtypeStruct(shape, jnp.bfloat16),
        in_specs=[VMEM] * len(parts),
        out_specs=VMEM,
        compiler_params=pltpu.CompilerParams(vmem_limit_bytes=16 << 20),
        name=name,
    )(*parts)


def body(cache_kv, fresh_qkv, list_rows, counts):
    device_count = lax.axis_size("blk")
    me = lax.axis_index("blk")
    slot_count = list_rows.shape[1]
    bits = device_count.bit_length() - 1
    width = cache_kv.shape[2]

    def swap(x, *masks):
        return lax.ppermute(x, "blk", [(i, i ^ masks[i % len(masks)]) for i in range(device_count)])

    fresh = fresh_qkv.transpose(1, 2, 0, 3)
    mine, fresh_key, fresh_value = (fresh[:, i] for i in range(3))
    most = width * 2 // 3
    early = sort_cache(cache_kv, 0, most, None, "sort_first")
    column = mine
    steps = [(1 << m, 1 << n) for m, n in zip(*exchange_order(bits))]
    for e, masks in enumerate(steps[:-2]):
        other = swap(column, *masks)
        if e == 0:
            other, early, counts, list_rows = lax.optimization_barrier((other, early, counts, list_rows))
        column = jnp.concatenate([column, other])
    table = jnp.concatenate([counts, list_rows, jnp.full((STEPS, 1), me, jnp.int32)], axis=1)
    late = sort_cache(cache_kv, most, width - most, (table, fresh_key, fresh_value), "sort_second")
    both = [m | n for m, n in zip(*steps[-2:])]
    others = [swap(column, *masks) for masks in (*steps[-2:], both)]
    others, column, late = lax.optimization_barrier((others, column, late))
    beside = swap(column, 1)
    others = jnp.concatenate(others)
    gathered = [column, others, beside, swap(others, 1)]
    key, value, fresh_key, fresh_value, target, bias, fresh_bias = late
    keep, send = attend(slot_count, target, bias, fresh_bias, fresh_key, fresh_value, [*early, key, value], gathered)
    chips = device_count // 2
    parts = merge(merge_cores_kernel, [keep, swap(send, 1)], (chips, PAIR, width + LANES), "merge_cores")
    groups = [[chip * 2 + core for chip in range(chips)] for core in range(2)]
    parts = lax.all_to_all(parts, "blk", split_axis=0, concat_axis=0, axis_index_groups=groups, tiled=True)
    return merge(merge_chips_kernel, [parts], (STEPS, SLOT, width), "merge_chips")


def solution(mesh):
    in_specs = (
        P(("groups", "blk"), None, None),
        P(None, ("groups", "blk"), None, None),
        P(None, ("groups", "blk")),
        P(None, "groups"),
    )
    out_specs = P(None, ("groups", "blk"), None)
    return jax.shard_map(body, mesh=mesh, in_specs=in_specs, out_specs=out_specs, check_vma=False)
```

```python
import jax
import jax.numpy as jnp
from jax import lax
from jax.experimental import pallas as pl
from jax.experimental.pallas import tpu as pltpu
from jax.sharding import PartitionSpec as P

HEAD = 128
SLOT = 4
STEPS = 2
PAIR = STEPS * SLOT
LOG2E = 1.4426950408889634
SCALE = HEAD ** -0.5 * LOG2E
FAR = -1e30
LANES = 128
PART = 16
SLOT_BITS = 2
WAITS = 4
SORT_VMEM = 46
VMEM = pl.BlockSpec(memory_space=pltpu.VMEM)
SMEM = pl.BlockSpec(memory_space=pltpu.SMEM)
HBM = pl.BlockSpec(memory_space=pltpu.HBM)


def exchange_order(bits):
    first = list(range(bits - 1, 0, -1))
    return first, first[:-3] + [first[-2], first[-1], first[-3]]


def place_of(dev, me, bits):
    mask = dev ^ me
    first, second = exchange_order(bits)
    places = [sum(((mask >> n) & 1) << e for e, n in enumerate(order)) for order in (first, second)]
    return jnp.where((dev & 1) == 1, places[1], places[0]) + ((mask & 1) << (bits - 1))


def plan_kernel_part(table_ref, slots, target_ref, bias_ref, fresh_bias_ref):
    device_count = table_ref.shape[1] - slots - 1
    bits = device_count.bit_length() - 1
    me = table_ref[0, device_count + slots]
    col = lax.broadcasted_iota(jnp.int32, target_ref.shape, 1)

    def one_device(dev, carry):
        start0, start1, target = carry
        count0, count1 = table_ref[0, dev], table_ref[1, dev]
        local = col - place_of(dev, me, bits) * (STEPS * slots)
        slot, step = local >> 1, local & 1
        rank = slot + jnp.where(step == 0, start0, start1)
        home = rank >> SLOT_BITS
        home = ((home ^ me) & 1) * (device_count // 2) + (home >> 1)
        row = home * PAIR + step * SLOT + (rank & (SLOT - 1))
        good = (local >= 0) & (slot < jnp.where(step == 0, count0, count1))
        return start0 + count0, start1 + count1, jnp.where(good, row, target)

    carry = (jnp.int32(0), jnp.int32(0), jnp.full(target_ref.shape, -1, jnp.int32))
    if device_count <= 16:
        for dev in range(device_count):
            carry = one_device(dev, carry)
    else:
        carry = lax.fori_loop(0, device_count, one_device, carry)
    target_ref[...] = carry[2]

    live0 = [i < table_ref[0, me] for i in range(slots)]
    live1 = [i < table_ref[1, me] for i in range(slots)]
    row0 = [jnp.where(live0[i], table_ref[0, device_count + i], -1) for i in range(slots)]
    row1 = [jnp.where(live1[i], table_ref[1, device_count + i], -2) for i in range(slots)]
    token = lax.broadcasted_iota(jnp.int32, bias_ref.shape, 1)
    second = lax.broadcasted_iota(jnp.int32, bias_ref.shape, 0) >= SLOT
    gone = token == row0[0]
    for i in range(1, slots):
        gone = gone | (token == row0[i])
    later = token == row1[0]
    for i in range(1, slots):
        later = later | (token == row1[i])
    bias_ref[...] = jnp.where(gone | (second & later), FAR, 0.0)
    col = lax.broadcasted_iota(jnp.int32, fresh_bias_ref.shape, 1)
    second = (lax.broadcasted_iota(jnp.int32, fresh_bias_ref.shape, 0) >= SLOT).astype(jnp.int32)
    seen = jnp.zeros(fresh_bias_ref.shape, jnp.int32)
    for i in range(slots):
        again = row1[0] == row0[i]
        for j in range(1, slots):
            again = again | (row1[j] == row0[i])
        kept = (live0[i] & jnp.logical_not(again)).astype(jnp.int32)
        early = jnp.where(second == 1, kept, live0[i].astype(jnp.int32))
        seen = jnp.where(col == 2 * i, early, seen)
        seen = jnp.where(col == 2 * i + 1, second * live1[i].astype(jnp.int32), seen)
    fresh_bias_ref[...] = jnp.where(seen == 1, 0.0, FAR)


def sort_kernel(first, planned, *refs):
    refs = list(refs)
    table_ref = refs.pop(0) if planned else None
    cache_ref = refs.pop(0)
    new_refs = [refs.pop(0) for _ in range(2)] if planned else []
    key_ref, value_ref, *small_refs, held, sems = refs
    tokens, width = key_ref.shape
    block = min(128, tokens)
    blocks = tokens // block

    def fetch(i):
        part = pl.ds(i * block, block)
        return pltpu.make_async_copy(
            cache_ref.at[part, :, pl.ds(first, width)], held.at[part, :, pl.ds(0, width)], sems.at[i]
        )

    for i in range(blocks):
        fetch(i).start()
    if planned:
        slots = new_refs[0].shape[0]
        for ref, new_ref in zip(small_refs[:2], new_refs):
            ref[...] = jnp.zeros_like(ref)
            ref[0:STEPS * slots, :] = new_ref.reshape(STEPS * slots, ref.shape[1])[...]
        plan_kernel_part(table_ref, slots, *small_refs[2:])
    out = lax.broadcasted_iota(jnp.int32, (2 * block, 2 * block), 0)
    src = lax.broadcasted_iota(jnp.int32, (2 * block, 2 * block), 1)
    order = (src == jnp.where(out < block, 2 * out, 2 * (out - block) + 1)).astype(jnp.bfloat16)
    pairs = held.reshape(2 * tokens, held.shape[2])
    for i in range(blocks):
        if i % WAITS == 0:
            for j in range(i, min(i + WAITS, blocks)):
                fetch(j).wait()
        rows = slice(i * block, (i + 1) * block)
        for c in range(0, width, 256):
            part = pairs[2 * i * block:2 * (i + 1) * block, c:c + 256]
            part = jnp.dot(order, part, preferred_element_type=jnp.float32).astype(jnp.bfloat16)
            key_ref[rows, c:c + 256] = part[:block]
            value_ref[rows, c:c + 256] = part[block:]


def sort_cache(cache, first, width, plan, name):
    tokens, _, full = cache.shape
    f32, bf16 = jnp.float32, jnp.bfloat16
    shapes = [jax.ShapeDtypeStruct((tokens, width), bf16)] * 2
    inputs, specs = [cache], [HBM]
    if plan:
        table, fresh_key, fresh_value = plan
        slots = fresh_key.shape[0]
        device_count = table.shape[1] - slots - 1
        fresh_rows = -(-STEPS * slots // 16) * 16
        shapes += [jax.ShapeDtypeStruct((fresh_rows, full), bf16)] * 2
        shapes += [
            jax.ShapeDtypeStruct((1, device_count * STEPS * slots), jnp.int32),
            jax.ShapeDtypeStruct((PAIR, tokens), f32),
            jax.ShapeDtypeStruct((PAIR, fresh_rows), f32),
        ]
        inputs, specs = [table, cache, fresh_key, fresh_value], [SMEM, HBM, VMEM, VMEM]

    def kernel(*refs):
        sort_kernel(first, bool(plan), *refs)

    blocks = tokens // min(128, tokens)
    return pl.pallas_call(
        kernel,
        out_shape=tuple(shapes),
        in_specs=specs,
        out_specs=(VMEM,) * len(shapes),
        scratch_shapes=[
            pltpu.VMEM((tokens, 2, width + LANES), bf16),
            pltpu.SemaphoreType.DMA((blocks,)),
        ],
        compiler_params=pltpu.CompilerParams(vmem_limit_bytes=SORT_VMEM << 20),
        cost_estimate=pl.CostEstimate(
            flops=8 * 128 * tokens * width, bytes_accessed=8 * tokens * width, transcendentals=0
        ),
        name=name,
    )(*inputs)


def two_parts(x):
    high = x.astype(jnp.bfloat16).astype(jnp.float32)
    return high, x - high


def pack_stats(high, total):
    lane = lax.broadcasted_iota(jnp.int32, high.shape, 1)
    high = jnp.where(lane < PART, high, 0.0)
    total = jnp.where(lane < PART, total, 0.0)
    stats, rest = two_parts(high)
    second, third = two_parts(rest)
    for n, part in enumerate((second, third) + two_parts(total)):
        stats = stats + pltpu.roll(part, PART * (n + 1), 1)
    return stats


def unpack_stats(stats):
    def part(n):
        return pltpu.roll(stats, LANES - PART * n, 1)

    return stats + part(1) + part(2), part(3) + part(4)


def attend_kernel(target_ref, bias_ref, fresh_bias_ref, fresh_key_ref, fresh_value_ref, *rest):
    key_refs, value_refs, gathered_refs, (keep_ref, send_ref) = rest[0:4:2], rest[1:4:2], rest[4:-2], rest[-2:]
    width = fresh_key_ref.shape[1]
    part_heads = key_refs[0].shape[1] // HEAD
    tokens = key_refs[0].shape[0]
    heads = width // HEAD
    half = keep_ref.shape[0]
    nt = (((1,), (1,)), ((), ()))

    def attend_rows(base, chunk, stores):
        row = lax.broadcasted_iota(jnp.int32, (chunk, target_ref.shape[1]), 0)
        pick = (row == target_ref[...] - base).astype(jnp.bfloat16)
        slots = [ref.reshape(ref.shape[0] * STEPS, width)[...].astype(jnp.float32) for ref in gathered_refs]
        slots = jnp.concatenate(slots).astype(jnp.bfloat16)
        queries = jnp.dot(pick, slots, preferred_element_type=jnp.float32).astype(jnp.bfloat16)
        bias = bias_ref[...]
        fresh_bias = fresh_bias_ref[...]
        lane = lax.broadcasted_iota(jnp.int32, (chunk, LANES), 1)
        highs = jnp.zeros((chunk, LANES), jnp.float32)
        totals = jnp.zeros((chunk, LANES), jnp.float32)
        ones = jnp.ones((tokens, LANES), jnp.bfloat16)

        def block_of(refs, h):
            part, at = (0, h) if h < part_heads else (1, h - part_heads)
            return refs[part][:, at * HEAD:(at + 1) * HEAD]

        def score(h):
            cols = slice(h * HEAD, (h + 1) * HEAD)
            q = queries[:, cols]
            s = lax.dot_general(q, block_of(key_refs, h), nt, preferred_element_type=jnp.float32)
            sf = lax.dot_general(q, fresh_key_ref[:, cols], nt, preferred_element_type=jnp.float32)
            s = (s.reshape(chunk // PAIR, PAIR, -1) + bias[None]).reshape(chunk, -1)
            sf = (sf.reshape(chunk // PAIR, PAIR, -1) + fresh_bias[None]).reshape(chunk, -1)
            return s, sf

        following = score(0)
        for h in range(heads):
            cols = slice(h * HEAD, (h + 1) * HEAD)
            s, sf = following
            if h + 1 < heads:
                following = score(h + 1)
            high = jnp.maximum(jnp.max(s, axis=1, keepdims=True), jnp.max(sf, axis=1, keepdims=True))
            w = jnp.exp2((s - high) * SCALE).astype(jnp.bfloat16)
            wf = jnp.exp2((sf - high) * SCALE).astype(jnp.bfloat16)
            value = jnp.concatenate([block_of(value_refs, h), ones], axis=1)
            fresh_value = jnp.concatenate([fresh_value_ref[:, cols], ones[:fresh_value_ref.shape[0]]], axis=1)
            o = jnp.dot(w, value, preferred_element_type=jnp.float32)
            o += jnp.dot(wf, fresh_value, preferred_element_type=jnp.float32)
            total = o[:, HEAD:]
            o = o[:, :HEAD] * (1.0 / total)
            for ref, to, start, count in stores:
                ref[pl.ds(to, count), cols] = o[start:start + count].astype(ref.dtype)
            highs = jnp.where(lane == h, high, highs)
            totals = jnp.where(lane == h, total, totals)
        stats = pack_stats(highs, totals)
        for ref, to, start, count in stores:
            ref[pl.ds(to, count), width:] = stats[start:start + count].astype(ref.dtype)

    if 2 * half <= 128:
        attend_rows(0, 2 * half, [(keep_ref, 0, 0, half), (send_ref, 0, half, half)])
    else:
        for ref, base in ((keep_ref, 0), (send_ref, half)):
            @pl.loop(0, half // 128)
            def _(i, ref=ref, base=base):
                to = pl.multiple_of(i * 128, 128)
                attend_rows(base + to, 128, [(ref, to, 0, 128)])


def attend(slots, target, bias, fresh_bias, fresh_key, fresh_value, sorted_parts, gathered):
    tokens, width = sorted_parts[0].shape[0], fresh_key.shape[1]
    rows = target.shape[1] * SLOT // slots
    shape = (rows // 2, width + LANES)
    return pl.pallas_call(
        attend_kernel,
        out_shape=(jax.ShapeDtypeStruct(shape, jnp.float32), jax.ShapeDtypeStruct(shape, jnp.bfloat16)),
        in_specs=[VMEM] * (5 + len(sorted_parts) + len(gathered)),
        out_specs=(VMEM, VMEM),
        compiler_params=pltpu.CompilerParams(vmem_limit_bytes=24 << 20),
        cost_estimate=pl.CostEstimate(
            flops=4 * rows * tokens * width, bytes_accessed=4 * tokens * width,
            transcendentals=rows * tokens * width // HEAD,
        ),
        name="attend",
    )(target, bias, fresh_bias, fresh_key, fresh_value, *sorted_parts, *gathered)


def merged(parts):
    width = parts[0].shape[1] - LANES
    stats = [unpack_stats(part[:, width:].astype(jnp.float32)) for part in parts]
    top = stats[0][0]
    for high, _ in stats[1:]:
        top = jnp.maximum(top, high)
    weights = [total * jnp.exp2((high - top) * SCALE) for high, total in stats]
    total = weights[0]
    for w in weights[1:]:
        total = total + w
    used = lax.broadcasted_iota(jnp.int32, total.shape, 1) < width // HEAD
    share = 1.0 / jnp.where(used, total, 1.0)
    weights = [w * share for w in weights]
    for h in range(width // HEAD):
        cols = slice(h * HEAD, (h + 1) * HEAD)
        o = parts[0][:, cols].astype(jnp.float32) * weights[0][:, h:h + 1]
        for part, w in zip(parts[1:], weights[1:]):
            o = o + part[:, cols].astype(jnp.float32) * w[:, h:h + 1]
        yield cols, o
    yield slice(width, width + LANES), pack_stats(jnp.where(used, top, 0.0), jnp.where(used, total, 0.0))


def merge_cores_kernel(keep_ref, other_ref, out_ref):
    for cols, o in merged([keep_ref, other_ref]):
        out_ref[:, :, cols] = o.reshape(o.shape[0] // PAIR, PAIR, -1).astype(jnp.bfloat16)


def merge_chips_kernel(parts_ref, out_ref):
    width = out_ref.shape[2]
    for cols, o in merged([parts_ref.at[n] for n in range(parts_ref.shape[0])]):
        if cols.start < width:
            for s in range(STEPS):
                out_ref[s, :, cols] = o[s * SLOT:(s + 1) * SLOT].astype(jnp.bfloat16)


def merge(kernel, parts, shape, name):
    return pl.pallas_call(
        kernel,
        out_shape=jax.ShapeDtypeStruct(shape, jnp.bfloat16),
        in_specs=[VMEM] * len(parts),
        out_specs=VMEM,
        compiler_params=pltpu.CompilerParams(vmem_limit_bytes=16 << 20),
        name=name,
    )(*parts)


def body(cache_kv, fresh_qkv, list_rows, counts):
    device_count = lax.axis_size("blk")
    me = lax.axis_index("blk")
    slot_count = list_rows.shape[1]
    bits = device_count.bit_length() - 1
    width = cache_kv.shape[2]

    def swap(x, *masks):
        return lax.ppermute(x, "blk", [(i, i ^ masks[i % len(masks)]) for i in range(device_count)])

    fresh = fresh_qkv.transpose(1, 2, 0, 3)
    mine, fresh_key, fresh_value = (fresh[:, i] for i in range(3))
    most = width * 2 // 3
    early = sort_cache(cache_kv, 0, most, None, "sort_first")
    column = mine
    steps = [(1 << m, 1 << n) for m, n in zip(*exchange_order(bits))]
    for e, masks in enumerate(steps[:-2]):
        other = swap(column, *masks)
        if e == 0:
            other, early, counts, list_rows = lax.optimization_barrier((other, early, counts, list_rows))
        column = jnp.concatenate([column, other])
    table = jnp.concatenate([counts, list_rows, jnp.full((STEPS, 1), me, jnp.int32)], axis=1)
    late = sort_cache(cache_kv, most, width - most, (table, fresh_key, fresh_value), "sort_second")
    both = [m | n for m, n in zip(*steps[-2:])]
    others = [swap(column, *masks) for masks in (*steps[-2:], both)]
    others, column, late = lax.optimization_barrier((others, column, late))
    beside = swap(column, 1)
    others = jnp.concatenate(others)
    gathered = [column, others, beside, swap(others, 1)]
    key, value, fresh_key, fresh_value, target, bias, fresh_bias = late
    keep, send = attend(slot_count, target, bias, fresh_bias, fresh_key, fresh_value, [*early, key, value], gathered)
    chips = device_count // 2
    parts = merge(merge_cores_kernel, [keep, swap(send, 1)], (chips, PAIR, width + LANES), "merge_cores")
    groups = [[chip * 2 + core for chip in range(chips)] for core in range(2)]
    parts = lax.all_to_all(parts, "blk", split_axis=0, concat_axis=0, axis_index_groups=groups, tiled=True)
    return merge(merge_chips_kernel, [parts], (STEPS, SLOT, width), "merge_chips")


def solution(mesh):
    in_specs = (
        P(("groups", "blk"), None, None),
        P(None, ("groups", "blk"), None, None),
        P(None, ("groups", "blk")),
        P(None, "groups"),
    )
    out_specs = P(None, ("groups", "blk"), None)
    return jax.shard_map(body, mesh=mesh, in_specs=in_specs, out_specs=out_specs, check_vma=False)
```

```python
import jax
import jax.numpy as jnp
from jax import lax
from jax.experimental import pallas as pl
from jax.experimental.pallas import tpu as pltpu
from jax.sharding import PartitionSpec as P

HEAD = 128
SLOT = 4
STEPS = 2
PAIR = STEPS * SLOT
LOG2E = 1.4426950408889634
SCALE = HEAD ** -0.5 * LOG2E
FAR = -1e30
LANES = 128
PART = 16
SLOT_BITS = 2
WAITS = 4
SORT_VMEM = (46, 38)
VMEM = pl.BlockSpec(memory_space=pltpu.VMEM)
SMEM = pl.BlockSpec(memory_space=pltpu.SMEM)
HBM = pl.BlockSpec(memory_space=pltpu.HBM)


def exchange_order(bits):
    first = list(range(bits - 1, 0, -1))
    return first, first[:-3] + [first[-2], first[-1], first[-3]]


def place_of(dev, me, bits):
    mask = dev ^ me
    first, second = exchange_order(bits)
    places = [sum(((mask >> n) & 1) << e for e, n in enumerate(order)) for order in (first, second)]
    return jnp.where((dev & 1) == 1, places[1], places[0]) + ((mask & 1) << (bits - 1))


def plan_kernel_part(table_ref, slots, target_ref, bias_ref, fresh_bias_ref):
    device_count = table_ref.shape[1] - slots - 1
    bits = device_count.bit_length() - 1
    me = table_ref[0, device_count + slots]
    col = lax.broadcasted_iota(jnp.int32, target_ref.shape, 1)

    def one_device(dev, carry):
        start0, start1, target = carry
        count0, count1 = table_ref[0, dev], table_ref[1, dev]
        local = col - place_of(dev, me, bits) * (STEPS * slots)
        slot, step = local >> 1, local & 1
        rank = slot + jnp.where(step == 0, start0, start1)
        home = rank >> SLOT_BITS
        home = ((home ^ me) & 1) * (device_count // 2) + (home >> 1)
        row = home * PAIR + step * SLOT + (rank & (SLOT - 1))
        good = (local >= 0) & (slot < jnp.where(step == 0, count0, count1))
        return start0 + count0, start1 + count1, jnp.where(good, row, target)

    carry = (jnp.int32(0), jnp.int32(0), jnp.full(target_ref.shape, -1, jnp.int32))
    if device_count <= 16:
        for dev in range(device_count):
            carry = one_device(dev, carry)
    else:
        carry = lax.fori_loop(0, device_count, one_device, carry)
    target_ref[...] = carry[2]

    live0 = [i < table_ref[0, me] for i in range(slots)]
    live1 = [i < table_ref[1, me] for i in range(slots)]
    row0 = [jnp.where(live0[i], table_ref[0, device_count + i], -1) for i in range(slots)]
    row1 = [jnp.where(live1[i], table_ref[1, device_count + i], -2) for i in range(slots)]
    token = lax.broadcasted_iota(jnp.int32, bias_ref.shape, 1)
    second = lax.broadcasted_iota(jnp.int32, bias_ref.shape, 0) >= SLOT
    gone = token == row0[0]
    for i in range(1, slots):
        gone = gone | (token == row0[i])
    later = token == row1[0]
    for i in range(1, slots):
        later = later | (token == row1[i])
    bias_ref[...] = jnp.where(gone | (second & later), FAR, 0.0)
    col = lax.broadcasted_iota(jnp.int32, fresh_bias_ref.shape, 1)
    second = (lax.broadcasted_iota(jnp.int32, fresh_bias_ref.shape, 0) >= SLOT).astype(jnp.int32)
    seen = jnp.zeros(fresh_bias_ref.shape, jnp.int32)
    for i in range(slots):
        again = row1[0] == row0[i]
        for j in range(1, slots):
            again = again | (row1[j] == row0[i])
        kept = (live0[i] & jnp.logical_not(again)).astype(jnp.int32)
        early = jnp.where(second == 1, kept, live0[i].astype(jnp.int32))
        seen = jnp.where(col == 2 * i, early, seen)
        seen = jnp.where(col == 2 * i + 1, second * live1[i].astype(jnp.int32), seen)
    fresh_bias_ref[...] = jnp.where(seen == 1, 0.0, FAR)


def sort_kernel(first, planned, *refs):
    refs = list(refs)
    table_ref = refs.pop(0) if planned else None
    cache_ref = refs.pop(0)
    new_refs = [refs.pop(0) for _ in range(2)] if planned else []
    key_ref, value_ref, *small_refs, held, sems = refs
    tokens, width = key_ref.shape
    block = min(128, tokens)
    blocks = tokens // block

    def fetch(i):
        part = pl.ds(i * block, block)
        return pltpu.make_async_copy(
            cache_ref.at[part, :, pl.ds(first, width)], held.at[part, :, pl.ds(0, width)], sems.at[i]
        )

    for i in range(blocks):
        fetch(i).start()
    if planned:
        slots = new_refs[0].shape[0]
        for ref, new_ref in zip(small_refs[:2], new_refs):
            ref[...] = jnp.zeros_like(ref)
            ref[0:STEPS * slots, :] = new_ref.reshape(STEPS * slots, ref.shape[1])[...]
        plan_kernel_part(table_ref, slots, *small_refs[2:])
    out = lax.broadcasted_iota(jnp.int32, (2 * block, 2 * block), 0)
    src = lax.broadcasted_iota(jnp.int32, (2 * block, 2 * block), 1)
    order = (src == jnp.where(out < block, 2 * out, 2 * (out - block) + 1)).astype(jnp.bfloat16)
    pairs = held.reshape(2 * tokens, held.shape[2])
    for i in range(blocks):
        if i % WAITS == 0:
            for j in range(i, min(i + WAITS, blocks)):
                fetch(j).wait()
        rows = slice(i * block, (i + 1) * block)
        for c in range(0, width, 256):
            part = pairs[2 * i * block:2 * (i + 1) * block, c:c + 256]
            part = jnp.dot(order, part, preferred_element_type=jnp.float32).astype(jnp.bfloat16)
            key_ref[rows, c:c + 256] = part[:block]
            value_ref[rows, c:c + 256] = part[block:]


def sort_cache(cache, first, width, plan, name):
    tokens, _, full = cache.shape
    f32, bf16 = jnp.float32, jnp.bfloat16
    shapes = [jax.ShapeDtypeStruct((tokens, width), bf16)] * 2
    inputs, specs = [cache], [HBM]
    if plan:
        table, fresh_key, fresh_value = plan
        slots = fresh_key.shape[0]
        device_count = table.shape[1] - slots - 1
        fresh_rows = -(-STEPS * slots // 16) * 16
        shapes += [jax.ShapeDtypeStruct((fresh_rows, full), bf16)] * 2
        shapes += [
            jax.ShapeDtypeStruct((1, device_count * STEPS * slots), jnp.int32),
            jax.ShapeDtypeStruct((PAIR, tokens), f32),
            jax.ShapeDtypeStruct((PAIR, fresh_rows), f32),
        ]
        inputs, specs = [table, cache, fresh_key, fresh_value], [SMEM, HBM, VMEM, VMEM]

    def kernel(*refs):
        sort_kernel(first, bool(plan), *refs)

    blocks = tokens // min(128, tokens)
    return pl.pallas_call(
        kernel,
        out_shape=tuple(shapes),
        in_specs=specs,
        out_specs=(VMEM,) * len(shapes),
        scratch_shapes=[
            pltpu.VMEM((tokens, 2, width + LANES), bf16),
            pltpu.SemaphoreType.DMA((blocks,)),
        ],
        compiler_params=pltpu.CompilerParams(vmem_limit_bytes=SORT_VMEM[bool(plan)] << 20),
        cost_estimate=pl.CostEstimate(
            flops=8 * 128 * tokens * width, bytes_accessed=8 * tokens * width, transcendentals=0
        ),
        name=name,
    )(*inputs)


def two_parts(x):
    high = x.astype(jnp.bfloat16).astype(jnp.float32)
    return high, x - high


def pack_stats(high, total):
    lane = lax.broadcasted_iota(jnp.int32, high.shape, 1)
    high = jnp.where(lane < PART, high, 0.0)
    total = jnp.where(lane < PART, total, 0.0)
    stats, rest = two_parts(high)
    second, third = two_parts(rest)
    for n, part in enumerate((second, third) + two_parts(total)):
        stats = stats + pltpu.roll(part, PART * (n + 1), 1)
    return stats


def unpack_stats(stats):
    def part(n):
        return pltpu.roll(stats, LANES - PART * n, 1)

    return stats + part(1) + part(2), part(3) + part(4)


def attend_kernel(target_ref, bias_ref, fresh_bias_ref, fresh_key_ref, fresh_value_ref, *rest):
    key_refs, value_refs, gathered_refs, (keep_ref, send_ref) = rest[0:4:2], rest[1:4:2], rest[4:-2], rest[-2:]
    width = fresh_key_ref.shape[1]
    part_heads = key_refs[0].shape[1] // HEAD
    tokens = key_refs[0].shape[0]
    heads = width // HEAD
    half = keep_ref.shape[0]
    nt = (((1,), (1,)), ((), ()))

    def attend_rows(base, chunk, stores):
        row = lax.broadcasted_iota(jnp.int32, (chunk, target_ref.shape[1]), 0)
        pick = (row == target_ref[...] - base).astype(jnp.bfloat16)
        slots = [ref.reshape(ref.shape[0] * STEPS, width)[...].astype(jnp.float32) for ref in gathered_refs]
        slots = jnp.concatenate(slots).astype(jnp.bfloat16)
        queries = jnp.dot(pick, slots, preferred_element_type=jnp.float32).astype(jnp.bfloat16)
        bias = bias_ref[...]
        fresh_bias = fresh_bias_ref[...]
        lane = lax.broadcasted_iota(jnp.int32, (chunk, LANES), 1)
        highs = jnp.zeros((chunk, LANES), jnp.float32)
        totals = jnp.zeros((chunk, LANES), jnp.float32)
        ones = jnp.ones((tokens, LANES), jnp.bfloat16)

        def block_of(refs, h):
            part, at = (0, h) if h < part_heads else (1, h - part_heads)
            return refs[part][:, at * HEAD:(at + 1) * HEAD]

        def score(h):
            cols = slice(h * HEAD, (h + 1) * HEAD)
            q = queries[:, cols]
            s = lax.dot_general(q, block_of(key_refs, h), nt, preferred_element_type=jnp.float32)
            sf = lax.dot_general(q, fresh_key_ref[:, cols], nt, preferred_element_type=jnp.float32)
            s = (s.reshape(chunk // PAIR, PAIR, -1) + bias[None]).reshape(chunk, -1)
            sf = (sf.reshape(chunk // PAIR, PAIR, -1) + fresh_bias[None]).reshape(chunk, -1)
            return s, sf

        following = score(0)
        for h in range(heads):
            cols = slice(h * HEAD, (h + 1) * HEAD)
            s, sf = following
            if h + 1 < heads:
                following = score(h + 1)
            high = jnp.maximum(jnp.max(s, axis=1, keepdims=True), jnp.max(sf, axis=1, keepdims=True))
            w = jnp.exp2((s - high) * SCALE).astype(jnp.bfloat16)
            wf = jnp.exp2((sf - high) * SCALE).astype(jnp.bfloat16)
            value = jnp.concatenate([block_of(value_refs, h), ones], axis=1)
            fresh_value = jnp.concatenate([fresh_value_ref[:, cols], ones[:fresh_value_ref.shape[0]]], axis=1)
            o = jnp.dot(w, value, preferred_element_type=jnp.float32)
            o += jnp.dot(wf, fresh_value, preferred_element_type=jnp.float32)
            total = o[:, HEAD:]
            o = o[:, :HEAD] * (1.0 / total)
            for ref, to, start, count in stores:
                ref[pl.ds(to, count), cols] = o[start:start + count].astype(ref.dtype)
            highs = jnp.where(lane == h, high, highs)
            totals = jnp.where(lane == h, total, totals)
        stats = pack_stats(highs, totals)
        for ref, to, start, count in stores:
            ref[pl.ds(to, count), width:] = stats[start:start + count].astype(ref.dtype)

    if 2 * half <= 128:
        attend_rows(0, 2 * half, [(keep_ref, 0, 0, half), (send_ref, 0, half, half)])
    else:
        for ref, base in ((keep_ref, 0), (send_ref, half)):
            @pl.loop(0, half // 128)
            def _(i, ref=ref, base=base):
                to = pl.multiple_of(i * 128, 128)
                attend_rows(base + to, 128, [(ref, to, 0, 128)])


def attend(slots, target, bias, fresh_bias, fresh_key, fresh_value, sorted_parts, gathered):
    tokens, width = sorted_parts[0].shape[0], fresh_key.shape[1]
    rows = target.shape[1] * SLOT // slots
    shape = (rows // 2, width + LANES)
    return pl.pallas_call(
        attend_kernel,
        out_shape=(jax.ShapeDtypeStruct(shape, jnp.float32), jax.ShapeDtypeStruct(shape, jnp.bfloat16)),
        in_specs=[VMEM] * (5 + len(sorted_parts) + len(gathered)),
        out_specs=(VMEM, VMEM),
        compiler_params=pltpu.CompilerParams(vmem_limit_bytes=24 << 20),
        cost_estimate=pl.CostEstimate(
            flops=4 * rows * tokens * width, bytes_accessed=4 * tokens * width,
            transcendentals=rows * tokens * width // HEAD,
        ),
        name="attend",
    )(target, bias, fresh_bias, fresh_key, fresh_value, *sorted_parts, *gathered)


def merged(parts):
    width = parts[0].shape[1] - LANES
    stats = [unpack_stats(part[:, width:].astype(jnp.float32)) for part in parts]
    top = stats[0][0]
    for high, _ in stats[1:]:
        top = jnp.maximum(top, high)
    weights = [total * jnp.exp2((high - top) * SCALE) for high, total in stats]
    total = weights[0]
    for w in weights[1:]:
        total = total + w
    used = lax.broadcasted_iota(jnp.int32, total.shape, 1) < width // HEAD
    share = 1.0 / jnp.where(used, total, 1.0)
    weights = [w * share for w in weights]
    for h in range(width // HEAD):
        cols = slice(h * HEAD, (h + 1) * HEAD)
        o = parts[0][:, cols].astype(jnp.float32) * weights[0][:, h:h + 1]
        for part, w in zip(parts[1:], weights[1:]):
            o = o + part[:, cols].astype(jnp.float32) * w[:, h:h + 1]
        yield cols, o
    yield slice(width, width + LANES), pack_stats(jnp.where(used, top, 0.0), jnp.where(used, total, 0.0))


def merge_cores_kernel(keep_ref, other_ref, out_ref):
    for cols, o in merged([keep_ref, other_ref]):
        out_ref[:, :, cols] = o.reshape(o.shape[0] // PAIR, PAIR, -1).astype(jnp.bfloat16)


def merge_chips_kernel(parts_ref, out_ref):
    width = out_ref.shape[2]
    for cols, o in merged([parts_ref.at[n] for n in range(parts_ref.shape[0])]):
        if cols.start < width:
            for s in range(STEPS):
                out_ref[s, :, cols] = o[s * SLOT:(s + 1) * SLOT].astype(jnp.bfloat16)


def merge(kernel, parts, shape, name):
    return pl.pallas_call(
        kernel,
        out_shape=jax.ShapeDtypeStruct(shape, jnp.bfloat16),
        in_specs=[VMEM] * len(parts),
        out_specs=VMEM,
        compiler_params=pltpu.CompilerParams(vmem_limit_bytes=16 << 20),
        name=name,
    )(*parts)


def body(cache_kv, fresh_qkv, list_rows, counts):
    device_count = lax.axis_size("blk")
    me = lax.axis_index("blk")
    slot_count = list_rows.shape[1]
    bits = device_count.bit_length() - 1
    width = cache_kv.shape[2]

    def swap(x, *masks):
        return lax.ppermute(x, "blk", [(i, i ^ masks[i % len(masks)]) for i in range(device_count)])

    fresh = fresh_qkv.transpose(1, 2, 0, 3)
    mine, fresh_key, fresh_value = (fresh[:, i] for i in range(3))
    most = width * 2 // 3
    early = sort_cache(cache_kv, 0, most, None, "sort_first")
    column = mine
    steps = [(1 << m, 1 << n) for m, n in zip(*exchange_order(bits))]
    for e, masks in enumerate(steps[:-2]):
        other = swap(column, *masks)
        if e == 0:
            other, early, counts, list_rows = lax.optimization_barrier((other, early, counts, list_rows))
        column = jnp.concatenate([column, other])
    table = jnp.concatenate([counts, list_rows, jnp.full((STEPS, 1), me, jnp.int32)], axis=1)
    late = sort_cache(cache_kv, most, width - most, (table, fresh_key, fresh_value), "sort_second")
    both = [m | n for m, n in zip(*steps[-2:])]
    others = [swap(column, *masks) for masks in (*steps[-2:], both)]
    others, column, late = lax.optimization_barrier((others, column, late))
    beside = swap(column, 1)
    others = jnp.concatenate(others)
    gathered = [column, others, beside, swap(others, 1)]
    key, value, fresh_key, fresh_value, target, bias, fresh_bias = late
    keep, send = attend(slot_count, target, bias, fresh_bias, fresh_key, fresh_value, [*early, key, value], gathered)
    chips = device_count // 2
    parts = merge(merge_cores_kernel, [keep, swap(send, 1)], (chips, PAIR, width + LANES), "merge_cores")
    groups = [[chip * 2 + core for chip in range(chips)] for core in range(2)]
    parts = lax.all_to_all(parts, "blk", split_axis=0, concat_axis=0, axis_index_groups=groups, tiled=True)
    return merge(merge_chips_kernel, [parts], (STEPS, SLOT, width), "merge_chips")


def solution(mesh):
    in_specs = (
        P(("groups", "blk"), None, None),
        P(None, ("groups", "blk"), None, None),
        P(None, ("groups", "blk")),
        P(None, "groups"),
    )
    out_specs = P(None, ("groups", "blk"), None)
    return jax.shard_map(body, mesh=mesh, in_specs=in_specs, out_specs=out_specs, check_vma=False)
```

```python
import jax
import jax.numpy as jnp
from jax import lax
from jax.experimental import pallas as pl
from jax.experimental.pallas import tpu as pltpu
from jax.sharding import PartitionSpec as P

HEAD = 128
SLOT = 4
STEPS = 2
PAIR = STEPS * SLOT
LOG2E = 1.4426950408889634
SCALE = HEAD ** -0.5 * LOG2E
FAR = -1e30
LANES = 128
PART = 16
SLOT_BITS = 2
WAITS = 4
SORT_VMEM = 48
VMEM = pl.BlockSpec(memory_space=pltpu.VMEM)
SMEM = pl.BlockSpec(memory_space=pltpu.SMEM)
HBM = pl.BlockSpec(memory_space=pltpu.HBM)


def exchange_order(bits):
    first = list(range(bits - 1, 0, -1))
    return first, first[:-3] + [first[-2], first[-1], first[-3]]


def place_of(dev, me, bits):
    mask = dev ^ me
    first, second = exchange_order(bits)
    places = [sum(((mask >> n) & 1) << e for e, n in enumerate(order)) for order in (first, second)]
    return jnp.where((dev & 1) == 1, places[1], places[0]) + ((mask & 1) << (bits - 1))


def join_kernel(first_ref, second_ref, out_ref):
    count = first_ref.shape[0]
    out_ref[:count] = first_ref[...]
    out_ref[count:] = second_ref[...]


def join(first, second):
    shape = (2 * first.shape[0], *first.shape[1:])
    return pl.pallas_call(
        join_kernel,
        out_shape=jax.ShapeDtypeStruct(shape, first.dtype),
        in_specs=[VMEM, VMEM],
        out_specs=VMEM,
        compiler_params=pltpu.CompilerParams(vmem_limit_bytes=16 << 20),
        name="join",
    )(first, second)


def plan_kernel_part(me_ref, counts_ref, rows_ref, target_ref, bias_ref, fresh_bias_ref):
    device_count, slots = counts_ref.shape[1], rows_ref.shape[1]
    bits = device_count.bit_length() - 1
    me = me_ref[0]
    col = lax.broadcasted_iota(jnp.int32, target_ref.shape, 1)

    def one_device(dev, carry):
        start0, start1, target = carry
        count0, count1 = counts_ref[0, dev], counts_ref[1, dev]
        local = col - place_of(dev, me, bits) * (STEPS * slots)
        slot, step = local >> 1, local & 1
        rank = slot + jnp.where(step == 0, start0, start1)
        home = rank >> SLOT_BITS
        home = ((home ^ me) & 1) * (device_count // 2) + (home >> 1)
        row = home * PAIR + step * SLOT + (rank & (SLOT - 1))
        good = (local >= 0) & (slot < jnp.where(step == 0, count0, count1))
        return start0 + count0, start1 + count1, jnp.where(good, row, target)

    carry = (jnp.int32(0), jnp.int32(0), jnp.full(target_ref.shape, -1, jnp.int32))
    if device_count <= 16:
        for dev in range(device_count):
            carry = one_device(dev, carry)
    else:
        carry = lax.fori_loop(0, device_count, one_device, carry)
    target_ref[...] = carry[2]

    live0 = [i < counts_ref[0, me] for i in range(slots)]
    live1 = [i < counts_ref[1, me] for i in range(slots)]
    row0 = [jnp.where(live0[i], rows_ref[0, i], -1) for i in range(slots)]
    row1 = [jnp.where(live1[i], rows_ref[1, i], -2) for i in range(slots)]
    token = lax.broadcasted_iota(jnp.int32, bias_ref.shape, 1)
    second = lax.broadcasted_iota(jnp.int32, bias_ref.shape, 0) >= SLOT
    gone = token == row0[0]
    for i in range(1, slots):
        gone = gone | (token == row0[i])
    later = token == row1[0]
    for i in range(1, slots):
        later = later | (token == row1[i])
    bias_ref[...] = jnp.where(gone | (second & later), FAR, 0.0)
    col = lax.broadcasted_iota(jnp.int32, fresh_bias_ref.shape, 1)
    second = (lax.broadcasted_iota(jnp.int32, fresh_bias_ref.shape, 0) >= SLOT).astype(jnp.int32)
    seen = jnp.zeros(fresh_bias_ref.shape, jnp.int32)
    for i in range(slots):
        again = row1[0] == row0[i]
        for j in range(1, slots):
            again = again | (row1[j] == row0[i])
        kept = (live0[i] & jnp.logical_not(again)).astype(jnp.int32)
        early = jnp.where(second == 1, kept, live0[i].astype(jnp.int32))
        seen = jnp.where(col == 2 * i, early, seen)
        seen = jnp.where(col == 2 * i + 1, second * live1[i].astype(jnp.int32), seen)
    fresh_bias_ref[...] = jnp.where(seen == 1, 0.0, FAR)


def sort_kernel(first, planned, *refs):
    refs = list(refs)
    table_refs = [refs.pop(0) for _ in range(3)] if planned else []
    cache_ref = refs.pop(0)
    new_refs = [refs.pop(0) for _ in range(2)] if planned else []
    key_ref, value_ref, *small_refs, held, sems = refs
    tokens, width = key_ref.shape
    block = min(128, tokens)
    blocks = tokens // block

    def fetch(i):
        part = pl.ds(i * block, block)
        return pltpu.make_async_copy(
            cache_ref.at[part, :, pl.ds(first, width)], held.at[part, :, pl.ds(0, width)], sems.at[i]
        )

    for i in range(blocks):
        fetch(i).start()
    if planned:
        slots = new_refs[0].shape[0]
        for ref, new_ref in zip(small_refs[:2], new_refs):
            ref[...] = jnp.zeros_like(ref)
            ref[0:STEPS * slots, :] = new_ref.reshape(STEPS * slots, ref.shape[1])[...]
        plan_kernel_part(*table_refs, *small_refs[2:])
    out = lax.broadcasted_iota(jnp.int32, (2 * block, 2 * block), 0)
    src = lax.broadcasted_iota(jnp.int32, (2 * block, 2 * block), 1)
    order = (src == jnp.where(out < block, 2 * out, 2 * (out - block) + 1)).astype(jnp.bfloat16)
    pairs = held.reshape(2 * tokens, held.shape[2])
    for i in range(blocks):
        if i % WAITS == 0:
            for j in range(i, min(i + WAITS, blocks)):
                fetch(j).wait()
        rows = slice(i * block, (i + 1) * block)
        for c in range(0, width, 256):
            part = pairs[2 * i * block:2 * (i + 1) * block, c:c + 256]
            part = jnp.dot(order, part, preferred_element_type=jnp.float32).astype(jnp.bfloat16)
            key_ref[rows, c:c + 256] = part[:block]
            value_ref[rows, c:c + 256] = part[block:]


def sort_cache(cache, first, width, plan, name):
    tokens, _, full = cache.shape
    f32, bf16 = jnp.float32, jnp.bfloat16
    shapes = [jax.ShapeDtypeStruct((tokens, width), bf16)] * 2
    inputs, specs = [cache], [HBM]
    if plan:
        tables, fresh_key, fresh_value = plan
        slots = fresh_key.shape[0]
        device_count = tables[1].shape[1]
        fresh_rows = -(-STEPS * slots // 16) * 16
        shapes += [jax.ShapeDtypeStruct((fresh_rows, full), bf16)] * 2
        shapes += [
            jax.ShapeDtypeStruct((1, device_count * STEPS * slots), jnp.int32),
            jax.ShapeDtypeStruct((PAIR, tokens), f32),
            jax.ShapeDtypeStruct((PAIR, fresh_rows), f32),
        ]
        inputs = [*tables, cache, fresh_key, fresh_value]
        specs = [SMEM, SMEM, SMEM, HBM, VMEM, VMEM]

    def kernel(*refs):
        sort_kernel(first, bool(plan), *refs)

    blocks = tokens // min(128, tokens)
    return pl.pallas_call(
        kernel,
        out_shape=tuple(shapes),
        in_specs=specs,
        out_specs=(VMEM,) * len(shapes),
        scratch_shapes=[
            pltpu.VMEM((tokens, 2, width + LANES), bf16),
            pltpu.SemaphoreType.DMA((blocks,)),
        ],
        compiler_params=pltpu.CompilerParams(vmem_limit_bytes=SORT_VMEM << 20),
        cost_estimate=pl.CostEstimate(
            flops=8 * 128 * tokens * width, bytes_accessed=8 * tokens * width, transcendentals=0
        ),
        name=name,
    )(*inputs)


def two_parts(x):
    high = x.astype(jnp.bfloat16).astype(jnp.float32)
    return high, x - high


def pack_stats(high, total):
    lane = lax.broadcasted_iota(jnp.int32, high.shape, 1)
    high = jnp.where(lane < PART, high, 0.0)
    total = jnp.where(lane < PART, total, 0.0)
    stats, rest = two_parts(high)
    second, third = two_parts(rest)
    for n, part in enumerate((second, third) + two_parts(total)):
        stats = stats + pltpu.roll(part, PART * (n + 1), 1)
    return stats


def unpack_stats(stats):
    def part(n):
        return pltpu.roll(stats, LANES - PART * n, 1)

    return stats + part(1) + part(2), part(3) + part(4)


def attend_kernel(target_ref, bias_ref, fresh_bias_ref, fresh_key_ref, fresh_value_ref, *rest):
    key_refs, value_refs, gathered_refs, (keep_ref, send_ref) = rest[0:4:2], rest[1:4:2], rest[4:-2], rest[-2:]
    width = fresh_key_ref.shape[1]
    part_heads = key_refs[0].shape[1] // HEAD
    tokens = key_refs[0].shape[0]
    heads = width // HEAD
    half = keep_ref.shape[0]
    nt = (((1,), (1,)), ((), ()))

    def attend_rows(base, chunk, stores):
        row = lax.broadcasted_iota(jnp.int32, (chunk, target_ref.shape[1]), 0)
        pick = (row == target_ref[...] - base).astype(jnp.bfloat16)
        slots = [ref.reshape(ref.shape[0] * STEPS, width)[...].astype(jnp.float32) for ref in gathered_refs]
        slots = jnp.concatenate(slots).astype(jnp.bfloat16)
        queries = jnp.dot(pick, slots, preferred_element_type=jnp.float32).astype(jnp.bfloat16)
        bias = bias_ref[...]
        fresh_bias = fresh_bias_ref[...]
        lane = lax.broadcasted_iota(jnp.int32, (chunk, LANES), 1)
        highs = jnp.zeros((chunk, LANES), jnp.float32)
        totals = jnp.zeros((chunk, LANES), jnp.float32)
        ones = jnp.ones((tokens, LANES), jnp.bfloat16)

        def block_of(refs, h):
            part, at = (0, h) if h < part_heads else (1, h - part_heads)
            return refs[part][:, at * HEAD:(at + 1) * HEAD]

        def score(h):
            cols = slice(h * HEAD, (h + 1) * HEAD)
            q = queries[:, cols]
            s = lax.dot_general(q, block_of(key_refs, h), nt, preferred_element_type=jnp.float32)
            sf = lax.dot_general(q, fresh_key_ref[:, cols], nt, preferred_element_type=jnp.float32)
            s = (s.reshape(chunk // PAIR, PAIR, -1) + bias[None]).reshape(chunk, -1)
            sf = (sf.reshape(chunk // PAIR, PAIR, -1) + fresh_bias[None]).reshape(chunk, -1)
            return s, sf

        following = score(0)
        for h in range(heads):
            cols = slice(h * HEAD, (h + 1) * HEAD)
            s, sf = following
            if h + 1 < heads:
                following = score(h + 1)
            high = jnp.maximum(jnp.max(s, axis=1, keepdims=True), jnp.max(sf, axis=1, keepdims=True))
            w = jnp.exp2((s - high) * SCALE).astype(jnp.bfloat16)
            wf = jnp.exp2((sf - high) * SCALE).astype(jnp.bfloat16)
            value = jnp.concatenate([block_of(value_refs, h), ones], axis=1)
            fresh_value = jnp.concatenate([fresh_value_ref[:, cols], ones[:fresh_value_ref.shape[0]]], axis=1)
            o = jnp.dot(w, value, preferred_element_type=jnp.float32)
            o += jnp.dot(wf, fresh_value, preferred_element_type=jnp.float32)
            total = o[:, HEAD:]
            o = o[:, :HEAD] * (1.0 / total)
            for ref, to, start, count in stores:
                ref[pl.ds(to, count), cols] = o[start:start + count].astype(ref.dtype)
            highs = jnp.where(lane == h, high, highs)
            totals = jnp.where(lane == h, total, totals)
        stats = pack_stats(highs, totals)
        for ref, to, start, count in stores:
            ref[pl.ds(to, count), width:] = stats[start:start + count].astype(ref.dtype)

    if 2 * half <= 128:
        attend_rows(0, 2 * half, [(keep_ref, 0, 0, half), (send_ref, 0, half, half)])
    else:
        for ref, base in ((keep_ref, 0), (send_ref, half)):
            @pl.loop(0, half // 128)
            def _(i, ref=ref, base=base):
                to = pl.multiple_of(i * 128, 128)
                attend_rows(base + to, 128, [(ref, to, 0, 128)])


def attend(slots, target, bias, fresh_bias, fresh_key, fresh_value, sorted_parts, gathered):
    tokens, width = sorted_parts[0].shape[0], fresh_key.shape[1]
    rows = target.shape[1] * SLOT // slots
    shape = (rows // 2, width + LANES)
    return pl.pallas_call(
        attend_kernel,
        out_shape=(jax.ShapeDtypeStruct(shape, jnp.float32), jax.ShapeDtypeStruct(shape, jnp.bfloat16)),
        in_specs=[VMEM] * (5 + len(sorted_parts) + len(gathered)),
        out_specs=(VMEM, VMEM),
        compiler_params=pltpu.CompilerParams(vmem_limit_bytes=24 << 20),
        cost_estimate=pl.CostEstimate(
            flops=4 * rows * tokens * width, bytes_accessed=4 * tokens * width,
            transcendentals=rows * tokens * width // HEAD,
        ),
        name="attend",
    )(target, bias, fresh_bias, fresh_key, fresh_value, *sorted_parts, *gathered)


def merged(parts):
    width = parts[0].shape[1] - LANES
    stats = [unpack_stats(part[:, width:].astype(jnp.float32)) for part in parts]
    top = stats[0][0]
    for high, _ in stats[1:]:
        top = jnp.maximum(top, high)
    weights = [total * jnp.exp2((high - top) * SCALE) for high, total in stats]
    total = weights[0]
    for w in weights[1:]:
        total = total + w
    used = lax.broadcasted_iota(jnp.int32, total.shape, 1) < width // HEAD
    share = 1.0 / jnp.where(used, total, 1.0)
    weights = [w * share for w in weights]
    for h in range(width // HEAD):
        cols = slice(h * HEAD, (h + 1) * HEAD)
        o = parts[0][:, cols].astype(jnp.float32) * weights[0][:, h:h + 1]
        for part, w in zip(parts[1:], weights[1:]):
            o = o + part[:, cols].astype(jnp.float32) * w[:, h:h + 1]
        yield cols, o
    yield slice(width, width + LANES), pack_stats(jnp.where(used, top, 0.0), jnp.where(used, total, 0.0))


def merge_cores_kernel(keep_ref, other_ref, out_ref):
    for cols, o in merged([keep_ref, other_ref]):
        out_ref[:, :, cols] = o.reshape(o.shape[0] // PAIR, PAIR, -1).astype(jnp.bfloat16)


def merge_chips_kernel(parts_ref, out_ref):
    width = out_ref.shape[2]
    for cols, o in merged([parts_ref.at[n] for n in range(parts_ref.shape[0])]):
        if cols.start < width:
            for s in range(STEPS):
                out_ref[s, :, cols] = o[s * SLOT:(s + 1) * SLOT].astype(jnp.bfloat16)


def merge(kernel, parts, shape, name):
    return pl.pallas_call(
        kernel,
        out_shape=jax.ShapeDtypeStruct(shape, jnp.bfloat16),
        in_specs=[VMEM] * len(parts),
        out_specs=VMEM,
        compiler_params=pltpu.CompilerParams(vmem_limit_bytes=16 << 20),
        name=name,
    )(*parts)


def body(cache_kv, fresh_qkv, list_rows, counts):
    device_count = lax.axis_size("blk")
    me = lax.axis_index("blk")
    slot_count = list_rows.shape[1]
    bits = device_count.bit_length() - 1
    width = cache_kv.shape[2]

    def swap(x, *masks):
        return lax.ppermute(x, "blk", [(i, i ^ masks[i % len(masks)]) for i in range(device_count)])

    fresh = fresh_qkv.transpose(1, 2, 0, 3)
    mine, fresh_key, fresh_value = (fresh[:, i] for i in range(3))
    most = width * 2 // 3
    early = sort_cache(cache_kv, 0, most, None, "sort_first")
    column = mine
    steps = [(1 << m, 1 << n) for m, n in zip(*exchange_order(bits))]
    for e, masks in enumerate(steps[:-2]):
        other = swap(column, *masks)
        if e == 0:
            other, early, counts, list_rows = lax.optimization_barrier((other, early, counts, list_rows))
        column = join(column, other)
    tables = (me.reshape(1), counts, list_rows)
    late = sort_cache(cache_kv, most, width - most, (tables, fresh_key, fresh_value), "sort_second")
    both = [m | n for m, n in zip(*steps[-2:])]
    others = [swap(column, *masks) for masks in (*steps[-2:], both)]
    others, column, late = lax.optimization_barrier((others, column, late))
    beside = swap(column, 1)
    others = jnp.concatenate(others)
    gathered = [column, others, beside, swap(others, 1)]
    key, value, fresh_key, fresh_value, target, bias, fresh_bias = late
    keep, send = attend(slot_count, target, bias, fresh_bias, fresh_key, fresh_value, [*early, key, value], gathered)
    chips = device_count // 2
    parts = merge(merge_cores_kernel, [keep, swap(send, 1)], (chips, PAIR, width + LANES), "merge_cores")
    groups = [[chip * 2 + core for chip in range(chips)] for core in range(2)]
    parts = lax.all_to_all(parts, "blk", split_axis=0, concat_axis=0, axis_index_groups=groups, tiled=True)
    return merge(merge_chips_kernel, [parts], (STEPS, SLOT, width), "merge_chips")


def solution(mesh):
    in_specs = (
        P(("groups", "blk"), None, None),
        P(None, ("groups", "blk"), None, None),
        P(None, ("groups", "blk")),
        P(None, "groups"),
    )
    out_specs = P(None, ("groups", "blk"), None)
    return jax.shard_map(body, mesh=mesh, in_specs=in_specs, out_specs=out_specs, check_vma=False)
```

```python
import jax
import jax.numpy as jnp
from jax import lax
from jax.experimental import pallas as pl
from jax.experimental.pallas import tpu as pltpu
from jax.sharding import PartitionSpec as P

HEAD = 128
SLOT = 4
STEPS = 2
PAIR = STEPS * SLOT
LOG2E = 1.4426950408889634
SCALE = HEAD ** -0.5 * LOG2E
FAR = -1e30
LANES = 128
PART = 16
SLOT_BITS = 2
WAITS = 4
SORT_VMEM = 48
VMEM = pl.BlockSpec(memory_space=pltpu.VMEM)
SMEM = pl.BlockSpec(memory_space=pltpu.SMEM)
HBM = pl.BlockSpec(memory_space=pltpu.HBM)


def exchange_order(bits):
    first = list(range(bits - 1, 0, -1))
    return first, first[:-3] + [first[-2], first[-1], first[-3]]


def place_of(dev, me, bits):
    mask = dev ^ me
    first, second = exchange_order(bits)
    places = [sum(((mask >> n) & 1) << e for e, n in enumerate(order)) for order in (first, second)]
    return jnp.where((dev & 1) == 1, places[1], places[0]) + ((mask & 1) << (bits - 1))


def join_kernel(*refs):
    *part_refs, out_ref = refs
    at = 0
    for ref in part_refs:
        out_ref[at:at + ref.shape[0]] = ref[...]
        at += ref.shape[0]


def join(*parts):
    shape = (sum(x.shape[0] for x in parts), *parts[0].shape[1:])
    return pl.pallas_call(
        join_kernel,
        out_shape=jax.ShapeDtypeStruct(shape, parts[0].dtype),
        in_specs=[VMEM] * len(parts),
        out_specs=VMEM,
        compiler_params=pltpu.CompilerParams(vmem_limit_bytes=16 << 20),
        name="join",
    )(*parts)


def plan_kernel_part(me_ref, counts_ref, rows_ref, target_ref, bias_ref, fresh_bias_ref):
    device_count, slots = counts_ref.shape[1], rows_ref.shape[1]
    bits = device_count.bit_length() - 1
    me = me_ref[0]
    col = lax.broadcasted_iota(jnp.int32, target_ref.shape, 1)

    def one_device(dev, carry):
        start0, start1, target = carry
        count0, count1 = counts_ref[0, dev], counts_ref[1, dev]
        local = col - place_of(dev, me, bits) * (STEPS * slots)
        slot, step = local >> 1, local & 1
        rank = slot + jnp.where(step == 0, start0, start1)
        home = rank >> SLOT_BITS
        home = ((home ^ me) & 1) * (device_count // 2) + (home >> 1)
        row = home * PAIR + step * SLOT + (rank & (SLOT - 1))
        good = (local >= 0) & (slot < jnp.where(step == 0, count0, count1))
        return start0 + count0, start1 + count1, jnp.where(good, row, target)

    carry = (jnp.int32(0), jnp.int32(0), jnp.full(target_ref.shape, -1, jnp.int32))
    if device_count <= 16:
        for dev in range(device_count):
            carry = one_device(dev, carry)
    else:
        carry = lax.fori_loop(0, device_count, one_device, carry)
    target_ref[...] = carry[2]

    live0 = [i < counts_ref[0, me] for i in range(slots)]
    live1 = [i < counts_ref[1, me] for i in range(slots)]
    row0 = [jnp.where(live0[i], rows_ref[0, i], -1) for i in range(slots)]
    row1 = [jnp.where(live1[i], rows_ref[1, i], -2) for i in range(slots)]
    token = lax.broadcasted_iota(jnp.int32, bias_ref.shape, 1)
    second = lax.broadcasted_iota(jnp.int32, bias_ref.shape, 0) >= SLOT
    gone = token == row0[0]
    for i in range(1, slots):
        gone = gone | (token == row0[i])
    later = token == row1[0]
    for i in range(1, slots):
        later = later | (token == row1[i])
    bias_ref[...] = jnp.where(gone | (second & later), FAR, 0.0)
    col = lax.broadcasted_iota(jnp.int32, fresh_bias_ref.shape, 1)
    second = (lax.broadcasted_iota(jnp.int32, fresh_bias_ref.shape, 0) >= SLOT).astype(jnp.int32)
    seen = jnp.zeros(fresh_bias_ref.shape, jnp.int32)
    for i in range(slots):
        again = row1[0] == row0[i]
        for j in range(1, slots):
            again = again | (row1[j] == row0[i])
        kept = (live0[i] & jnp.logical_not(again)).astype(jnp.int32)
        early = jnp.where(second == 1, kept, live0[i].astype(jnp.int32))
        seen = jnp.where(col == 2 * i, early, seen)
        seen = jnp.where(col == 2 * i + 1, second * live1[i].astype(jnp.int32), seen)
    fresh_bias_ref[...] = jnp.where(seen == 1, 0.0, FAR)


def sort_kernel(first, planned, *refs):
    refs = list(refs)
    table_refs = [refs.pop(0) for _ in range(3)] if planned else []
    cache_ref = refs.pop(0)
    new_refs = [refs.pop(0) for _ in range(2)] if planned else []
    key_ref, value_ref, *small_refs, held, sems = refs
    tokens, width = key_ref.shape
    block = min(128, tokens)
    blocks = tokens // block

    def fetch(i):
        part = pl.ds(i * block, block)
        return pltpu.make_async_copy(
            cache_ref.at[part, :, pl.ds(first, width)], held.at[part, :, pl.ds(0, width)], sems.at[i]
        )

    for i in range(blocks):
        fetch(i).start()
    if planned:
        slots = new_refs[0].shape[0]
        for ref, new_ref in zip(small_refs[:2], new_refs):
            ref[...] = jnp.zeros_like(ref)
            ref[0:STEPS * slots, :] = new_ref.reshape(STEPS * slots, ref.shape[1])[...]
        plan_kernel_part(*table_refs, *small_refs[2:])
    out = lax.broadcasted_iota(jnp.int32, (2 * block, 2 * block), 0)
    src = lax.broadcasted_iota(jnp.int32, (2 * block, 2 * block), 1)
    order = (src == jnp.where(out < block, 2 * out, 2 * (out - block) + 1)).astype(jnp.bfloat16)
    pairs = held.reshape(2 * tokens, held.shape[2])
    for i in range(blocks):
        if i % WAITS == 0:
            for j in range(i, min(i + WAITS, blocks)):
                fetch(j).wait()
        rows = slice(i * block, (i + 1) * block)
        for c in range(0, width, 256):
            part = pairs[2 * i * block:2 * (i + 1) * block, c:c + 256]
            part = jnp.dot(order, part, preferred_element_type=jnp.float32).astype(jnp.bfloat16)
            key_ref[rows, c:c + 256] = part[:block]
            value_ref[rows, c:c + 256] = part[block:]


def sort_cache(cache, first, width, plan, name):
    tokens, _, full = cache.shape
    f32, bf16 = jnp.float32, jnp.bfloat16
    shapes = [jax.ShapeDtypeStruct((tokens, width), bf16)] * 2
    inputs, specs = [cache], [HBM]
    if plan:
        tables, fresh_key, fresh_value = plan
        slots = fresh_key.shape[0]
        device_count = tables[1].shape[1]
        fresh_rows = -(-STEPS * slots // 16) * 16
        shapes += [jax.ShapeDtypeStruct((fresh_rows, full), bf16)] * 2
        shapes += [
            jax.ShapeDtypeStruct((1, device_count * STEPS * slots), jnp.int32),
            jax.ShapeDtypeStruct((PAIR, tokens), f32),
            jax.ShapeDtypeStruct((PAIR, fresh_rows), f32),
        ]
        inputs = [*tables, cache, fresh_key, fresh_value]
        specs = [SMEM, SMEM, SMEM, HBM, VMEM, VMEM]

    def kernel(*refs):
        sort_kernel(first, bool(plan), *refs)

    blocks = tokens // min(128, tokens)
    return pl.pallas_call(
        kernel,
        out_shape=tuple(shapes),
        in_specs=specs,
        out_specs=(VMEM,) * len(shapes),
        scratch_shapes=[
            pltpu.VMEM((tokens, 2, width + LANES), bf16),
            pltpu.SemaphoreType.DMA((blocks,)),
        ],
        compiler_params=pltpu.CompilerParams(vmem_limit_bytes=SORT_VMEM << 20),
        cost_estimate=pl.CostEstimate(
            flops=8 * 128 * tokens * width, bytes_accessed=8 * tokens * width, transcendentals=0
        ),
        name=name,
    )(*inputs)


def two_parts(x):
    high = x.astype(jnp.bfloat16).astype(jnp.float32)
    return high, x - high


def pack_stats(high, total):
    lane = lax.broadcasted_iota(jnp.int32, high.shape, 1)
    high = jnp.where(lane < PART, high, 0.0)
    total = jnp.where(lane < PART, total, 0.0)
    stats, rest = two_parts(high)
    second, third = two_parts(rest)
    for n, part in enumerate((second, third) + two_parts(total)):
        stats = stats + pltpu.roll(part, PART * (n + 1), 1)
    return stats


def unpack_stats(stats):
    def part(n):
        return pltpu.roll(stats, LANES - PART * n, 1)

    return stats + part(1) + part(2), part(3) + part(4)


def attend_kernel(target_ref, bias_ref, fresh_bias_ref, fresh_key_ref, fresh_value_ref, *rest):
    key_refs, value_refs, gathered_refs, (keep_ref, send_ref) = rest[0:4:2], rest[1:4:2], rest[4:-2], rest[-2:]
    width = fresh_key_ref.shape[1]
    part_heads = key_refs[0].shape[1] // HEAD
    tokens = key_refs[0].shape[0]
    heads = width // HEAD
    half = keep_ref.shape[0]
    nt = (((1,), (1,)), ((), ()))

    def attend_rows(base, chunk, stores):
        row = lax.broadcasted_iota(jnp.int32, (chunk, target_ref.shape[1]), 0)
        pick = (row == target_ref[...] - base).astype(jnp.bfloat16)
        slots = [ref.reshape(ref.shape[0] * STEPS, width)[...].astype(jnp.float32) for ref in gathered_refs]
        slots = jnp.concatenate(slots).astype(jnp.bfloat16)
        queries = jnp.dot(pick, slots, preferred_element_type=jnp.float32).astype(jnp.bfloat16)
        bias = bias_ref[...]
        fresh_bias = fresh_bias_ref[...]
        lane = lax.broadcasted_iota(jnp.int32, (chunk, LANES), 1)
        highs = jnp.zeros((chunk, LANES), jnp.float32)
        totals = jnp.zeros((chunk, LANES), jnp.float32)
        ones = jnp.ones((tokens, LANES), jnp.bfloat16)

        def block_of(refs, h):
            part, at = (0, h) if h < part_heads else (1, h - part_heads)
            return refs[part][:, at * HEAD:(at + 1) * HEAD]

        def score(h):
            cols = slice(h * HEAD, (h + 1) * HEAD)
            q = queries[:, cols]
            s = lax.dot_general(q, block_of(key_refs, h), nt, preferred_element_type=jnp.float32)
            sf = lax.dot_general(q, fresh_key_ref[:, cols], nt, preferred_element_type=jnp.float32)
            s = (s.reshape(chunk // PAIR, PAIR, -1) + bias[None]).reshape(chunk, -1)
            sf = (sf.reshape(chunk // PAIR, PAIR, -1) + fresh_bias[None]).reshape(chunk, -1)
            return s, sf

        following = score(0)
        for h in range(heads):
            cols = slice(h * HEAD, (h + 1) * HEAD)
            s, sf = following
            if h + 1 < heads:
                following = score(h + 1)
            high = jnp.maximum(jnp.max(s, axis=1, keepdims=True), jnp.max(sf, axis=1, keepdims=True))
            w = jnp.exp2((s - high) * SCALE).astype(jnp.bfloat16)
            wf = jnp.exp2((sf - high) * SCALE).astype(jnp.bfloat16)
            value = jnp.concatenate([block_of(value_refs, h), ones], axis=1)
            fresh_value = jnp.concatenate([fresh_value_ref[:, cols], ones[:fresh_value_ref.shape[0]]], axis=1)
            o = jnp.dot(w, value, preferred_element_type=jnp.float32)
            o += jnp.dot(wf, fresh_value, preferred_element_type=jnp.float32)
            total = o[:, HEAD:]
            o = o[:, :HEAD] * (1.0 / total)
            for ref, to, start, count in stores:
                ref[pl.ds(to, count), cols] = o[start:start + count].astype(ref.dtype)
            highs = jnp.where(lane == h, high, highs)
            totals = jnp.where(lane == h, total, totals)
        stats = pack_stats(highs, totals)
        for ref, to, start, count in stores:
            ref[pl.ds(to, count), width:] = stats[start:start + count].astype(ref.dtype)

    if 2 * half <= 128:
        attend_rows(0, 2 * half, [(keep_ref, 0, 0, half), (send_ref, 0, half, half)])
    else:
        for ref, base in ((keep_ref, 0), (send_ref, half)):
            @pl.loop(0, half // 128)
            def _(i, ref=ref, base=base):
                to = pl.multiple_of(i * 128, 128)
                attend_rows(base + to, 128, [(ref, to, 0, 128)])


def attend(slots, target, bias, fresh_bias, fresh_key, fresh_value, sorted_parts, gathered):
    tokens, width = sorted_parts[0].shape[0], fresh_key.shape[1]
    rows = target.shape[1] * SLOT // slots
    shape = (rows // 2, width + LANES)
    return pl.pallas_call(
        attend_kernel,
        out_shape=(jax.ShapeDtypeStruct(shape, jnp.float32), jax.ShapeDtypeStruct(shape, jnp.bfloat16)),
        in_specs=[VMEM] * (5 + len(sorted_parts) + len(gathered)),
        out_specs=(VMEM, VMEM),
        compiler_params=pltpu.CompilerParams(vmem_limit_bytes=24 << 20),
        cost_estimate=pl.CostEstimate(
            flops=4 * rows * tokens * width, bytes_accessed=4 * tokens * width,
            transcendentals=rows * tokens * width // HEAD,
        ),
        name="attend",
    )(target, bias, fresh_bias, fresh_key, fresh_value, *sorted_parts, *gathered)


def merged(parts):
    width = parts[0].shape[1] - LANES
    stats = [unpack_stats(part[:, width:].astype(jnp.float32)) for part in parts]
    top = stats[0][0]
    for high, _ in stats[1:]:
        top = jnp.maximum(top, high)
    weights = [total * jnp.exp2((high - top) * SCALE) for high, total in stats]
    total = weights[0]
    for w in weights[1:]:
        total = total + w
    used = lax.broadcasted_iota(jnp.int32, total.shape, 1) < width // HEAD
    share = 1.0 / jnp.where(used, total, 1.0)
    weights = [w * share for w in weights]
    for h in range(width // HEAD):
        cols = slice(h * HEAD, (h + 1) * HEAD)
        o = parts[0][:, cols].astype(jnp.float32) * weights[0][:, h:h + 1]
        for part, w in zip(parts[1:], weights[1:]):
            o = o + part[:, cols].astype(jnp.float32) * w[:, h:h + 1]
        yield cols, o
    yield slice(width, width + LANES), pack_stats(jnp.where(used, top, 0.0), jnp.where(used, total, 0.0))


def merge_cores_kernel(keep_ref, other_ref, out_ref):
    for cols, o in merged([keep_ref, other_ref]):
        out_ref[:, :, cols] = o.reshape(o.shape[0] // PAIR, PAIR, -1).astype(jnp.bfloat16)


def merge_chips_kernel(parts_ref, out_ref):
    width = out_ref.shape[2]
    for cols, o in merged([parts_ref.at[n] for n in range(parts_ref.shape[0])]):
        if cols.start < width:
            for s in range(STEPS):
                out_ref[s, :, cols] = o[s * SLOT:(s + 1) * SLOT].astype(jnp.bfloat16)


def merge(kernel, parts, shape, name):
    return pl.pallas_call(
        kernel,
        out_shape=jax.ShapeDtypeStruct(shape, jnp.bfloat16),
        in_specs=[VMEM] * len(parts),
        out_specs=VMEM,
        compiler_params=pltpu.CompilerParams(vmem_limit_bytes=16 << 20),
        name=name,
    )(*parts)


def body(cache_kv, fresh_qkv, list_rows, counts):
    device_count = lax.axis_size("blk")
    me = lax.axis_index("blk")
    slot_count = list_rows.shape[1]
    bits = device_count.bit_length() - 1
    width = cache_kv.shape[2]

    def swap(x, *masks):
        return lax.ppermute(x, "blk", [(i, i ^ masks[i % len(masks)]) for i in range(device_count)])

    fresh = fresh_qkv.transpose(1, 2, 0, 3)
    mine, fresh_key, fresh_value = (fresh[:, i] for i in range(3))
    most = width // 2
    early = sort_cache(cache_kv, 0, most, None, "sort_first")
    column = mine
    steps = [(1 << m, 1 << n) for m, n in zip(*exchange_order(bits))]
    for e, masks in enumerate(steps[:-2]):
        other = swap(column, *masks)
        if e == 0:
            other, early, counts, list_rows = lax.optimization_barrier((other, early, counts, list_rows))
        column = join(column, other)
    tables = (me.reshape(1), counts, list_rows)
    late = sort_cache(cache_kv, most, width - most, (tables, fresh_key, fresh_value), "sort_second")
    both = [m | n for m, n in zip(*steps[-2:])]
    others = [swap(column, *masks) for masks in (*steps[-2:], both)]
    others, column, late = lax.optimization_barrier((others, column, late))
    beside = swap(column, 1)
    others = join(*others)
    gathered = [column, others, beside, swap(others, 1)]
    key, value, fresh_key, fresh_value, target, bias, fresh_bias = late
    keep, send = attend(slot_count, target, bias, fresh_bias, fresh_key, fresh_value, [*early, key, value], gathered)
    chips = device_count // 2
    parts = merge(merge_cores_kernel, [keep, swap(send, 1)], (chips, PAIR, width + LANES), "merge_cores")
    groups = [[chip * 2 + core for chip in range(chips)] for core in range(2)]
    parts = lax.all_to_all(parts, "blk", split_axis=0, concat_axis=0, axis_index_groups=groups, tiled=True)
    return merge(merge_chips_kernel, [parts], (STEPS, SLOT, width), "merge_chips")


def solution(mesh):
    in_specs = (
        P(("groups", "blk"), None, None),
        P(None, ("groups", "blk"), None, None),
        P(None, ("groups", "blk")),
        P(None, "groups"),
    )
    out_specs = P(None, ("groups", "blk"), None)
    return jax.shard_map(body, mesh=mesh, in_specs=in_specs, out_specs=out_specs, check_vma=False)
```

```python
import jax
import jax.numpy as jnp
from jax import lax
from jax.experimental import pallas as pl
from jax.experimental.pallas import tpu as pltpu
from jax.sharding import PartitionSpec as P

HEAD = 128
SLOT = 4
STEPS = 2
PAIR = STEPS * SLOT
LOG2E = 1.4426950408889634
SCALE = HEAD ** -0.5 * LOG2E
FAR = -1e30
LANES = 128
PART = 16
SLOT_BITS = 2
WAITS = 2
SORT_VMEM = 48
VMEM = pl.BlockSpec(memory_space=pltpu.VMEM)
SMEM = pl.BlockSpec(memory_space=pltpu.SMEM)
HBM = pl.BlockSpec(memory_space=pltpu.HBM)


def exchange_order(bits):
    first = list(range(bits - 1, 0, -1))
    return first, first[:-3] + [first[-2], first[-1], first[-3]]


def place_of(dev, me, bits):
    mask = dev ^ me
    first, second = exchange_order(bits)
    places = [sum(((mask >> n) & 1) << e for e, n in enumerate(order)) for order in (first, second)]
    return jnp.where((dev & 1) == 1, places[1], places[0]) + ((mask & 1) << (bits - 1))


def join_kernel(*refs):
    *part_refs, out_ref = refs
    at = 0
    for ref in part_refs:
        out_ref[at:at + ref.shape[0]] = ref[...]
        at += ref.shape[0]


def join(*parts):
    shape = (sum(x.shape[0] for x in parts), *parts[0].shape[1:])
    return pl.pallas_call(
        join_kernel,
        out_shape=jax.ShapeDtypeStruct(shape, parts[0].dtype),
        in_specs=[VMEM] * len(parts),
        out_specs=VMEM,
        compiler_params=pltpu.CompilerParams(vmem_limit_bytes=16 << 20),
        name="join",
    )(*parts)


def plan_kernel_part(me_ref, counts_ref, rows_ref, target_ref, bias_ref, fresh_bias_ref):
    device_count, slots = counts_ref.shape[1], rows_ref.shape[1]
    bits = device_count.bit_length() - 1
    me = me_ref[0]
    col = lax.broadcasted_iota(jnp.int32, target_ref.shape, 1)

    def one_device(dev, carry):
        start0, start1, target = carry
        count0, count1 = counts_ref[0, dev], counts_ref[1, dev]
        local = col - place_of(dev, me, bits) * (STEPS * slots)
        slot, step = local >> 1, local & 1
        rank = slot + jnp.where(step == 0, start0, start1)
        home = rank >> SLOT_BITS
        home = ((home ^ me) & 1) * (device_count // 2) + (home >> 1)
        row = home * PAIR + step * SLOT + (rank & (SLOT - 1))
        good = (local >= 0) & (slot < jnp.where(step == 0, count0, count1))
        return start0 + count0, start1 + count1, jnp.where(good, row, target)

    carry = (jnp.int32(0), jnp.int32(0), jnp.full(target_ref.shape, -1, jnp.int32))
    if device_count <= 16:
        for dev in range(device_count):
            carry = one_device(dev, carry)
    else:
        carry = lax.fori_loop(0, device_count, one_device, carry)
    target_ref[...] = carry[2]

    live0 = [i < counts_ref[0, me] for i in range(slots)]
    live1 = [i < counts_ref[1, me] for i in range(slots)]
    row0 = [jnp.where(live0[i], rows_ref[0, i], -1) for i in range(slots)]
    row1 = [jnp.where(live1[i], rows_ref[1, i], -2) for i in range(slots)]
    token = lax.broadcasted_iota(jnp.int32, bias_ref.shape, 1)
    second = lax.broadcasted_iota(jnp.int32, bias_ref.shape, 0) >= SLOT
    gone = token == row0[0]
    for i in range(1, slots):
        gone = gone | (token == row0[i])
    later = token == row1[0]
    for i in range(1, slots):
        later = later | (token == row1[i])
    bias_ref[...] = jnp.where(gone | (second & later), FAR, 0.0)
    col = lax.broadcasted_iota(jnp.int32, fresh_bias_ref.shape, 1)
    second = (lax.broadcasted_iota(jnp.int32, fresh_bias_ref.shape, 0) >= SLOT).astype(jnp.int32)
    seen = jnp.zeros(fresh_bias_ref.shape, jnp.int32)
    for i in range(slots):
        again = row1[0] == row0[i]
        for j in range(1, slots):
            again = again | (row1[j] == row0[i])
        kept = (live0[i] & jnp.logical_not(again)).astype(jnp.int32)
        early = jnp.where(second == 1, kept, live0[i].astype(jnp.int32))
        seen = jnp.where(col == 2 * i, early, seen)
        seen = jnp.where(col == 2 * i + 1, second * live1[i].astype(jnp.int32), seen)
    fresh_bias_ref[...] = jnp.where(seen == 1, 0.0, FAR)


def sort_kernel(first, planned, *refs):
    refs = list(refs)
    table_refs = [refs.pop(0) for _ in range(3)] if planned else []
    cache_ref = refs.pop(0)
    new_refs = [refs.pop(0) for _ in range(2)] if planned else []
    key_ref, value_ref, *small_refs, held, sems = refs
    tokens, width = key_ref.shape
    block = min(128, tokens)
    blocks = tokens // block

    def fetch(i):
        part = pl.ds(i * block, block)
        return pltpu.make_async_copy(
            cache_ref.at[part, :, pl.ds(first, width)], held.at[part, :, pl.ds(0, width)], sems.at[i]
        )

    for i in range(blocks):
        fetch(i).start()
    if planned:
        slots = new_refs[0].shape[0]
        for ref, new_ref in zip(small_refs[:2], new_refs):
            ref[...] = jnp.zeros_like(ref)
            ref[0:STEPS * slots, :] = new_ref.reshape(STEPS * slots, ref.shape[1])[...]
        plan_kernel_part(*table_refs, *small_refs[2:])
    out = lax.broadcasted_iota(jnp.int32, (2 * block, 2 * block), 0)
    src = lax.broadcasted_iota(jnp.int32, (2 * block, 2 * block), 1)
    order = (src == jnp.where(out < block, 2 * out, 2 * (out - block) + 1)).astype(jnp.bfloat16)
    pairs = held.reshape(2 * tokens, held.shape[2])
    for i in range(blocks):
        if i % WAITS == 0:
            for j in range(i, min(i + WAITS, blocks)):
                fetch(j).wait()
        rows = slice(i * block, (i + 1) * block)
        for c in range(0, width, 256):
            part = pairs[2 * i * block:2 * (i + 1) * block, c:c + 256]
            part = jnp.dot(order, part, preferred_element_type=jnp.float32).astype(jnp.bfloat16)
            key_ref[rows, c:c + 256] = part[:block]
            value_ref[rows, c:c + 256] = part[block:]


def sort_cache(cache, first, width, plan, name):
    tokens, _, full = cache.shape
    f32, bf16 = jnp.float32, jnp.bfloat16
    shapes = [jax.ShapeDtypeStruct((tokens, width), bf16)] * 2
    inputs, specs = [cache], [HBM]
    if plan:
        tables, fresh_key, fresh_value = plan
        slots = fresh_key.shape[0]
        device_count = tables[1].shape[1]
        fresh_rows = -(-STEPS * slots // 16) * 16
        shapes += [jax.ShapeDtypeStruct((fresh_rows, full), bf16)] * 2
        shapes += [
            jax.ShapeDtypeStruct((1, device_count * STEPS * slots), jnp.int32),
            jax.ShapeDtypeStruct((PAIR, tokens), f32),
            jax.ShapeDtypeStruct((PAIR, fresh_rows), f32),
        ]
        inputs = [*tables, cache, fresh_key, fresh_value]
        specs = [SMEM, SMEM, SMEM, HBM, VMEM, VMEM]

    def kernel(*refs):
        sort_kernel(first, bool(plan), *refs)

    blocks = tokens // min(128, tokens)
    return pl.pallas_call(
        kernel,
        out_shape=tuple(shapes),
        in_specs=specs,
        out_specs=(VMEM,) * len(shapes),
        scratch_shapes=[
            pltpu.VMEM((tokens, 2, width + LANES), bf16),
            pltpu.SemaphoreType.DMA((blocks,)),
        ],
        compiler_params=pltpu.CompilerParams(vmem_limit_bytes=SORT_VMEM << 20),
        cost_estimate=pl.CostEstimate(
            flops=8 * 128 * tokens * width, bytes_accessed=8 * tokens * width, transcendentals=0
        ),
        name=name,
    )(*inputs)


def two_parts(x):
    high = x.astype(jnp.bfloat16).astype(jnp.float32)
    return high, x - high


def pack_stats(high, total):
    lane = lax.broadcasted_iota(jnp.int32, high.shape, 1)
    high = jnp.where(lane < PART, high, 0.0)
    total = jnp.where(lane < PART, total, 0.0)
    stats, rest = two_parts(high)
    second, third = two_parts(rest)
    for n, part in enumerate((second, third) + two_parts(total)):
        stats = stats + pltpu.roll(part, PART * (n + 1), 1)
    return stats


def unpack_stats(stats):
    def part(n):
        return pltpu.roll(stats, LANES - PART * n, 1)

    return stats + part(1) + part(2), part(3) + part(4)


def attend_kernel(target_ref, bias_ref, fresh_bias_ref, fresh_key_ref, fresh_value_ref, *rest):
    key_refs, value_refs, gathered_refs, (keep_ref, send_ref) = rest[0:4:2], rest[1:4:2], rest[4:-2], rest[-2:]
    width = fresh_key_ref.shape[1]
    part_heads = key_refs[0].shape[1] // HEAD
    tokens = key_refs[0].shape[0]
    heads = width // HEAD
    half = keep_ref.shape[0]
    nt = (((1,), (1,)), ((), ()))

    def attend_rows(base, chunk, stores):
        row = lax.broadcasted_iota(jnp.int32, (chunk, target_ref.shape[1]), 0)
        pick = (row == target_ref[...] - base).astype(jnp.bfloat16)
        slots = [ref.reshape(ref.shape[0] * STEPS, width)[...].astype(jnp.float32) for ref in gathered_refs]
        slots = jnp.concatenate(slots).astype(jnp.bfloat16)
        queries = jnp.dot(pick, slots, preferred_element_type=jnp.float32).astype(jnp.bfloat16)
        bias = bias_ref[...]
        fresh_bias = fresh_bias_ref[...]
        lane = lax.broadcasted_iota(jnp.int32, (chunk, LANES), 1)
        highs = jnp.zeros((chunk, LANES), jnp.float32)
        totals = jnp.zeros((chunk, LANES), jnp.float32)
        ones = jnp.ones((tokens, LANES), jnp.bfloat16)

        def block_of(refs, h):
            part, at = (0, h) if h < part_heads else (1, h - part_heads)
            return refs[part][:, at * HEAD:(at + 1) * HEAD]

        def score(h):
            cols = slice(h * HEAD, (h + 1) * HEAD)
            q = queries[:, cols]
            s = lax.dot_general(q, block_of(key_refs, h), nt, preferred_element_type=jnp.float32)
            sf = lax.dot_general(q, fresh_key_ref[:, cols], nt, preferred_element_type=jnp.float32)
            s = (s.reshape(chunk // PAIR, PAIR, -1) + bias[None]).reshape(chunk, -1)
            sf = (sf.reshape(chunk // PAIR, PAIR, -1) + fresh_bias[None]).reshape(chunk, -1)
            return s, sf

        following = score(0)
        for h in range(heads):
            cols = slice(h * HEAD, (h + 1) * HEAD)
            s, sf = following
            if h + 1 < heads:
                following = score(h + 1)
            high = jnp.maximum(jnp.max(s, axis=1, keepdims=True), jnp.max(sf, axis=1, keepdims=True))
            w = jnp.exp2((s - high) * SCALE).astype(jnp.bfloat16)
            wf = jnp.exp2((sf - high) * SCALE).astype(jnp.bfloat16)
            value = jnp.concatenate([block_of(value_refs, h), ones], axis=1)
            fresh_value = jnp.concatenate([fresh_value_ref[:, cols], ones[:fresh_value_ref.shape[0]]], axis=1)
            o = jnp.dot(w, value, preferred_element_type=jnp.float32)
            o += jnp.dot(wf, fresh_value, preferred_element_type=jnp.float32)
            total = o[:, HEAD:]
            o = o[:, :HEAD] * (1.0 / total)
            for ref, to, start, count in stores:
                ref[pl.ds(to, count), cols] = o[start:start + count].astype(ref.dtype)
            highs = jnp.where(lane == h, high, highs)
            totals = jnp.where(lane == h, total, totals)
        stats = pack_stats(highs, totals)
        for ref, to, start, count in stores:
            ref[pl.ds(to, count), width:] = stats[start:start + count].astype(ref.dtype)

    if 2 * half <= 128:
        attend_rows(0, 2 * half, [(keep_ref, 0, 0, half), (send_ref, 0, half, half)])
    else:
        for ref, base in ((keep_ref, 0), (send_ref, half)):
            @pl.loop(0, half // 128)
            def _(i, ref=ref, base=base):
                to = pl.multiple_of(i * 128, 128)
                attend_rows(base + to, 128, [(ref, to, 0, 128)])


def attend(slots, target, bias, fresh_bias, fresh_key, fresh_value, sorted_parts, gathered):
    tokens, width = sorted_parts[0].shape[0], fresh_key.shape[1]
    rows = target.shape[1] * SLOT // slots
    shape = (rows // 2, width + LANES)
    return pl.pallas_call(
        attend_kernel,
        out_shape=(jax.ShapeDtypeStruct(shape, jnp.float32), jax.ShapeDtypeStruct(shape, jnp.bfloat16)),
        in_specs=[VMEM] * (5 + len(sorted_parts) + len(gathered)),
        out_specs=(VMEM, VMEM),
        compiler_params=pltpu.CompilerParams(vmem_limit_bytes=24 << 20),
        cost_estimate=pl.CostEstimate(
            flops=4 * rows * tokens * width, bytes_accessed=4 * tokens * width,
            transcendentals=rows * tokens * width // HEAD,
        ),
        name="attend",
    )(target, bias, fresh_bias, fresh_key, fresh_value, *sorted_parts, *gathered)


def merged(parts):
    width = parts[0].shape[1] - LANES
    stats = [unpack_stats(part[:, width:].astype(jnp.float32)) for part in parts]
    top = stats[0][0]
    for high, _ in stats[1:]:
        top = jnp.maximum(top, high)
    weights = [total * jnp.exp2((high - top) * SCALE) for high, total in stats]
    total = weights[0]
    for w in weights[1:]:
        total = total + w
    used = lax.broadcasted_iota(jnp.int32, total.shape, 1) < width // HEAD
    share = 1.0 / jnp.where(used, total, 1.0)
    weights = [w * share for w in weights]
    for h in range(width // HEAD):
        cols = slice(h * HEAD, (h + 1) * HEAD)
        o = parts[0][:, cols].astype(jnp.float32) * weights[0][:, h:h + 1]
        for part, w in zip(parts[1:], weights[1:]):
            o = o + part[:, cols].astype(jnp.float32) * w[:, h:h + 1]
        yield cols, o
    yield slice(width, width + LANES), pack_stats(jnp.where(used, top, 0.0), jnp.where(used, total, 0.0))


def merge_cores_kernel(keep_ref, other_ref, out_ref):
    for cols, o in merged([keep_ref, other_ref]):
        out_ref[:, :, cols] = o.reshape(o.shape[0] // PAIR, PAIR, -1).astype(jnp.bfloat16)


def merge_chips_kernel(parts_ref, out_ref):
    width = out_ref.shape[2]
    for cols, o in merged([parts_ref.at[n] for n in range(parts_ref.shape[0])]):
        if cols.start < width:
            for s in range(STEPS):
                out_ref[s, :, cols] = o[s * SLOT:(s + 1) * SLOT].astype(jnp.bfloat16)


def merge(kernel, parts, shape, name):
    return pl.pallas_call(
        kernel,
        out_shape=jax.ShapeDtypeStruct(shape, jnp.bfloat16),
        in_specs=[VMEM] * len(parts),
        out_specs=VMEM,
        compiler_params=pltpu.CompilerParams(vmem_limit_bytes=16 << 20),
        name=name,
    )(*parts)


def body(cache_kv, fresh_qkv, list_rows, counts):
    device_count = lax.axis_size("blk")
    me = lax.axis_index("blk")
    slot_count = list_rows.shape[1]
    bits = device_count.bit_length() - 1
    width = cache_kv.shape[2]

    def swap(x, *masks):
        return lax.ppermute(x, "blk", [(i, i ^ masks[i % len(masks)]) for i in range(device_count)])

    fresh = fresh_qkv.transpose(1, 2, 0, 3)
    mine, fresh_key, fresh_value = (fresh[:, i] for i in range(3))
    most = width // 2
    early = sort_cache(cache_kv, 0, most, None, "sort_first")
    column = mine
    steps = [(1 << m, 1 << n) for m, n in zip(*exchange_order(bits))]
    for e, masks in enumerate(steps[:-2]):
        other = swap(column, *masks)
        if e == 0:
            other, early, counts, list_rows = lax.optimization_barrier((other, early, counts, list_rows))
        column = join(column, other)
    tables = (me.reshape(1), counts, list_rows)
    late = sort_cache(cache_kv, most, width - most, (tables, fresh_key, fresh_value), "sort_second")
    both = [m | n for m, n in zip(*steps[-2:])]
    others = [swap(column, *masks) for masks in (*steps[-2:], both)]
    others, column, late = lax.optimization_barrier((others, column, late))
    beside = swap(column, 1)
    others = join(*others)
    gathered = [column, others, beside, swap(others, 1)]
    key, value, fresh_key, fresh_value, target, bias, fresh_bias = late
    keep, send = attend(slot_count, target, bias, fresh_bias, fresh_key, fresh_value, [*early, key, value], gathered)
    chips = device_count // 2
    parts = merge(merge_cores_kernel, [keep, swap(send, 1)], (chips, PAIR, width + LANES), "merge_cores")
    groups = [[chip * 2 + core for chip in range(chips)] for core in range(2)]
    parts = lax.all_to_all(parts, "blk", split_axis=0, concat_axis=0, axis_index_groups=groups, tiled=True)
    return merge(merge_chips_kernel, [parts], (STEPS, SLOT, width), "merge_chips")


def solution(mesh):
    in_specs = (
        P(("groups", "blk"), None, None),
        P(None, ("groups", "blk"), None, None),
        P(None, ("groups", "blk")),
        P(None, "groups"),
    )
    out_specs = P(None, ("groups", "blk"), None)
    return jax.shard_map(body, mesh=mesh, in_specs=in_specs, out_specs=out_specs, check_vma=False)
```

```python
import jax
import jax.numpy as jnp
from jax import lax
from jax.experimental import pallas as pl
from jax.experimental.pallas import tpu as pltpu
from jax.sharding import PartitionSpec as P

HEAD = 128
SLOT = 4
STEPS = 2
PAIR = STEPS * SLOT
LOG2E = 1.4426950408889634
SCALE = HEAD ** -0.5 * LOG2E
FAR = -1e30
LANES = 128
PART = 16
SLOT_BITS = 2
WAITS = 2
SORT_VMEM = 48
VMEM = pl.BlockSpec(memory_space=pltpu.VMEM)
SMEM = pl.BlockSpec(memory_space=pltpu.SMEM)
HBM = pl.BlockSpec(memory_space=pltpu.HBM)


def exchange_order(bits):
    first = list(range(bits - 1, 0, -1))
    return first, first[:-3] + [first[-2], first[-1], first[-3]]


def place_of(dev, me, bits):
    mask = dev ^ me
    first, second = exchange_order(bits)
    places = [sum(((mask >> n) & 1) << e for e, n in enumerate(order)) for order in (first, second)]
    return jnp.where((dev & 1) == 1, places[1], places[0]) + ((mask & 1) << (bits - 1))


def join_kernel(*refs):
    *part_refs, out_ref = refs
    at = 0
    for ref in part_refs:
        out_ref[at:at + ref.shape[0]] = ref[...]
        at += ref.shape[0]


def join(*parts):
    shape = (sum(x.shape[0] for x in parts), *parts[0].shape[1:])
    return pl.pallas_call(
        join_kernel,
        out_shape=jax.ShapeDtypeStruct(shape, parts[0].dtype),
        in_specs=[VMEM] * len(parts),
        out_specs=VMEM,
        compiler_params=pltpu.CompilerParams(vmem_limit_bytes=16 << 20),
        name="join",
    )(*parts)


def plan_kernel_part(me_ref, counts_ref, rows_ref, target_ref, bias_ref, fresh_bias_ref):
    device_count, slots = counts_ref.shape[1], rows_ref.shape[1]
    bits = device_count.bit_length() - 1
    me = me_ref[0]
    col = lax.broadcasted_iota(jnp.int32, target_ref.shape, 1)

    def one_device(dev, carry):
        start0, start1, target = carry
        count0, count1 = counts_ref[0, dev], counts_ref[1, dev]
        local = col - place_of(dev, me, bits) * (STEPS * slots)
        slot, step = local >> 1, local & 1
        rank = slot + jnp.where(step == 0, start0, start1)
        home = rank >> SLOT_BITS
        home = ((home ^ me) & 1) * (device_count // 2) + (home >> 1)
        row = home * PAIR + step * SLOT + (rank & (SLOT - 1))
        good = (local >= 0) & (slot < jnp.where(step == 0, count0, count1))
        return start0 + count0, start1 + count1, jnp.where(good, row, target)

    carry = (jnp.int32(0), jnp.int32(0), jnp.full(target_ref.shape, -1, jnp.int32))
    if device_count <= 16:
        for dev in range(device_count):
            carry = one_device(dev, carry)
    else:
        carry = lax.fori_loop(0, device_count, one_device, carry)
    target_ref[...] = carry[2]

    live0 = [i < counts_ref[0, me] for i in range(slots)]
    live1 = [i < counts_ref[1, me] for i in range(slots)]
    row0 = [jnp.where(live0[i], rows_ref[0, i], -1) for i in range(slots)]
    row1 = [jnp.where(live1[i], rows_ref[1, i], -2) for i in range(slots)]
    token = lax.broadcasted_iota(jnp.int32, bias_ref.shape, 1)
    second = lax.broadcasted_iota(jnp.int32, bias_ref.shape, 0) >= SLOT
    gone = token == row0[0]
    for i in range(1, slots):
        gone = gone | (token == row0[i])
    later = token == row1[0]
    for i in range(1, slots):
        later = later | (token == row1[i])
    bias_ref[...] = jnp.where(gone | (second & later), FAR, 0.0)
    col = lax.broadcasted_iota(jnp.int32, fresh_bias_ref.shape, 1)
    second = (lax.broadcasted_iota(jnp.int32, fresh_bias_ref.shape, 0) >= SLOT).astype(jnp.int32)
    seen = jnp.zeros(fresh_bias_ref.shape, jnp.int32)
    for i in range(slots):
        again = row1[0] == row0[i]
        for j in range(1, slots):
            again = again | (row1[j] == row0[i])
        kept = (live0[i] & jnp.logical_not(again)).astype(jnp.int32)
        early = jnp.where(second == 1, kept, live0[i].astype(jnp.int32))
        seen = jnp.where(col == 2 * i, early, seen)
        seen = jnp.where(col == 2 * i + 1, second * live1[i].astype(jnp.int32), seen)
    fresh_bias_ref[...] = jnp.where(seen == 1, 0.0, FAR)


def sort_kernel(first, planned, *refs):
    refs = list(refs)
    table_refs = [refs.pop(0) for _ in range(3)] if planned else []
    cache_ref = refs.pop(0)
    new_refs = [refs.pop(0) for _ in range(2)] if planned else []
    key_ref, value_ref, *small_refs, held, sems = refs
    tokens, width = key_ref.shape
    block = min(128, tokens)
    blocks = tokens // block

    def fetch(i):
        part = pl.ds(i * block, block)
        return pltpu.make_async_copy(
            cache_ref.at[part, :, pl.ds(first, width)], held.at[part, :, pl.ds(0, width)], sems.at[i]
        )

    for i in range(blocks):
        fetch(i).start()
    if planned:
        slots = new_refs[0].shape[0]
        for ref, new_ref in zip(small_refs[:2], new_refs):
            ref[...] = jnp.zeros_like(ref)
            ref[0:STEPS * slots, :] = new_ref.reshape(STEPS * slots, ref.shape[1])[...]
        plan_kernel_part(*table_refs, *small_refs[2:])
    out = lax.broadcasted_iota(jnp.int32, (2 * block, 2 * block), 0)
    src = lax.broadcasted_iota(jnp.int32, (2 * block, 2 * block), 1)
    order = (src == jnp.where(out < block, 2 * out, 2 * (out - block) + 1)).astype(jnp.bfloat16)
    pairs = held.reshape(2 * tokens, held.shape[2])
    for i in range(blocks):
        if i % WAITS == 0:
            for j in range(i, min(i + WAITS, blocks)):
                fetch(j).wait()
        rows = slice(i * block, (i + 1) * block)
        for c in range(0, width, 256):
            part = pairs[2 * i * block:2 * (i + 1) * block, c:c + 256]
            part = jnp.dot(order, part, preferred_element_type=jnp.float32).astype(jnp.bfloat16)
            key_ref[rows, c:c + 256] = part[:block]
            value_ref[rows, c:c + 256] = part[block:]


def sort_cache(cache, first, width, plan, name):
    tokens, _, full = cache.shape
    f32, bf16 = jnp.float32, jnp.bfloat16
    shapes = [jax.ShapeDtypeStruct((tokens, width), bf16)] * 2
    inputs, specs = [cache], [HBM]
    if plan:
        tables, fresh_key, fresh_value = plan
        slots = fresh_key.shape[0]
        device_count = tables[1].shape[1]
        fresh_rows = -(-STEPS * slots // 16) * 16
        shapes += [jax.ShapeDtypeStruct((fresh_rows, full), bf16)] * 2
        shapes += [
            jax.ShapeDtypeStruct((1, device_count * STEPS * slots), jnp.int32),
            jax.ShapeDtypeStruct((PAIR, tokens), f32),
            jax.ShapeDtypeStruct((PAIR, fresh_rows), f32),
        ]
        inputs = [*tables, cache, fresh_key, fresh_value]
        specs = [SMEM, SMEM, SMEM, HBM, VMEM, VMEM]

    def kernel(*refs):
        sort_kernel(first, bool(plan), *refs)

    blocks = tokens // min(128, tokens)
    return pl.pallas_call(
        kernel,
        out_shape=tuple(shapes),
        in_specs=specs,
        out_specs=(VMEM,) * len(shapes),
        scratch_shapes=[
            pltpu.VMEM((tokens, 2, width + LANES), bf16),
            pltpu.SemaphoreType.DMA((blocks,)),
        ],
        compiler_params=pltpu.CompilerParams(vmem_limit_bytes=SORT_VMEM << 20),
        cost_estimate=pl.CostEstimate(
            flops=8 * 128 * tokens * width, bytes_accessed=8 * tokens * width, transcendentals=0
        ),
        name=name,
    )(*inputs)


def two_parts(x):
    high = x.astype(jnp.bfloat16).astype(jnp.float32)
    return high, x - high


def pack_stats(high, total):
    lane = lax.broadcasted_iota(jnp.int32, high.shape, 1)
    high = jnp.where(lane < PART, high, 0.0)
    total = jnp.where(lane < PART, total, 0.0)
    stats, rest = two_parts(high)
    second, third = two_parts(rest)
    for n, part in enumerate((second, third) + two_parts(total)):
        stats = stats + pltpu.roll(part, PART * (n + 1), 1)
    return stats


def unpack_stats(stats):
    def part(n):
        return pltpu.roll(stats, LANES - PART * n, 1)

    return stats + part(1) + part(2), part(3) + part(4)


def attend_kernel(target_ref, bias_ref, fresh_bias_ref, fresh_key_ref, fresh_value_ref, *rest):
    key_refs, value_refs, gathered_refs, (keep_ref, send_ref) = rest[0:4:2], rest[1:4:2], rest[4:-2], rest[-2:]
    width = fresh_key_ref.shape[1]
    part_heads = key_refs[0].shape[1] // HEAD
    tokens = key_refs[0].shape[0]
    heads = width // HEAD
    half = keep_ref.shape[0]
    nt = (((1,), (1,)), ((), ()))

    def attend_rows(base, chunk, stores):
        row = lax.broadcasted_iota(jnp.int32, (chunk, target_ref.shape[1]), 0)
        pick = (row == target_ref[...] - base).astype(jnp.bfloat16)
        slots = [ref.reshape(ref.shape[0] * STEPS, width)[...].astype(jnp.float32) for ref in gathered_refs]
        slots = jnp.concatenate(slots).astype(jnp.bfloat16)
        queries = jnp.dot(pick, slots, preferred_element_type=jnp.float32).astype(jnp.bfloat16)
        bias = bias_ref[...]
        fresh_bias = fresh_bias_ref[...]
        lane = lax.broadcasted_iota(jnp.int32, (chunk, LANES), 1)
        highs = jnp.zeros((chunk, LANES), jnp.float32)
        totals = jnp.zeros((chunk, LANES), jnp.float32)
        ones = jnp.ones((tokens, LANES), jnp.bfloat16)

        def block_of(refs, h):
            part, at = (0, h) if h < part_heads else (1, h - part_heads)
            return refs[part][:, at * HEAD:(at + 1) * HEAD]

        def score(h):
            cols = slice(h * HEAD, (h + 1) * HEAD)
            q = queries[:, cols]
            s = lax.dot_general(q, block_of(key_refs, h), nt, preferred_element_type=jnp.float32)
            sf = lax.dot_general(q, fresh_key_ref[:, cols], nt, preferred_element_type=jnp.float32)
            s = (s.reshape(chunk // PAIR, PAIR, -1) + bias[None]).reshape(chunk, -1)
            sf = (sf.reshape(chunk // PAIR, PAIR, -1) + fresh_bias[None]).reshape(chunk, -1)
            return s, sf

        following = score(0)
        for h in range(heads):
            cols = slice(h * HEAD, (h + 1) * HEAD)
            s, sf = following
            if h + 1 < heads:
                following = score(h + 1)
            high = jnp.maximum(jnp.max(s, axis=1, keepdims=True), jnp.max(sf, axis=1, keepdims=True))
            w = jnp.exp2((s - high) * SCALE).astype(jnp.bfloat16)
            wf = jnp.exp2((sf - high) * SCALE).astype(jnp.bfloat16)
            value = jnp.concatenate([block_of(value_refs, h), ones], axis=1)
            fresh_value = jnp.concatenate([fresh_value_ref[:, cols], ones[:fresh_value_ref.shape[0]]], axis=1)
            o = jnp.dot(w, value, preferred_element_type=jnp.float32)
            o += jnp.dot(wf, fresh_value, preferred_element_type=jnp.float32)
            total = o[:, HEAD:]
            o = o[:, :HEAD] * (1.0 / total)
            for ref, to, start, count in stores:
                ref[pl.ds(to, count), cols] = o[start:start + count].astype(ref.dtype)
            highs = jnp.where(lane == h, high, highs)
            totals = jnp.where(lane == h, total, totals)
        stats = pack_stats(highs, totals)
        for ref, to, start, count in stores:
            ref[pl.ds(to, count), width:] = stats[start:start + count].astype(ref.dtype)

    if 2 * half <= 128:
        attend_rows(0, 2 * half, [(keep_ref, 0, 0, half), (send_ref, 0, half, half)])
    else:
        for ref, base in ((keep_ref, 0), (send_ref, half)):
            @pl.loop(0, half // 128)
            def _(i, ref=ref, base=base):
                to = pl.multiple_of(i * 128, 128)
                attend_rows(base + to, 128, [(ref, to, 0, 128)])


def attend(slots, target, bias, fresh_bias, fresh_key, fresh_value, sorted_parts, gathered):
    tokens, width = sorted_parts[0].shape[0], fresh_key.shape[1]
    rows = target.shape[1] * SLOT // slots
    shape = (rows // 2, width + LANES)
    return pl.pallas_call(
        attend_kernel,
        out_shape=(jax.ShapeDtypeStruct(shape, jnp.float32), jax.ShapeDtypeStruct(shape, jnp.bfloat16)),
        in_specs=[VMEM] * (5 + len(sorted_parts) + len(gathered)),
        out_specs=(VMEM, VMEM),
        compiler_params=pltpu.CompilerParams(vmem_limit_bytes=24 << 20),
        cost_estimate=pl.CostEstimate(
            flops=4 * rows * tokens * width, bytes_accessed=4 * tokens * width,
            transcendentals=rows * tokens * width // HEAD,
        ),
        name="attend",
    )(target, bias, fresh_bias, fresh_key, fresh_value, *sorted_parts, *gathered)


def merged(parts):
    width = parts[0].shape[1] - LANES
    stats = [unpack_stats(part[:, width:].astype(jnp.float32)) for part in parts]
    top = stats[0][0]
    for high, _ in stats[1:]:
        top = jnp.maximum(top, high)
    weights = [total * jnp.exp2((high - top) * SCALE) for high, total in stats]
    total = weights[0]
    for w in weights[1:]:
        total = total + w
    used = lax.broadcasted_iota(jnp.int32, total.shape, 1) < width // HEAD
    share = 1.0 / jnp.where(used, total, 1.0)
    weights = [w * share for w in weights]
    for h in range(width // HEAD):
        cols = slice(h * HEAD, (h + 1) * HEAD)
        o = parts[0][:, cols].astype(jnp.float32) * weights[0][:, h:h + 1]
        for part, w in zip(parts[1:], weights[1:]):
            o = o + part[:, cols].astype(jnp.float32) * w[:, h:h + 1]
        yield cols, o
    yield slice(width, width + LANES), pack_stats(jnp.where(used, top, 0.0), jnp.where(used, total, 0.0))


def merge_cores_kernel(keep_ref, other_ref, out_ref):
    for cols, o in merged([keep_ref, other_ref]):
        out_ref[:, :, cols] = o.reshape(o.shape[0] // PAIR, PAIR, -1).astype(jnp.bfloat16)


def merge_chips_kernel(parts_ref, out_ref):
    width = out_ref.shape[2]
    for cols, o in merged([parts_ref.at[n] for n in range(parts_ref.shape[0])]):
        if cols.start < width:
            for s in range(STEPS):
                out_ref[s, :, cols] = o[s * SLOT:(s + 1) * SLOT].astype(jnp.bfloat16)


def merge(kernel, parts, shape, name):
    return pl.pallas_call(
        kernel,
        out_shape=jax.ShapeDtypeStruct(shape, jnp.bfloat16),
        in_specs=[VMEM] * len(parts),
        out_specs=VMEM,
        compiler_params=pltpu.CompilerParams(vmem_limit_bytes=16 << 20),
        name=name,
    )(*parts)


def body(cache_kv, fresh_qkv, list_rows, counts):
    device_count = lax.axis_size("blk")
    me = lax.axis_index("blk")
    slot_count = list_rows.shape[1]
    bits = device_count.bit_length() - 1
    width = cache_kv.shape[2]

    def swap(x, *masks):
        return lax.ppermute(x, "blk", [(i, i ^ masks[i % len(masks)]) for i in range(device_count)])

    fresh = fresh_qkv.transpose(1, 2, 0, 3)
    mine, fresh_key, fresh_value = (fresh[:, i] for i in range(3))
    most = width // 2
    early = sort_cache(cache_kv, 0, most, None, "sort_first")
    column = mine
    steps = [(1 << m, 1 << n) for m, n in zip(*exchange_order(bits))]
    for e, masks in enumerate(steps[:-2]):
        other = swap(column, *masks)
        if e == 0:
            other, early, counts, list_rows = lax.optimization_barrier((other, early, counts, list_rows))
        column = join(column, other)
    tables = (me.reshape(1), counts, list_rows)
    late = sort_cache(cache_kv, most, width - most, (tables, fresh_key, fresh_value), "sort_second")
    both = [m | n for m, n in zip(*steps[-2:])]
    others = [swap(column, *masks) for masks in (*steps[-2:], both)]
    beside = swap(column, 1)
    others, beside, late = lax.optimization_barrier((others, beside, late))
    others = join(*others)
    gathered = [column, others, beside, swap(others, 1)]
    key, value, fresh_key, fresh_value, target, bias, fresh_bias = late
    keep, send = attend(slot_count, target, bias, fresh_bias, fresh_key, fresh_value, [*early, key, value], gathered)
    chips = device_count // 2
    parts = merge(merge_cores_kernel, [keep, swap(send, 1)], (chips, PAIR, width + LANES), "merge_cores")
    groups = [[chip * 2 + core for chip in range(chips)] for core in range(2)]
    parts = lax.all_to_all(parts, "blk", split_axis=0, concat_axis=0, axis_index_groups=groups, tiled=True)
    return merge(merge_chips_kernel, [parts], (STEPS, SLOT, width), "merge_chips")


def solution(mesh):
    in_specs = (
        P(("groups", "blk"), None, None),
        P(None, ("groups", "blk"), None, None),
        P(None, ("groups", "blk")),
        P(None, "groups"),
    )
    out_specs = P(None, ("groups", "blk"), None)
    return jax.shard_map(body, mesh=mesh, in_specs=in_specs, out_specs=out_specs, check_vma=False)
```
